32 devices in a mesh: dp: 8 (over z, core), seq: 4 (over y, x).
Axes of the slice: x: 2, y: 2, z: 4, core: 2. Of those that a mesh axis runs over, the one named last changes fastest.
Arguments:
- inputs: float32 [32, 2048, 512], P('dp', 'seq'), may hold values from -6 to 6
- cotangent: float32 [32, 2048, 512], P('dp', 'seq'), may hold values from -6 to 6
- masked: int32 [32, 2048], P('dp', 'seq'), may hold values from 0 to 1, as said below
- proj_seed: int32 [1], replicated, may hold values from 0 to 999999
- gain_attn: float32 [512], P('dp'), may hold values from 0.5 to 1.5
- w_query: float32 [512, 512], P('dp'), may hold values from -0.25 to 0.25
- w_key: float32 [512, 512], P('dp'), may hold values from -0.25 to 0.25
- w_value: float32 [512, 512], P('dp'), may hold values from -0.25 to 0.25
- w_out: float32 [512, 512], P('dp'), may hold values from -6 to 6
- gain_ffn: float32 [512], P('dp'), may hold values from 0.5 to 1.5
- w_up: float32 [512, 2048], P('dp'), may hold values from -0.25 to 0.25
- w_down: float32 [2048, 512], P('dp'), may hold values from -0.125 to 0.125
Outputs:
- outputs: float32 [32, 2048, 512], P('dp', 'seq')
- input_grad: float32 [32, 2048, 512], P('dp', 'seq')
- gain_attn_grad: float32 [512], P('dp')
- w_query_grad: float32 [512, 512], P('dp')
- w_key_grad: float32 [512, 512], P('dp')
- w_value_grad: float32 [512, 512], P('dp')
- w_out_grad: float32 [512, 512], P('dp')
- gain_ffn_grad: float32 [512], P('dp')
- w_up_grad: float32 [512, 2048], P('dp')
- w_down_grad: float32 [2048, 512], P('dp')
The draws below stay inside these ranges and needn't reach their ends.
Inputs may be any that keep to these rules, and one draw needn't show every extreme that they name: 1 marks a masked residue, whose output gradient counts.
All inputs are finite; a program needn't handle non-finite values.
Results may differ from the reference program's by a relative error of at most 0.025.
Values may be sent and summed in bfloat16 or wider, within the bound.
A program may use at most 256 MiB of HBM per device.

```python
import math
import jax
import jax.numpy as jnp
from jax import lax

D = 512
HEADS = 8
HEAD_DIM = 64
FEATURES = 256
FF = 2048
LENGTH = 2048
BATCH = 32


def draw_masked(key, part):
    key = jax.random.fold_in(key, 11)
    rate_key, roll_key = jax.random.split(key)
    rates = jax.random.randint(rate_key, (BATCH, 1), 5, 26)
    rolls = jax.random.randint(roll_key, (BATCH, LENGTH), 0, 100)
    return (rolls < rates).astype(jnp.int32)


def block_scale(rng, shape, pieces, least, high):
    gain, own = 1.0, jax.random.fold_in(rng, 6)
    for position, shards_of in pieces:
        draws = jnp.exp(jax.random.uniform(jax.random.fold_in(own, position), (shards_of,), jnp.float32, least / len(pieces), high / len(pieces)))
        gain = gain * jnp.repeat(draws, shape[position] // shards_of).reshape([-1 if axis == position else 1 for axis in range(len(shape))])
    return gain


def normal_values(stream_key, dims, scale, most, shards=(), kind=jnp.bfloat16):
    loudness = block_scale(stream_key, dims, shards, -0.22, 0.18) if shards else 1.0
    values = jax.random.normal(stream_key, dims, jnp.float32) * scale * loudness
    return jnp.minimum(jnp.maximum(values, -most), most).astype(kind)


def setup_inputs(seed: int = 0) -> dict:
    splits = jax.random.split(jax.random.key(seed), 13)
    return {
        "inputs": normal_values(splits[0], (BATCH, LENGTH, D), 1.0, 6.0, ((0, 8), (1, 4)), jnp.float32),
        "cotangent": normal_values(splits[1], (BATCH, LENGTH, D), 1.0, 6.0, ((0, 8), (1, 4)), jnp.float32),
        "masked": draw_masked(jax.random.fold_in(splits[12], 71), 0),
        "proj_seed": jax.random.randint(splits[3], (1,), 0, 1000000).astype(jnp.int32),
        "gain_attn": jnp.clip(1.0 + 0.1 * jax.random.normal(splits[4], (D,), jnp.float32), 0.5, 1.5),
        "w_query": normal_values(splits[5], (D, D), D ** -0.5, 0.25, ((0, 8),), jnp.float32),
        "w_key": normal_values(splits[6], (D, D), D ** -0.5, 0.25, ((0, 8),), jnp.float32),
        "w_value": normal_values(splits[7], (D, D), D ** -0.5, 0.25, ((0, 8),), jnp.float32),
        "w_out": normal_values(splits[8], (D, D), 1.0, 6.0, ((0, 8),), jnp.float32),
        "gain_ffn": jnp.clip(1.0 + 0.1 * jax.random.normal(splits[9], (D,), jnp.float32), 0.5, 1.5),
        "w_up": normal_values(splits[10], (D, FF), D ** -0.5, 0.25, ((0, 8),), jnp.float32),
        "w_down": normal_values(splits[11], (FF, D), FF ** -0.5, 0.125, ((0, 8),), jnp.float32),
    }


epsilon = 1e-05
top_precision = lax.Precision.HIGHEST

@jax.custom_vjp
def low(v):
    return lax.optimization_barrier(v.astype(jnp.bfloat16)).astype(jnp.float32)

@jax.custom_vjp
def low_back(v):
    return v

def low_keep(v):
    return (low(v), None)

def low_pass(kept, grad):
    return (grad,)

def back_keep(v):
    return (v, None)

def back_low(kept, grad):
    return (low(grad),)
low.defvjp(low_keep, low_pass)
low_back.defvjp(back_keep, back_low)

def scramble(hashed):
    return jnp.bitwise_xor(hashed, lax.shift_right_logical(hashed, jnp.full_like(hashed, 16)))

def feature_matrix(proj_seed):
    entries = FEATURES * HEAD_DIM
    counter = jnp.arange(2 * entries, dtype=jnp.int32)
    hashed = counter * 1664525 + proj_seed[0] * 22695477 + 1013904223
    hashed = scramble(hashed) * 73244475
    hashed = scramble(hashed) * 73244475
    hashed = scramble(hashed)
    low_bits = jnp.bitwise_and(hashed, 8388607)
    uniform_vals = (low_bits.astype(jnp.float32) + 0.5) * (1.0 / 8388608.0)
    radius = jnp.sqrt(-2.0 * jnp.log(uniform_vals[:entries]))
    normal_vals = radius * jnp.cos(2.0 * math.pi * uniform_vals[entries:])
    return normal_vals.reshape(FEATURES, HEAD_DIM)

def layer_norm(values):
    centred = values - lax.optimization_barrier(jnp.mean(values, axis=-1, keepdims=True))
    spread = lax.optimization_barrier(jnp.mean(centred * centred, axis=-1, keepdims=True))
    return centred * lax.rsqrt(spread + epsilon)

def matmul(left, right):
    return jnp.dot(left, right, precision=top_precision, preferred_element_type=jnp.float32)

def feature_map(projected, feature_dirs):
    scaled = projected.reshape(-1, HEADS, HEAD_DIM) * HEAD_DIM ** (-0.25)
    angles = jnp.einsum('lhd,md->lhm', scaled, feature_dirs, precision=top_precision)
    half_square = 0.5 * lax.optimization_barrier(jnp.sum(scaled * scaled, axis=-1, keepdims=True))
    return jnp.exp(angles - half_square) * FEATURES ** (-0.5)

def layer(inputs, gain_attn, w_query, w_key, w_value, w_out, gain_ffn, w_up, w_down, feature_dirs):
    normed = low(layer_norm(inputs) * low(gain_attn))
    queries = low_back(matmul(normed, low(w_query)))
    key_rows = low_back(matmul(normed, low(w_key)))
    values = low(low_back(matmul(normed, low(w_value))))
    query_feat = low(feature_map(queries, feature_dirs))
    key_feat = low(feature_map(key_rows, feature_dirs))
    head_values = values.reshape(-1, HEADS, HEAD_DIM)
    summary = low(low_back(jnp.einsum('lhm,lhe->hme', key_feat, head_values, precision=top_precision)))
    totals = low(low_back(lax.optimization_barrier(jnp.sum(key_feat, axis=0))))
    numerator = low_back(jnp.einsum('lhm,hme->lhe', query_feat, summary, precision=top_precision))
    denominator = low_back(jnp.einsum('lhm,hm->lh', query_feat, totals, precision=top_precision))
    attended = low((numerator / denominator[:, :, None]).reshape(-1, HEADS * HEAD_DIM))
    middle = inputs + low_back(matmul(attended, low(w_out)))
    normed_two = low(layer_norm(middle) * low(gain_ffn))
    hidden = low_back(matmul(normed_two, low(w_up)))
    activated = low(jax.nn.gelu(hidden, approximate=False))
    return middle + low_back(matmul(activated, low(w_down)))

def reference(inputs, cotangent, masked, proj_seed, gain_attn, w_query, w_key, w_value, w_out, gain_ffn, w_up, w_down):
    feature_dirs = feature_matrix(proj_seed)
    weights = (gain_attn, w_query, w_key, w_value, w_out, gain_ffn, w_up, w_down)

    def sequence_step(running, sequence):
        tokens, upstream, mask_row = sequence

        def apply_layer(tokens_in, *params):
            return layer(tokens_in, *params, feature_dirs)
        output, pullback = jax.vjp(apply_layer, tokens, *weights)
        gradients = pullback(upstream * mask_row[:, None].astype(jnp.float32))
        running = tuple((running_sum + addend for running_sum, addend in zip(running, gradients[1:])))
        return (running, (output, gradients[0]))
    initial = tuple((jnp.zeros(weight.shape, jnp.float32) for weight in weights))
    summed, (outputs, input_grad) = lax.scan(sequence_step, initial, (inputs, cotangent, masked))
    return (outputs, input_grad, summed[0], summed[1], summed[2], summed[3], summed[4], summed[5], summed[6], summed[7])
```

```python
import functools
import math

import jax
import jax.numpy as jnp
from jax import lax
from jax.experimental import pallas as pl
from jax.experimental.pallas import tpu as pltpu
from jax.sharding import PartitionSpec as P

D = 512
HEADS = 8
PAIRS = 4
HEAD_DIM = 64
FEATURES = 256
FF = 2048
CHUNK = 512

epsilon = 1e-05
LOG2E = math.log2(math.e)
LOW = jnp.bfloat16
F32 = jnp.float32


def scramble(hashed):
    return jnp.bitwise_xor(hashed, lax.shift_right_logical(hashed, jnp.full_like(hashed, 16)))


def uniform_entries(counter, seed):
    hashed = counter * 1664525 + seed * 22695477 + 1013904223
    hashed = scramble(hashed) * 73244475
    hashed = scramble(hashed) * 73244475
    hashed = scramble(hashed)
    low_bits = jnp.bitwise_and(hashed, 8388607)
    return (low_bits.astype(F32) + 0.5) * (1.0 / 8388608.0)


def direction_entries(index, seed):
    radius = jnp.sqrt(-2.0 * jnp.log(uniform_entries(index, seed)))
    turn = uniform_entries(index + FEATURES * HEAD_DIM, seed)
    return radius * jnp.cos(2.0 * math.pi * turn)


def dot(left, right):
    return jnp.dot(left, right, preferred_element_type=F32)


def dot_nt(left, right):
    return lax.dot_general(left, right, (((1,), (1,)), ((), ())), preferred_element_type=F32)


def normalize(values):
    centred = values - jnp.mean(values, axis=-1, keepdims=True)
    scale = lax.rsqrt(jnp.mean(centred * centred, axis=-1, keepdims=True) + epsilon)
    return centred * scale, scale


def norm_grad(grad_normed, unit_rows, scale, gain):
    scaled_grad = grad_normed * gain
    first = jnp.mean(scaled_grad, axis=-1, keepdims=True)
    second = jnp.mean(scaled_grad * unit_rows, axis=-1, keepdims=True)
    return scale * (scaled_grad - first - unit_rows * second)


def feature_pair(rows, forms_ref):
    high = rows.astype(LOW)
    rest = (rows - high.astype(F32)).astype(LOW)
    square = (rows * rows * (LOG2E / 16.0) + 1.0 / 16.0).astype(LOW)
    h0, h1 = high[:, :64], high[:, 64:]
    r0, r1 = rest[:, :64], rest[:, 64:]
    s0, s1 = square[:, :64], square[:, 64:]
    left0 = jnp.concatenate([r0, h0, h0, s0], axis=1)
    left1 = jnp.concatenate([h1, r1, s1, h1], axis=1)
    return jnp.exp2(dot(left0, forms_ref[0])), jnp.exp2(dot(left1, forms_ref[1]))


def keys_phase(x, gain_ref, w_kv_ref, forms_ref, n1_ref, k_ref, v_ref, pk_ref, sums_ref):
    unit, _ = normalize(x)
    normed = (unit * gain_ref[...]).astype(LOW)
    n1_ref[...] = normed
    values = dot(normed, w_kv_ref[:, D:]).astype(LOW)
    v_ref[...] = values
    keys = dot(normed, w_kv_ref[:, :D])
    k_ref[...] = keys.astype(LOW)
    ones = jnp.ones((16, x.shape[0]), LOW)
    for pair in range(PAIRS):
        lanes = slice(pair * 128, pair * 128 + 128)
        phi = feature_pair(keys[:, lanes], forms_ref)
        values_t = values[:, lanes].T
        for half in range(2):
            head = 2 * pair + half
            low = phi[half].astype(LOW)
            pk_ref[:, head * 256 : head * 256 + 256] = low
            left = jnp.concatenate([values_t[half * 64 : half * 64 + 64], ones], axis=0)
            got = dot(left, low)
            sums_ref[head * 64 : head * 64 + 64] = got[:64]
            sums_ref[512 + head : 513 + head] = got[64:65]


def spread_sums(sums_ref, spread_ref):
    for head in range(HEADS):
        own, other = (head % 2) * 64, 64 - (head % 2) * 64
        spread_ref[head, own : own + 64] = sums_ref[head * 64 : head * 64 + 64].astype(LOW)
        spread_ref[head, 128 + own : 192 + own] = jnp.broadcast_to(
            sums_ref[512 + head : 513 + head], (64, 256)
        ).astype(LOW)
        spread_ref[head, other : other + 64] = jnp.zeros((64, 256), LOW)
        spread_ref[head, 128 + other : 192 + other] = jnp.zeros((64, 256), LOW)


def middle_phase(
    x, upstream, mask, sums_ref, n1_ref, gain_ref, w_query_ref, w_out_ref, w_up_ref, w_down_ref, forms_ref, back_ref,
    out_ref, dmid_ref, dq_ref, grad_sums_ref, gain_grad_ref, w_out_grad_ref, w_up_grad_ref, w_down_grad_ref,
    spread_ref, pq_ref, q_ref, att_ref, rden_ref, n2_ref, mid_ref, dy_ref, dn2_ref,
):
    spread_sums(sums_ref, spread_ref)
    queries = dot(n1_ref[...], w_query_ref[...])
    q_ref[...] = queries
    for pair in range(PAIRS):
        lanes = slice(pair * 128, pair * 128 + 128)
        phi0, phi1 = feature_pair(queries[:, lanes], forms_ref)
        low0, low1 = phi0.astype(LOW), phi1.astype(LOW)
        pq_ref[:, pair * 512 : pair * 512 + 256] = low0
        pq_ref[:, pair * 512 + 256 : pair * 512 + 512] = low1
        both = dot_nt(low0, spread_ref[2 * pair]) + dot_nt(low1, spread_ref[2 * pair + 1])
        reciprocal = 1.0 / both[:, 128:]
        rden_ref[:, lanes] = reciprocal
        att_ref[:, lanes] = (both[:, :128] * reciprocal).astype(LOW)
    mid = x + dot(att_ref[...], w_out_ref[...])
    unit, scale = normalize(mid)
    gain = gain_ref[...]
    n2 = (unit * gain).astype(LOW)
    n2_ref[...] = n2
    mid_ref[...] = mid
    dy = upstream * mask
    dy_low = dy.astype(LOW)
    dy_ref[...] = dy_low
    n2_t = n2.T
    dy_t = dy_low.T
    out_ref[...] = mid
    for chunk in range(FF // CHUNK):
        cols = slice(chunk * CHUNK, chunk * CHUNK + CHUNK)
        hidden = dot(n2, w_up_ref[:, cols])
        cumulative = 0.5 * (1.0 + lax.erf(hidden * (1.0 / math.sqrt(2.0))))
        density = jnp.exp2(hidden * hidden * (-0.5 * LOG2E)) * (1.0 / math.sqrt(2.0 * math.pi))
        act = (hidden * cumulative).astype(LOW)
        dg = dot_nt(dy_low, w_down_ref[cols])
        du = (dg * (cumulative + hidden * density)).astype(LOW)
        out_ref[...] += dot(act, w_down_ref[cols])
        if chunk == 0:
            dn2_ref[...] = dot_nt(du, w_up_ref[:, cols])
        else:
            dn2_ref[...] += dot_nt(du, w_up_ref[:, cols])
        w_up_grad_ref[:, cols] += dot(n2_t, du)
        w_down_grad_ref[:, cols] += dot(dy_t, act)
    dn2 = dn2_ref[...]
    gain_grad_ref[...] += jnp.sum(dn2 * unit, axis=0, keepdims=True)
    dmid = dy + norm_grad(dn2, unit, scale, gain)
    dmid_ref[...] = dmid
    da = dmid.astype(LOW)
    w_out_grad_ref[...] += dot(att_ref[...].T, da)
    datt = dot_nt(da, w_out_ref[...])
    for pair in range(PAIRS):
        lanes = slice(pair * 128, pair * 128 + 128)
        dnumer = datt[:, lanes] * rden_ref[:, lanes]
        weighted = -dnumer * att_ref[:, lanes].astype(F32)
        left = jnp.concatenate([dnumer.astype(LOW), weighted.astype(LOW)], axis=1)
        left_t = left.T
        parts = []
        for half in range(2):
            head = 2 * pair + half
            own = half * 64
            pq = pq_ref[:, head * 256 : head * 256 + 256]
            dden = jnp.sum(left_t[128 + own : 192 + own].astype(F32), axis=0, keepdims=True)
            rows = jnp.concatenate(
                [left_t[own : own + 64], jnp.broadcast_to(dden, (16, dden.shape[1])).astype(LOW)], axis=0
            )
            got = dot(rows, pq)
            grad_sums_ref[head * 64 : head * 64 + 64] = got[:64]
            grad_sums_ref[512 + head : 513 + head] = got[64:65]
            dpq = dot(left, spread_ref[head])
            parts.append((dpq * pq.astype(F32)).astype(LOW))
        grads = dot(parts[0], back_ref[:256]) + dot(parts[1], back_ref[256:])
        dq_ref[:, lanes] = (grads[:, :128] - grads[:, 128:] * q_ref[:, lanes] * 0.125).astype(LOW)


def spread_grads(sums_ref, spread_ref):
    for head in range(HEADS):
        own, other = (head % 2) * 64, 64 - (head % 2) * 64
        spread_ref[head, own : own + 64] = sums_ref[head * 64 : head * 64 + 64].astype(LOW)
        spread_ref[head, other : other + 64] = jnp.zeros((64, 256), LOW)
        row = lax.broadcasted_iota(jnp.int32, (128, 256), 0)
        totals = jnp.broadcast_to(sums_ref[512 + head : 513 + head], (128, 256)).astype(F32)
        spread_ref[head, 128:] = jnp.where(row == 0, totals, 0.0).astype(LOW)


def last_phase(
    x, dmid, sums_ref, n1_ref, k_ref, v_ref, pk_ref, gain_ref, w_qkv_ref, back_ref,
    input_grad_ref, gain_grad_ref, w_grad_ref, spread_ref, dqkv_ref,
):
    spread_grads(sums_ref, spread_ref)
    ones = jnp.ones((x.shape[0], 128), LOW)
    for pair in range(PAIRS):
        lanes = slice(pair * 128, pair * 128 + 128)
        left = jnp.concatenate([v_ref[:, lanes], ones], axis=1)
        parts = []
        dv = None
        for half in range(2):
            head = 2 * pair + half
            pk = pk_ref[:, head * 256 : head * 256 + 256]
            dpk = dot(left, spread_ref[head])
            parts.append((dpk * pk.astype(F32)).astype(LOW))
            piece = dot_nt(pk, spread_ref[head, :128])
            dv = piece if dv is None else dv + piece
        dqkv_ref[:, D + D + pair * 128 : D + D + pair * 128 + 128] = dv.astype(LOW)
        grads = dot(parts[0], back_ref[:256]) + dot(parts[1], back_ref[256:])
        dqkv_ref[:, D + pair * 128 : D + pair * 128 + 128] = (
            grads[:, :128] - grads[:, 128:] * k_ref[:, lanes].astype(F32) * 0.125
        ).astype(LOW)
    dqkv = dqkv_ref[...]
    n1_t = n1_ref[...].T
    for part in range(3):
        cols = slice(part * D, part * D + D)
        w_grad_ref[:, cols] += dot(n1_t, dqkv_ref[:, cols])
    dn1 = dot_nt(dqkv, w_qkv_ref[...])
    unit, scale = normalize(x)
    gain_grad_ref[...] += jnp.sum(dn1 * unit, axis=0, keepdims=True)
    input_grad_ref[...] = dmid + norm_grad(dn1, unit, scale, gain_ref[...])


def feature_forms(seed):
    col = lax.broadcasted_iota(jnp.int32, (HEAD_DIM, FEATURES), 1)
    row = lax.broadcasted_iota(jnp.int32, (HEAD_DIM, FEATURES), 0)
    dirs_t = direction_entries(col * HEAD_DIM + row, seed) * HEAD_DIM ** (-0.25)
    scaled = dirs_t * LOG2E
    high = scaled.astype(LOW)
    rest = (scaled - high.astype(F32)).astype(LOW)
    minus = jnp.full((HEAD_DIM, FEATURES), -1.0, LOW)
    forms = jnp.stack(
        [jnp.concatenate([high, high, rest, minus], axis=0), jnp.concatenate([high, high, minus, rest], axis=0)]
    )
    back = dirs_t.T.astype(LOW)
    one, zero = jnp.ones_like(back), jnp.zeros_like(back)
    back = jnp.concatenate(
        [jnp.concatenate([back, zero, one, zero], axis=1), jnp.concatenate([zero, back, zero, one], axis=1)], axis=0
    )
    return forms, back


def whole(shape):
    return pl.BlockSpec(shape, lambda i: (0,) * len(shape))


def each(shape):
    return pl.BlockSpec((None,) + shape, lambda i: (i,) + (0,) * len(shape))


def on_device(inputs, cotangent, masked, proj_seed, gain_attn, w_query, w_key, w_value, w_out, gain_ffn, w_up, w_down):
    count, length = inputs.shape[0], inputs.shape[1]
    params = pltpu.CompilerParams(vmem_limit_bytes=60 * 2**20)
    forms, back = feature_forms(proj_seed[0])
    own_rows = gain_attn.shape[0]
    packed = jnp.concatenate(
        [w_query, w_key, w_value, w_out, w_up, w_down.reshape(own_rows, -1)], axis=1
    ).astype(LOW)
    gains = jnp.stack([gain_attn, gain_ffn], axis=1).astype(LOW)
    packed = lax.all_gather(packed, "dp", axis=0, tiled=True)
    gains = lax.all_gather(gains, "dp", axis=0, tiled=True).astype(F32)
    w_qkv, w_o, w_u = packed[:, :1536], packed[:, 1536:2048], packed[:, 2048:4096]
    w_d = packed[:, 4096:].reshape(FF, D)
    w_q = w_qkv[:, :512]
    w_kv = w_qkv[:, 512:]
    gain_one, gain_two = gains[:, 0].reshape(1, D), gains[:, 1].reshape(1, D)
    sd = jax.ShapeDtypeStruct

    def keys_kernel(x_ref, *refs):
        keys_phase(x_ref[...], *refs)

    n1, keys, values, pk, sums = pl.pallas_call(
        keys_kernel,
        grid=(count,),
        in_specs=[each((length, D)), whole((1, D)), whole((D, 2 * D)), whole((2, 256, 256))],
        out_specs=[each((length, D)), each((length, D)), each((length, D)), each((length, 2048)), each((528, 256))],
        out_shape=[
            sd((count, length, D), LOW), sd((count, length, D), LOW), sd((count, length, D), LOW),
            sd((count, length, 2048), LOW), sd((count, 528, 256), F32),
        ],
        compiler_params=params,
        name="keys_phase",
    )(inputs, gain_one, w_kv, forms)
    sums = lax.psum(sums[:, :520].astype(LOW), "seq")

    def middle_kernel(x_ref, up_ref, mask_ref, *refs):
        @pl.when(pl.program_id(0) == 0)
        def _():
            for ref in refs[13:17]:
                ref[...] = jnp.zeros_like(ref)

        middle_phase(x_ref[...], up_ref[...], mask_ref[...].astype(F32), *refs)

    outputs, dmid, dq, grad_sums, gain_two_grad, w_out_grad, w_up_grad, w_down_grad = pl.pallas_call(
        middle_kernel,
        grid=(count,),
        in_specs=[
            each((length, D)), each((length, D)), each((length, 1)), each((520, 256)), each((length, D)), whole((1, D)),
            whole((D, D)), whole((D, D)), whole((D, FF)), whole((FF, D)), whole((2, 256, 256)), whole((512, 256)),
        ],
        out_specs=[
            each((length, D)), each((length, D)), each((length, D)), each((528, 256)),
            whole((1, D)), whole((D, D)), whole((D, FF)), whole((D, FF)),
        ],
        out_shape=[
            sd((count, length, D), F32), sd((count, length, D), F32), sd((count, length, D), LOW), sd((count, 528, 256), F32),
            sd((1, D), F32), sd((D, D), F32), sd((D, FF), F32), sd((D, FF), F32),
        ],
        scratch_shapes=[
            pltpu.VMEM((HEADS, 256, 256), LOW), pltpu.VMEM((length, 2048), LOW), pltpu.VMEM((length, D), F32),
            pltpu.VMEM((length, D), LOW), pltpu.VMEM((length, D), F32), pltpu.VMEM((length, D), LOW),
            pltpu.VMEM((length, D), F32), pltpu.VMEM((length, D), LOW), pltpu.VMEM((length, D), F32),
        ],
        compiler_params=params,
        name="middle_phase",
    )(inputs, cotangent, masked[:, :, None], sums, n1, gain_two, w_q, w_o, w_u, w_d, forms, back)
    grad_sums = lax.psum(grad_sums[:, :520].astype(LOW), "seq")

    def last_kernel(x_ref, dmid_ref, dq_ref, *refs):
        @pl.when(pl.program_id(0) == 0)
        def _():
            for ref in refs[9:11]:
                ref[...] = jnp.zeros_like(ref)

        refs[-1][:, :D] = dq_ref[...]
        last_phase(x_ref[...], dmid_ref[...], *refs)

    input_grad, gain_one_grad, w_qkv_grad = pl.pallas_call(
        last_kernel,
        grid=(count,),
        in_specs=[
            each((length, D)), each((length, D)), each((length, D)), each((520, 256)), each((length, D)), each((length, D)),
            each((length, D)), each((length, 2048)), whole((1, D)), whole((D, 3 * D)), whole((512, 256)),
        ],
        out_specs=[each((length, D)), whole((1, D)), whole((D, 3 * D))],
        out_shape=[sd((count, length, D), F32), sd((1, D), F32), sd((D, 3 * D), F32)],
        scratch_shapes=[pltpu.VMEM((HEADS, 256, 256), LOW), pltpu.VMEM((length, 3 * D), LOW)],
        compiler_params=params,
        name="last_phase",
    )(inputs, dmid, dq, grad_sums, n1, keys, values, pk, gain_one, w_qkv, back)

    n_dp = D // own_rows
    down = w_down_grad.astype(LOW).reshape(D, n_dp, FF // n_dp).transpose(1, 0, 2).reshape(n_dp, -1)
    total = jnp.concatenate(
        [
            w_qkv_grad.astype(LOW).reshape(n_dp, -1),
            w_out_grad.astype(LOW).reshape(n_dp, -1),
            w_up_grad.astype(LOW).reshape(n_dp, -1),
            down,
            jnp.stack([gain_one_grad[0], gain_two_grad[0]], axis=1).astype(LOW).reshape(n_dp, -1),
        ],
        axis=1,
    )
    mine = lax.psum_scatter(total, "dp", scatter_dimension=0, tiled=True)
    mine = lax.psum(mine, "seq").astype(F32).reshape(-1)
    sizes = [own_rows * 1536, own_rows * 512, own_rows * 2048, own_rows * 2048, own_rows * 2]
    pieces, at = [], 0
    for size in sizes:
        pieces.append(mine[at : at + size])
        at += size
    qkv = pieces[0].reshape(own_rows, 1536)
    gains_grad = pieces[4].reshape(own_rows, 2)
    return (
        outputs,
        input_grad,
        gains_grad[:, 0],
        qkv[:, :512],
        qkv[:, 512:1024],
        qkv[:, 1024:],
        pieces[1].reshape(own_rows, 512),
        gains_grad[:, 1],
        pieces[2].reshape(own_rows, 2048),
        pieces[3].reshape(D, FF // n_dp).T,
    )


def solution(mesh):
    in_specs = (
        P("dp", "seq", None),
        P("dp", "seq", None),
        P("dp", "seq"),
        P(),
        P("dp"),
        P("dp", None),
        P("dp", None),
        P("dp", None),
        P("dp", None),
        P("dp"),
        P("dp", None),
        P("dp", None),
    )
    out_specs = (
        P("dp", "seq", None),
        P("dp", "seq", None),
        P("dp"),
        P("dp", None),
        P("dp", None),
        P("dp", None),
        P("dp", None),
        P("dp"),
        P("dp", None),
        P("dp", None),
    )
    return jax.shard_map(on_device, mesh=mesh, in_specs=in_specs, out_specs=out_specs, check_vma=False)
```

```python
import functools
import math

import jax
import jax.numpy as jnp
from jax import lax
from jax.experimental import pallas as pl
from jax.experimental.pallas import tpu as pltpu
from jax.sharding import PartitionSpec as P

D = 512
HEADS = 8
PAIRS = 4
HEAD_DIM = 64
FEATURES = 256
FF = 2048
CHUNK = 512

epsilon = 1e-05
LOG2E = math.log2(math.e)
LOW = jnp.bfloat16
F32 = jnp.float32


def scramble(hashed):
    return jnp.bitwise_xor(hashed, lax.shift_right_logical(hashed, jnp.full_like(hashed, 16)))


def uniform_entries(counter, seed):
    hashed = counter * 1664525 + seed * 22695477 + 1013904223
    hashed = scramble(hashed) * 73244475
    hashed = scramble(hashed) * 73244475
    hashed = scramble(hashed)
    low_bits = jnp.bitwise_and(hashed, 8388607)
    return (low_bits.astype(F32) + 0.5) * (1.0 / 8388608.0)


def direction_entries(index, seed):
    radius = jnp.sqrt(-2.0 * jnp.log(uniform_entries(index, seed)))
    turn = uniform_entries(index + FEATURES * HEAD_DIM, seed)
    return radius * jnp.cos(2.0 * math.pi * turn)


def dot(left, right):
    return jnp.dot(left, right, preferred_element_type=F32)


def dot_nt(left, right):
    return lax.dot_general(left, right, (((1,), (1,)), ((), ())), preferred_element_type=F32)


def normalize(values):
    centred = values - jnp.mean(values, axis=-1, keepdims=True)
    scale = lax.rsqrt(jnp.mean(centred * centred, axis=-1, keepdims=True) + epsilon)
    return centred * scale, scale


def norm_grad(grad_normed, unit_rows, scale, gain):
    scaled_grad = grad_normed * gain
    first = jnp.mean(scaled_grad, axis=-1, keepdims=True)
    second = jnp.mean(scaled_grad * unit_rows, axis=-1, keepdims=True)
    return scale * (scaled_grad - first - unit_rows * second)


def feature_pair(rows, forms_ref):
    high = rows.astype(LOW)
    rest = (rows - high.astype(F32)).astype(LOW)
    square = (rows * rows * (LOG2E / 16.0) + 1.0 / 16.0).astype(LOW)
    h0, h1 = high[:, :64], high[:, 64:]
    r0, r1 = rest[:, :64], rest[:, 64:]
    s0, s1 = square[:, :64], square[:, 64:]
    left0 = jnp.concatenate([r0, h0, h0, s0], axis=1)
    left1 = jnp.concatenate([h1, r1, s1, h1], axis=1)
    return jnp.exp2(dot(left0, forms_ref[0])), jnp.exp2(dot(left1, forms_ref[1]))


def keys_phase(x, gain_ref, w_kv_ref, forms_ref, n1_ref, k_ref, v_ref, pk_ref, sums_ref):
    unit, _ = normalize(x)
    normed = (unit * gain_ref[...]).astype(LOW)
    n1_ref[...] = normed
    values = dot(normed, w_kv_ref[:, D : 2 * D]).astype(LOW)
    v_ref[...] = values
    keys = dot(normed, w_kv_ref[:, :D])
    k_ref[...] = keys.astype(LOW)
    ones = jnp.ones((16, x.shape[0]), LOW)
    for pair in range(PAIRS):
        lanes = slice(pair * 128, pair * 128 + 128)
        phi = feature_pair(keys[:, lanes], forms_ref)
        values_t = values[:, lanes].T
        for half in range(2):
            head = 2 * pair + half
            low = phi[half].astype(LOW)
            pk_ref[:, head * 256 : head * 256 + 256] = low
            left = jnp.concatenate([values_t[half * 64 : half * 64 + 64], ones], axis=0)
            got = dot(left, low)
            put_sums(sums_ref, head, got[:64], got[64:65])


def put_sums(sums_ref, head, rows, totals):
    parts = sums_ref.shape[0]
    step = HEADS * HEAD_DIM // parts
    block = min(step, HEAD_DIM)
    for at in range(0, HEAD_DIM, block):
        part, row = divmod(head * HEAD_DIM + at, step)
        sums_ref[part, row : row + block] = rows[at : at + block].astype(LOW)
    part = head * HEAD_DIM // step
    row = step + head - -(-part * step // HEAD_DIM)
    sums_ref[part, row : row + 1] = totals.astype(LOW)


def get_sums(sums_ref, head):
    parts = sums_ref.shape[0]
    step = HEADS * HEAD_DIM // parts
    block = min(step, HEAD_DIM)
    rows = []
    for at in range(0, HEAD_DIM, block):
        part, row = divmod(head * HEAD_DIM + at, step)
        rows.append(sums_ref[part, row : row + block])
    part = head * HEAD_DIM // step
    row = step + head - -(-part * step // HEAD_DIM)
    rows = rows[0] if len(rows) == 1 else jnp.concatenate(rows, axis=0)
    return rows, sums_ref[part, row : row + 1]


def spread_sums(sums_ref, spread_ref):
    for head in range(HEADS):
        own, other = (head % 2) * 64, 64 - (head % 2) * 64
        rows, totals = get_sums(sums_ref, head)
        spread_ref[head, own : own + 64] = rows
        spread_ref[head, 128 + own : 192 + own] = jnp.broadcast_to(totals.astype(F32), (64, 256)).astype(LOW)
        spread_ref[head, other : other + 64] = jnp.zeros((64, 256), LOW)
        spread_ref[head, 128 + other : 192 + other] = jnp.zeros((64, 256), LOW)


def middle_phase(
    x, upstream, mask, sums_ref, n1_ref, gain_ref, w_query_ref, w_out_ref, w_up_ref, w_down_ref, forms_ref, back_ref,
    out_ref, dmid_ref, dq_ref, grad_sums_ref, gain_grad_ref, w_out_grad_ref, w_up_grad_ref, w_down_grad_ref,
    spread_ref, pq_ref, q_ref, att_ref, rden_ref, n2_ref, mid_ref, dy_ref, dn2_ref,
):
    spread_sums(sums_ref, spread_ref)
    queries = dot(n1_ref[...], w_query_ref[...])
    q_ref[...] = queries
    for pair in range(PAIRS):
        lanes = slice(pair * 128, pair * 128 + 128)
        phi0, phi1 = feature_pair(queries[:, lanes], forms_ref)
        low0, low1 = phi0.astype(LOW), phi1.astype(LOW)
        pq_ref[:, pair * 512 : pair * 512 + 256] = low0
        pq_ref[:, pair * 512 + 256 : pair * 512 + 512] = low1
        both = dot_nt(low0, spread_ref[2 * pair]) + dot_nt(low1, spread_ref[2 * pair + 1])
        reciprocal = 1.0 / both[:, 128:]
        rden_ref[:, lanes] = reciprocal
        att_ref[:, lanes] = (both[:, :128] * reciprocal).astype(LOW)
    mid = x + dot(att_ref[...], w_out_ref[...])
    unit, scale = normalize(mid)
    gain = gain_ref[...]
    n2 = (unit * gain).astype(LOW)
    n2_ref[...] = n2
    mid_ref[...] = mid
    dy = upstream * mask
    dy_low = dy.astype(LOW)
    dy_ref[...] = dy_low
    n2_t = n2.T
    dy_t = dy_low.T
    out_ref[...] = mid
    for chunk in range(FF // CHUNK):
        cols = slice(chunk * CHUNK, chunk * CHUNK + CHUNK)
        hidden = dot(n2, w_up_ref[:, cols])
        cumulative = 0.5 * (1.0 + lax.erf(hidden * (1.0 / math.sqrt(2.0))))
        density = jnp.exp2(hidden * hidden * (-0.5 * LOG2E)) * (1.0 / math.sqrt(2.0 * math.pi))
        act = (hidden * cumulative).astype(LOW)
        dg = dot_nt(dy_low, w_down_ref[cols])
        du = (dg * (cumulative + hidden * density)).astype(LOW)
        out_ref[...] += dot(act, w_down_ref[cols])
        if chunk == 0:
            dn2_ref[...] = dot_nt(du, w_up_ref[:, cols])
        else:
            dn2_ref[...] += dot_nt(du, w_up_ref[:, cols])
        w_up_grad_ref[:, cols] += dot(n2_t, du)
        owners, _, own_cols = w_down_grad_ref.shape
        for owner in range(chunk * CHUNK // own_cols, (chunk + 1) * CHUNK // own_cols):
            at = owner * own_cols - chunk * CHUNK
            w_down_grad_ref[owner] += dot(dy_t, act[:, at : at + own_cols])
    dn2 = dn2_ref[...]
    gain_grad_ref[...] += jnp.sum(dn2 * unit, axis=0, keepdims=True)
    dmid = dy + norm_grad(dn2, unit, scale, gain)
    dmid_ref[...] = dmid
    da = dmid.astype(LOW)
    w_out_grad_ref[...] += dot(att_ref[...].T, da)
    datt = dot_nt(da, w_out_ref[...])
    for pair in range(PAIRS):
        lanes = slice(pair * 128, pair * 128 + 128)
        dnumer = datt[:, lanes] * rden_ref[:, lanes]
        weighted = -dnumer * att_ref[:, lanes].astype(F32)
        left = jnp.concatenate([dnumer.astype(LOW), weighted.astype(LOW)], axis=1)
        left_t = left.T
        parts = []
        for half in range(2):
            head = 2 * pair + half
            own = half * 64
            pq = pq_ref[:, head * 256 : head * 256 + 256]
            dden = jnp.sum(left_t[128 + own : 192 + own].astype(F32), axis=0, keepdims=True)
            rows = jnp.concatenate(
                [left_t[own : own + 64], jnp.broadcast_to(dden, (16, dden.shape[1])).astype(LOW)], axis=0
            )
            got = dot(rows, pq)
            put_sums(grad_sums_ref, head, got[:64], got[64:65])
            dpq = dot(left, spread_ref[head])
            parts.append((dpq * pq.astype(F32)).astype(LOW))
        grads = dot(parts[0], back_ref[:256]) + dot(parts[1], back_ref[256:])
        dq_ref[:, lanes] = (grads[:, :128] - grads[:, 128:] * q_ref[:, lanes] * 0.125).astype(LOW)


def spread_grads(sums_ref, spread_ref):
    for head in range(HEADS):
        own, other = (head % 2) * 64, 64 - (head % 2) * 64
        rows, totals = get_sums(sums_ref, head)
        spread_ref[head, own : own + 64] = rows
        spread_ref[head, other : other + 64] = jnp.zeros((64, 256), LOW)
        row = lax.broadcasted_iota(jnp.int32, (128, 256), 0)
        totals = jnp.broadcast_to(totals.astype(F32), (128, 256))
        spread_ref[head, 128:] = jnp.where(row == 0, totals, 0.0).astype(LOW)


def last_phase(
    x, dmid, sums_ref, n1_ref, k_ref, v_ref, pk_ref, gain_ref, w_qkv_ref, back_ref,
    input_grad_ref, gain_grad_ref, w_grad_ref, spread_ref, dqkv_ref,
):
    spread_grads(sums_ref, spread_ref)
    ones = jnp.ones((x.shape[0], 128), LOW)
    for pair in range(PAIRS):
        lanes = slice(pair * 128, pair * 128 + 128)
        left = jnp.concatenate([v_ref[:, lanes], ones], axis=1)
        parts = []
        dv = None
        for half in range(2):
            head = 2 * pair + half
            pk = pk_ref[:, head * 256 : head * 256 + 256]
            dpk = dot(left, spread_ref[head])
            parts.append((dpk * pk.astype(F32)).astype(LOW))
            piece = dot_nt(pk, spread_ref[head, :128])
            dv = piece if dv is None else dv + piece
        dqkv_ref[:, D + D + pair * 128 : D + D + pair * 128 + 128] = dv.astype(LOW)
        grads = dot(parts[0], back_ref[:256]) + dot(parts[1], back_ref[256:])
        dqkv_ref[:, D + pair * 128 : D + pair * 128 + 128] = (
            grads[:, :128] - grads[:, 128:] * k_ref[:, lanes].astype(F32) * 0.125
        ).astype(LOW)
    dqkv = dqkv_ref[...]
    n1_t = n1_ref[...].T
    for part in range(3):
        cols = slice(part * D, part * D + D)
        w_grad_ref[:, cols] += dot(n1_t, dqkv_ref[:, cols])
    dn1 = dot_nt(dqkv[:, :D], w_qkv_ref[:, 2 * D : 3 * D]) + dot_nt(dqkv[:, D:], w_qkv_ref[:, : 2 * D])
    unit, scale = normalize(x)
    gain_grad_ref[...] += jnp.sum(dn1 * unit, axis=0, keepdims=True)
    input_grad_ref[...] = dmid + norm_grad(dn1, unit, scale, gain_ref[...])


MESH = pl.DeviceIdType.MESH


class Place:
    def __init__(self, n_dp, n_seq):
        self.n_dp, self.n_seq, self.n_z = n_dp, n_seq, n_dp // 2
        self.dp, self.seq = lax.axis_index("dp"), lax.axis_index("seq")
        self.z, self.core = self.dp // 2, lax.rem(self.dp, 2)

    def up_z(self, step):
        return lax.rem(self.z + step, self.n_z)

    def up_seq(self, step):
        return lax.rem(self.seq + step, self.n_seq)

    def down_z(self, step):
        return lax.rem(self.z + (self.n_z - step), self.n_z)

    def owner(self, z):
        return z * 2 + self.core

    def meet(self):
        barrier = pltpu.get_barrier_semaphore()
        for step in range(1, self.n_dp):
            other = lax.rem(self.dp + step, self.n_dp)
            pl.semaphore_signal(barrier, inc=1, device_id=(other, self.seq), device_id_type=MESH)
        for step in range(1, self.n_seq):
            pl.semaphore_signal(barrier, inc=1, device_id=(self.dp, self.up_seq(step)), device_id_type=MESH)
        pl.semaphore_wait(barrier, self.n_dp - 1 + self.n_seq - 1)


def remote(source, target, sems, at, device):
    return pltpu.make_async_remote_copy(
        src_ref=source, dst_ref=target, send_sem=sems[0].at[at], recv_sem=sems[1].at[at],
        device_id=device, device_id_type=MESH,
    )


def semaphores(*shape):
    return [pltpu.SemaphoreType.DMA(shape), pltpu.SemaphoreType.DMA(shape)]


class Gather:
    def __init__(self, place, ref, first, width, index, z_sems, plane_sems, core_sems):
        self.place, self.ref, self.first, self.width, self.index = place, ref, first, width, index
        self.rows = ref.shape[0] // place.n_dp
        self.across = min(place.n_seq, width // 128)
        self.along = place.n_seq // self.across
        self.z_sems, self.plane_sems, self.core_sems = z_sems, plane_sems, core_sems

    def piece(self, owner, part):
        rows, columns = self.rows // self.along, self.width // self.across
        top = pl.multiple_of(owner * self.rows + (part // self.across) * rows, rows)
        left = pl.multiple_of(self.first + lax.rem(part, self.across) * columns, 128)
        return self.ref.at[pl.ds(top, rows), pl.ds(left, columns)]

    def shard(self, owner):
        return self.ref.at[
            pl.ds(pl.multiple_of(owner * self.rows, self.rows), self.rows), pl.ds(self.first, self.width)
        ]

    def z_copy(self, step):
        place = self.place
        piece = self.piece(place.dp, place.seq)
        return remote(piece, piece, self.z_sems, (self.index, step - 1), (place.owner(place.up_z(step)), place.seq))

    def plane_copy(self, step, to):
        place = self.place
        piece = self.piece(place.owner(place.down_z(step)), place.seq)
        return remote(
            piece, piece, self.plane_sems, (self.index, step - 1, to - 1), (place.dp, place.up_seq(to))
        )

    def core_copy(self, step):
        place = self.place
        shard = self.shard(place.owner(place.down_z(step)))
        return remote(shard, shard, self.core_sems, (self.index, step), (place.z * 2 + 1 - place.core, place.seq))

    def start(self):
        for step in range(1, self.place.n_z):
            self.z_copy(step).start()
        self.core_copy(0).start()

    def to_plane(self):
        for step in range(1, self.place.n_z):
            self.z_copy(step).wait_recv()
            for to in range(1, self.place.n_seq):
                self.plane_copy(step, to).start()

    def to_core(self):
        for step in range(1, self.place.n_z):
            for to in range(1, self.place.n_seq):
                self.plane_copy(step, to).wait_recv()
            self.core_copy(step).start()

    def finish(self):
        for step in range(self.place.n_z):
            self.core_copy(step).wait_recv()

    def drain(self):
        for step in range(1, self.place.n_z):
            self.z_copy(step).wait_send()
            for to in range(1, self.place.n_seq):
                self.plane_copy(step, to).wait_send()
        for step in range(self.place.n_z):
            self.core_copy(step).wait_send()


class Sums:
    def __init__(self, place, local, arrived, full, add_sems, full_sems):
        self.place, self.local, self.arrived, self.full = place, local, arrived, full
        self.add_sems, self.full_sems = add_sems, full_sems

    def add_copy(self, slot, index, to):
        place = self.place
        other = place.up_seq(to)
        return remote(
            self.local.at[slot, other], self.arrived.at[index, to - 1], self.add_sems, (index, to - 1), (place.dp, other)
        )

    def full_copy(self, index, to):
        place = self.place
        mine = self.full.at[index, place.seq]
        return remote(mine, mine, self.full_sems, (index, to - 1), (place.dp, place.up_seq(to)))

    def start(self, slot, index):
        for to in range(1, self.place.n_seq):
            self.add_copy(slot, index, to).start()

    def add(self, slot, index):
        place = self.place
        total = self.local[slot, place.seq].astype(F32)
        for to in range(1, place.n_seq):
            self.add_copy(slot, index, to).wait_recv()
            total = total + self.arrived[index, to - 1].astype(F32)
        self.full[index, place.seq] = total.astype(LOW)
        for to in range(1, place.n_seq):
            self.full_copy(index, to).start()
        for to in range(1, place.n_seq):
            self.add_copy(slot, index, to).wait_send()

    def finish(self, index):
        for to in range(1, self.place.n_seq):
            self.full_copy(index, to).wait_recv()

    def drain(self, index):
        for to in range(1, self.place.n_seq):
            self.full_copy(index, to).wait_send()


class Scatter:
    def __init__(self, place, grads, first, width, by_rows, out, arrived, plane, column, final, sems):
        self.place, self.grads, self.first, self.width, self.by_rows = place, grads, first, width, by_rows
        self.out, self.arrived, self.plane, self.column, self.final = out, arrived, plane, column, final
        self.core_sems, self.plane_sems, self.z_sems, self.full_sems = sems

    @staticmethod
    def shapes(n_dp, n_seq, rows, width, by_rows):
        part = (rows // n_seq, width) if by_rows else (rows, width // n_seq)
        n_z = n_dp // 2
        return [
            pltpu.VMEM((n_seq, n_z) + part, LOW), pltpu.VMEM((n_seq, n_z) + part, LOW),
            pltpu.VMEM((n_seq - 1, n_z) + part, LOW), pltpu.VMEM((2 * n_z - 1,) + part, LOW),
            pltpu.VMEM((n_seq,) + part, LOW),
            *semaphores(1), *semaphores(n_seq - 1), *semaphores(n_z - 1), *semaphores(n_seq - 1),
        ]

    @classmethod
    def of(cls, place, grads, first, width, by_rows, refs):
        out, arrived, plane, column, final = refs[:5]
        sems = [refs[at : at + 2] for at in (5, 7, 9, 11)]
        return cls(place, grads, first, width, by_rows, out, arrived, plane, column, final, sems)

    N_REFS = 13

    def block(self, owner, part):
        rows, columns = self.out.shape[2:]
        if self.by_rows:
            return self.grads[owner, part * rows : part * rows + rows, self.first : self.first + columns]
        left = self.first + part * columns
        return self.grads[owner, :, left : left + columns]

    def core_copy(self):
        place = self.place
        return remote(self.out, self.arrived, self.core_sems, 0, (place.z * 2 + 1 - place.core, place.seq))

    def plane_copy(self, to):
        place = self.place
        other = place.up_seq(to)
        return remote(self.arrived.at[other], self.plane.at[to - 1], self.plane_sems, to - 1, (place.dp, other))

    def z_copy(self, step):
        place = self.place
        other = place.up_z(step)
        return remote(
            self.column.at[other], self.column.at[place.n_z + step - 1], self.z_sems, step - 1,
            (place.owner(other), place.seq),
        )

    def full_copy(self, to):
        place = self.place
        mine = self.final.at[place.seq]
        return remote(mine, mine, self.full_sems, to - 1, (place.dp, place.up_seq(to)))

    def start(self):
        place = self.place
        for part in range(place.n_seq):
            for z in range(place.n_z):
                self.out[part, z] = self.block(z * 2 + 1 - place.core, part).astype(LOW)
        self.core_copy().start()

    def to_plane(self):
        place = self.place
        self.core_copy().wait_recv()
        for part in range(place.n_seq):
            for z in range(place.n_z):
                mine = self.block(z * 2 + place.core, part)
                self.arrived[part, z] = (mine + self.arrived[part, z].astype(F32)).astype(LOW)
        for to in range(1, place.n_seq):
            self.plane_copy(to).start()

    def to_z(self):
        place = self.place
        for to in range(1, place.n_seq):
            self.plane_copy(to).wait_recv()
        for z in range(place.n_z):
            total = self.arrived[place.seq, z].astype(F32)
            for to in range(1, place.n_seq):
                total = total + self.plane[to - 1, z].astype(F32)
            self.column[z] = total.astype(LOW)
        for step in range(1, place.n_z):
            self.z_copy(step).start()

    def to_copies(self):
        place = self.place
        total = self.column[place.z].astype(F32)
        for step in range(1, place.n_z):
            self.z_copy(step).wait_recv()
            total = total + self.column[place.n_z + step - 1].astype(F32)
        self.final[place.seq] = total.astype(LOW)
        for to in range(1, place.n_seq):
            self.full_copy(to).start()

    def finish(self):
        for to in range(1, self.place.n_seq):
            self.full_copy(to).wait_recv()

    def drain(self):
        place = self.place
        self.core_copy().wait_send()
        for to in range(1, place.n_seq):
            self.plane_copy(to).wait_send()
            self.full_copy(to).wait_send()
        for step in range(1, place.n_z):
            self.z_copy(step).wait_send()


def feature_forms(seed):
    col = lax.broadcasted_iota(jnp.int32, (HEAD_DIM, FEATURES), 1)
    row = lax.broadcasted_iota(jnp.int32, (HEAD_DIM, FEATURES), 0)
    dirs_t = direction_entries(col * HEAD_DIM + row, seed) * HEAD_DIM ** (-0.25)
    scaled = dirs_t * LOG2E
    high = scaled.astype(LOW)
    rest = (scaled - high.astype(F32)).astype(LOW)
    minus = jnp.full((HEAD_DIM, FEATURES), -1.0, LOW)
    forms = jnp.stack(
        [jnp.concatenate([high, high, rest, minus], axis=0), jnp.concatenate([high, high, minus, rest], axis=0)]
    )
    back = dirs_t.T.astype(LOW)
    one, zero = jnp.ones_like(back), jnp.zeros_like(back)
    back = jnp.concatenate(
        [jnp.concatenate([back, zero, one, zero], axis=1), jnp.concatenate([zero, back, zero, one], axis=1)], axis=0
    )
    return forms, back


def whole(shape):
    return pl.BlockSpec(shape, lambda i: (0,) * len(shape))


def each(shape):
    return pl.BlockSpec((None,) + shape, lambda i: (i,) + (0,) * len(shape))


def column_cuts(n_seq):
    width = 2 * D if (2 * D) % (n_seq * 128) == 0 else 4 * D
    return [(first, width) for first in range(0, 4 * D, width)]


def on_device(sizes, inputs, cotangent, masked, proj_seed, gain_attn, w_query, w_key, w_value, w_out, gain_ffn, w_up, w_down):
    n_dp, n_seq = sizes
    count, length = inputs.shape[0], inputs.shape[1]
    own = D // n_dp
    own_ff = FF // n_dp
    cuts = column_cuts(n_seq)
    n_items = len(cuts) + 2
    part_rows = HEADS * HEAD_DIM // n_seq + 16
    forms, back = feature_forms(proj_seed[0])
    gains = jnp.pad(jnp.stack([gain_attn, gain_ffn], axis=1).astype(LOW), ((0, 0), (0, 126)))
    sd = jax.ShapeDtypeStruct
    vmem = pl.BlockSpec(memory_space=pltpu.VMEM)
    anywhere = pl.BlockSpec(memory_space=pl.ANY)

    def params(collective_id):
        return pltpu.CompilerParams(
            vmem_limit_bytes=60 * 2**20, collective_id=collective_id, has_side_effects=True
        )

    def keys_kernel(
        x_hbm, gains_own, wq, wk, wv, wo, wu, wd, forms_ref,
        w_att, w_up_full, w_down_full, gain_out, k_ref, v_ref, pk_ref, full,
        x_buf, gain_buf, gain_rows, n1_buf, local, arrived,
        x_sems, gain_send, gain_recv, z_send, z_recv, plane_send, plane_recv, core_send, core_recv,
        add_send, add_recv, full_send, full_recv,
    ):
        place = Place(n_dp, n_seq)
        rows = pl.ds(pl.multiple_of(place.dp * own, own), own)
        for at, ref in enumerate((wk, wv, wq, wo)):
            w_att[rows, at * D : at * D + D] = ref[...].astype(LOW)
        w_up_full[rows] = wu[...].astype(LOW)
        w_down_full[pl.ds(pl.multiple_of(place.dp * own_ff, own_ff), own_ff)] = wd[...].astype(LOW)
        gain_buf[rows] = gains_own[...]

        def x_copy(index):
            return pltpu.make_async_copy(x_hbm.at[index], x_buf.at[lax.rem(index, 2)], x_sems.at[lax.rem(index, 2)])

        x_copy(0).start()
        place.meet()
        sems = ((z_send, z_recv), (plane_send, plane_recv), (core_send, core_recv))
        items = [Gather(place, w_att, first, width, at, *sems) for at, (first, width) in enumerate(cuts)]
        items.append(Gather(place, w_up_full, 0, FF, len(cuts), *sems))
        items.append(Gather(place, w_down_full, 0, D, len(cuts) + 1, *sems))
        sums = Sums(place, local, arrived, full, (add_send, add_recv), (full_send, full_recv))

        def gain_copy(step):
            mine = gain_buf.at[rows]
            other = lax.rem(place.dp + step, n_dp)
            return remote(mine, mine, (gain_send, gain_recv), step - 1, (other, place.seq))

        for step in range(1, n_dp):
            gain_copy(step).start()
        for item in items:
            item.start()
        items[0].to_plane()
        items[0].to_core()
        for step in range(1, n_dp):
            gain_copy(step).wait_recv()
        gain_rows[...] = gain_buf[...].astype(F32).T[:8]
        gain_out[...] = gain_rows[...]
        items[0].finish()
        for item in items[1:]:
            item.to_plane()

        def step(index, carry):
            slot = lax.rem(index, 2)

            @pl.when(index + 1 < count)
            def _():
                x_copy(index + 1).start()

            x_copy(index).wait()
            keys_phase(
                x_buf[slot], gain_rows.at[0:1], w_att, forms_ref, n1_buf,
                k_ref.at[index], v_ref.at[index], pk_ref.at[index], local.at[slot],
            )
            sums.start(slot, index)

            @pl.when(index > 0)
            def _():
                sums.add(1 - slot, index - 1)

            return carry

        lax.fori_loop(0, count, step, 0)
        sums.add((count - 1) % 2, count - 1)
        for item in items[1:]:
            item.to_core()
        for item in items[1:]:
            item.finish()
        for index in range(count):
            sums.finish(index)
        for step in range(1, n_dp):
            gain_copy(step).wait_send()
        for item in items:
            item.drain()
        for index in range(count):
            sums.drain(index)

    w_att, w_u, w_d, gain_rows, keys, values, pk, sums = pl.pallas_call(
        keys_kernel,
        in_specs=[anywhere] + [vmem] * 8,
        out_specs=[vmem] * 8,
        out_shape=[
            sd((D, 4 * D), LOW), sd((D, FF), LOW), sd((FF, D), LOW), sd((8, D), F32),
            sd((count, length, D), LOW), sd((count, length, D), LOW), sd((count, length, 2048), LOW),
            sd((count, n_seq, part_rows, 256), LOW),
        ],
        scratch_shapes=[
            pltpu.VMEM((2, length, D), F32), pltpu.VMEM((D, 128), LOW), pltpu.VMEM((8, D), F32),
            pltpu.VMEM((length, D), LOW),
            pltpu.VMEM((2, n_seq, part_rows, 256), LOW), pltpu.VMEM((count, n_seq - 1, part_rows, 256), LOW),
            pltpu.SemaphoreType.DMA((2,)),
            *semaphores(n_dp - 1),
            *semaphores(n_items, n_dp // 2 - 1), *semaphores(n_items, n_dp // 2 - 1, n_seq - 1),
            *semaphores(n_items, n_dp // 2),
            *semaphores(count, n_seq - 1), *semaphores(count, n_seq - 1),
        ],
        compiler_params=params(0),
        name="keys_phase",
    )(inputs, gains, w_query, w_key, w_value, w_out, w_up, w_down, forms)
    gain_one, gain_two = gain_rows[0:1], gain_rows[1:2]

    def middle_kernel(x_ref, up_ref, mask_ref, sums_ref, gain_one_ref, *refs):
        @pl.when(pl.program_id(0) == 0)
        def _():
            for ref in refs[11:15]:
                ref[...] = jnp.zeros_like(ref)

        x = x_ref[...]
        n1_ref = refs[-1]
        unit, _ = normalize(x)
        n1_ref[...] = (unit * gain_one_ref[...]).astype(LOW)
        middle_phase(x, up_ref[...], mask_ref[...].astype(F32), sums_ref, n1_ref, *refs[:-1])

    outputs, dmid, dq, grad_sums, gain_two_grad, w_out_grad, w_up_grad, w_down_grad = pl.pallas_call(
        middle_kernel,
        grid=(count,),
        in_specs=[
            each((length, D)), each((length, D)), each((length, 1)), each((n_seq, part_rows, 256)), whole((1, D)),
            whole((1, D)),
            pl.BlockSpec((D, D), lambda i: (0, 2)), pl.BlockSpec((D, D), lambda i: (0, 3)), whole((D, FF)),
            whole((FF, D)), whole((2, 256, 256)), whole((512, 256)),
        ],
        out_specs=[
            each((length, D)), each((length, D)), each((length, D)), each((n_seq, part_rows, 256)),
            whole((1, D)), whole((D, D)), whole((D, FF)), whole((n_dp, D, own_ff)),
        ],
        out_shape=[
            sd((count, length, D), F32), sd((count, length, D), F32), sd((count, length, D), LOW),
            sd((count, n_seq, part_rows, 256), LOW),
            sd((1, D), F32), sd((D, D), F32), sd((D, FF), F32), sd((n_dp, D, own_ff), F32),
        ],
        scratch_shapes=[
            pltpu.VMEM((HEADS, 256, 256), LOW), pltpu.VMEM((length, 2048), LOW), pltpu.VMEM((length, D), F32),
            pltpu.VMEM((length, D), LOW), pltpu.VMEM((length, D), F32), pltpu.VMEM((length, D), LOW),
            pltpu.VMEM((length, D), F32), pltpu.VMEM((length, D), LOW), pltpu.VMEM((length, D), F32),
            pltpu.VMEM((length, D), LOW),
        ],
        compiler_params=pltpu.CompilerParams(vmem_limit_bytes=60 * 2**20),
        name="middle_phase",
    )(inputs, cotangent, masked[:, :, None], sums, gain_one, gain_two, w_att, w_att, w_u, w_d, forms, back)

    def sums_kernel(local, full, arrived, add_send, add_recv, full_send, full_recv):
        place = Place(n_dp, n_seq)
        place.meet()
        sums = Sums(place, local, arrived, full, (add_send, add_recv), (full_send, full_recv))
        for index in range(count):
            sums.start(index, index)
        for index in range(count):
            sums.add(index, index)
        for index in range(count):
            sums.finish(index)
        for index in range(count):
            sums.drain(index)

    grad_sums = pl.pallas_call(
        sums_kernel,
        in_specs=[vmem],
        out_specs=vmem,
        out_shape=sd((count, n_seq, part_rows, 256), LOW),
        scratch_shapes=[
            pltpu.VMEM((count, n_seq - 1, part_rows, 256), LOW),
            *semaphores(count, n_seq - 1), *semaphores(count, n_seq - 1),
        ],
        compiler_params=params(1),
        name="grad_sums",
    )(grad_sums)

    def last_kernel(x_ref, dmid_ref, dq_ref, sums_ref, *refs):
        @pl.when(pl.program_id(0) == 0)
        def _():
            for ref in refs[7:9]:
                ref[...] = jnp.zeros_like(ref)

        n1_ref = refs[-1]
        x = x_ref[...]
        unit, _ = normalize(x)
        n1_ref[...] = (unit * refs[3][...]).astype(LOW)
        refs[-2][:, :D] = dq_ref[...]
        last_phase(x, dmid_ref[...], sums_ref, n1_ref, *refs[:-1])

    input_grad, gain_one_grad, w_qkv_grad = pl.pallas_call(
        last_kernel,
        grid=(count,),
        in_specs=[
            each((length, D)), each((length, D)), each((length, D)), each((n_seq, part_rows, 256)), each((length, D)),
            each((length, D)), each((length, 2048)), whole((1, D)), whole((D, 4 * D)), whole((512, 256)),
        ],
        out_specs=[each((length, D)), whole((1, D)), whole((D, 3 * D))],
        out_shape=[sd((count, length, D), F32), sd((1, D), F32), sd((D, 3 * D), F32)],
        scratch_shapes=[
            pltpu.VMEM((HEADS, 256, 256), LOW), pltpu.VMEM((length, 3 * D), LOW), pltpu.VMEM((length, D), LOW),
        ],
        compiler_params=pltpu.CompilerParams(vmem_limit_bytes=60 * 2**20),
        name="last_phase",
    )(inputs, dmid, dq, grad_sums, keys, values, pk, gain_one, w_att, back)

    def scatter_kernel(gains_grad, att_grad, up_grad, down_grad, gain_ref, att_ref, up_ref, down_ref, gain_buf, gain_send, gain_recv, *refs):
        place = Place(n_dp, n_seq)
        place.meet()

        def gain_plane(step):
            mine = gain_buf.at[place.seq]
            return remote(mine, mine, (gain_send, gain_recv), step - 1, (place.dp, place.up_seq(step)))

        def gain_dp(step):
            mine = gain_buf.at[n_seq + place.dp]
            other = lax.rem(place.dp + step, n_dp)
            return remote(mine, mine, (gain_send, gain_recv), n_seq - 2 + step, (other, place.seq))

        gain_buf[place.seq] = gains_grad[...]
        for step in range(1, n_seq):
            gain_plane(step).start()
        specs = [(up_grad, 0, FF, False, up_ref), (down_grad, 0, own_ff, True, down_ref)]
        specs += [(att_grad, first, width, False, att_ref) for first, width in cuts]
        items = []
        for at, spec in enumerate(specs):
            items.append(Scatter.of(place, *spec[:4], refs[at * Scatter.N_REFS : (at + 1) * Scatter.N_REFS]))
        for item in items:
            item.start()
        for step in range(1, n_seq):
            gain_plane(step).wait_recv()
        total = gain_buf[0]
        for at in range(1, n_seq):
            total = total + gain_buf[at]
        gain_buf[n_seq + place.dp] = total
        for step in range(1, n_dp):
            gain_dp(step).start()
        for item in items:
            item.to_plane()
        for item in items:
            item.to_z()
        for step in range(1, n_dp):
            gain_dp(step).wait_recv()
        total = gain_buf[n_seq]
        for at in range(1, n_dp):
            total = total + gain_buf[n_seq + at]
        gain_ref[...] = total
        for item in items:
            item.to_copies()
        for item, spec in zip(items, specs):
            item.finish()
            for part in range(n_seq):
                got = item.final[part].astype(F32)
                if item.by_rows:
                    rows = got.shape[0]
                    spec[4][:, part * rows : part * rows + rows] = got.T
                else:
                    left = item.first + part * got.shape[1]
                    spec[4][:, left : left + got.shape[1]] = got
        for item in items:
            item.drain()
        for step in range(1, n_seq):
            gain_plane(step).wait_send()
        for step in range(1, n_dp):
            gain_dp(step).wait_send()

    att_grad = jnp.concatenate(
        [w_qkv_grad[:, D : 2 * D], w_qkv_grad[:, 2 * D :], w_qkv_grad[:, :D], w_out_grad], axis=1
    ).reshape(n_dp, own, 4 * D)
    gains_grad = jnp.pad(jnp.concatenate([gain_one_grad, gain_two_grad], axis=0), ((0, 6), (0, 0)))
    scatter_shapes = Scatter.shapes(n_dp, n_seq, own, FF, False) + Scatter.shapes(n_dp, n_seq, D, own_ff, True)
    for _, width in cuts:
        scatter_shapes += Scatter.shapes(n_dp, n_seq, own, width, False)
    gains_grad, att, up, down = pl.pallas_call(
        scatter_kernel,
        in_specs=[vmem] * 4,
        out_specs=[vmem] * 4,
        out_shape=[sd((8, D), F32), sd((own, 4 * D), F32), sd((own, FF), F32), sd((own_ff, D), F32)],
        scratch_shapes=[
            pltpu.VMEM((n_seq + n_dp, 8, D), F32), *semaphores(n_seq + n_dp - 2),
            *scatter_shapes,
        ],
        compiler_params=params(2),
        name="weight_grads",
    )(gains_grad, att_grad, w_up_grad.reshape(n_dp, own, FF), w_down_grad)
    gains_grad = lax.dynamic_slice(gains_grad, (0, lax.axis_index("dp") * own), (2, own))
    return (
        outputs,
        input_grad,
        gains_grad[0],
        att[:, 2 * D : 3 * D],
        att[:, :D],
        att[:, D : 2 * D],
        att[:, 3 * D :],
        gains_grad[1],
        up,
        down,
    )


def solution(mesh):
    in_specs = (
        P("dp", "seq", None),
        P("dp", "seq", None),
        P("dp", "seq"),
        P(),
        P("dp"),
        P("dp", None),
        P("dp", None),
        P("dp", None),
        P("dp", None),
        P("dp"),
        P("dp", None),
        P("dp", None),
    )
    out_specs = (
        P("dp", "seq", None),
        P("dp", "seq", None),
        P("dp"),
        P("dp", None),
        P("dp", None),
        P("dp", None),
        P("dp", None),
        P("dp"),
        P("dp", None),
        P("dp", None),
    )
    sizes = (mesh.shape["dp"], mesh.shape["seq"])
    return jax.shard_map(functools.partial(on_device, sizes), mesh=mesh, in_specs=in_specs, out_specs=out_specs, check_vma=False)
```

```python
import functools
import math

import jax
import jax.numpy as jnp
from jax import lax
from jax.experimental import pallas as pl
from jax.experimental.pallas import tpu as pltpu
from jax.sharding import PartitionSpec as P

D = 512
HEADS = 8
PAIRS = 4
HEAD_DIM = 64
FEATURES = 256
FF = 2048
CHUNKS = 4
KEY, VALUE, QUERY, OUT, UP, DOWN, UNITS = 0, 1, 2, 3, 4, 8, 12

epsilon = 1e-05
LOG2E = math.log2(math.e)
LOW = jnp.bfloat16
F32 = jnp.float32
MESH = pl.DeviceIdType.MESH


def scramble(hashed):
    return jnp.bitwise_xor(hashed, lax.shift_right_logical(hashed, jnp.full_like(hashed, 16)))


def uniform_entries(counter, seed):
    hashed = counter * 1664525 + seed * 22695477 + 1013904223
    hashed = scramble(hashed) * 73244475
    hashed = scramble(hashed) * 73244475
    hashed = scramble(hashed)
    low_bits = jnp.bitwise_and(hashed, 8388607)
    return (low_bits.astype(F32) + 0.5) * (1.0 / 8388608.0)


def direction_entries(index, seed):
    radius = jnp.sqrt(-2.0 * jnp.log(uniform_entries(index, seed)))
    turn = uniform_entries(index + FEATURES * HEAD_DIM, seed)
    return radius * jnp.cos(2.0 * math.pi * turn)


def feature_forms(seed):
    col = lax.broadcasted_iota(jnp.int32, (HEAD_DIM, FEATURES), 1)
    row = lax.broadcasted_iota(jnp.int32, (HEAD_DIM, FEATURES), 0)
    dirs_t = direction_entries(col * HEAD_DIM + row, seed) * HEAD_DIM ** (-0.25)
    scaled = dirs_t * LOG2E
    high = scaled.astype(LOW)
    rest = (scaled - high.astype(F32)).astype(LOW)
    minus = jnp.full((HEAD_DIM, FEATURES), -1.0, LOW)
    forms = jnp.stack(
        [jnp.concatenate([high, high, rest, minus], axis=0), jnp.concatenate([high, high, minus, rest], axis=0)]
    )
    back = dirs_t.T.astype(LOW)
    one, zero = jnp.ones_like(back), jnp.zeros_like(back)
    back = jnp.concatenate(
        [jnp.concatenate([back, zero, one, zero], axis=1), jnp.concatenate([zero, back, zero, one], axis=1)], axis=0
    )
    return forms, back


def dot(left, right):
    return jnp.dot(left, right, preferred_element_type=F32)


def dot_nt(left, right):
    return lax.dot_general(left, right, (((1,), (1,)), ((), ())), preferred_element_type=F32)


def dot_tn(left, right):
    return lax.dot_general(left, right, (((0,), (0,)), ((), ())), preferred_element_type=F32)


def normalize(values):
    centred = values - jnp.mean(values, axis=-1, keepdims=True)
    scale = lax.rsqrt(jnp.mean(centred * centred, axis=-1, keepdims=True) + epsilon)
    return centred * scale, scale


def norm_grad(grad_normed, unit_rows, scale, gain):
    scaled_grad = grad_normed * gain
    first = jnp.mean(scaled_grad, axis=-1, keepdims=True)
    second = jnp.mean(scaled_grad * unit_rows, axis=-1, keepdims=True)
    return scale * (scaled_grad - first - unit_rows * second)


def pair_lanes(pair, base=0):
    return slice(base + pair * 128, base + pair * 128 + 128)


def head_lanes(head):
    return slice(head * 256, head * 256 + 256)


def feature_pair(rows, forms_ref):
    high = rows.astype(LOW)
    rest = (rows - high.astype(F32)).astype(LOW)
    square = (rows * rows * (LOG2E / 16.0) + 1.0 / 16.0).astype(LOW)
    h0, h1 = high[:, :64], high[:, 64:]
    r0, r1 = rest[:, :64], rest[:, 64:]
    s0, s1 = square[:, :64], square[:, 64:]
    left0 = jnp.concatenate([r0, h0, h0, s0], axis=1)
    left1 = jnp.concatenate([h1, r1, s1, h1], axis=1)
    return jnp.exp2(dot(left0, forms_ref[0])), jnp.exp2(dot(left1, forms_ref[1]))


def sums_place(parts, head):
    step = HEADS * HEAD_DIM // parts
    block = min(step, HEAD_DIM)
    runs = [divmod(head * HEAD_DIM + at, step) + (at, block) for at in range(0, HEAD_DIM, block)]
    part = head * HEAD_DIM // step
    return runs, part, step + head - -(-part * step // HEAD_DIM)


def put_sums(sums_ref, head, rows, totals):
    runs, part, row = sums_place(sums_ref.shape[0], head)
    for run_part, run_row, at, block in runs:
        sums_ref[run_part, run_row : run_row + block] = rows[at : at + block].astype(LOW)
    sums_ref[part, row : row + 1] = totals.astype(LOW)


def get_sums(sums_ref, head):
    runs, part, row = sums_place(sums_ref.shape[0], head)
    rows = [sums_ref[run_part, run_row : run_row + block] for run_part, run_row, _, block in runs]
    rows = rows[0] if len(rows) == 1 else jnp.concatenate(rows, axis=0)
    return rows, sums_ref[part, row : row + 1].astype(F32)


def spread_sums(sums_ref, spread_ref):
    for head in range(HEADS):
        own, other = (head % 2) * 64, 64 - (head % 2) * 64
        rows, totals = get_sums(sums_ref, head)
        spread_ref[head, own : own + 64] = rows
        spread_ref[head, 128 + own : 192 + own] = jnp.broadcast_to(totals, (64, 256)).astype(LOW)
        spread_ref[head, other : other + 64] = jnp.zeros((64, 256), LOW)
        spread_ref[head, 128 + other : 192 + other] = jnp.zeros((64, 256), LOW)


def spread_grads(sums_ref, spread_ref):
    for head in range(HEADS):
        own, other = (head % 2) * 64, 64 - (head % 2) * 64
        rows, totals = get_sums(sums_ref, head)
        spread_ref[head, own : own + 64] = rows
        spread_ref[head, other : other + 64] = jnp.zeros((64, 256), LOW)
        row = lax.broadcasted_iota(jnp.int32, (128, 256), 0)
        spread_ref[head, 128:] = jnp.where(row == 0, jnp.broadcast_to(totals, (128, 256)), 0.0).astype(LOW)


def keys_phase(x, gain, weights, forms_ref, state_ref, sums_ref):
    unit, _ = normalize(x)
    normed = (unit * gain).astype(LOW)
    state_ref[:, 3072:3584] = normed
    values = dot(normed, weights[VALUE]).astype(LOW)
    state_ref[:, 2560:3072] = values
    keys = dot(normed, weights[KEY])
    state_ref[:, 2048:2560] = keys.astype(LOW)
    ones = jnp.ones((16, x.shape[0]), LOW)
    for pair in range(PAIRS):
        phi = feature_pair(keys[:, pair_lanes(pair)], forms_ref)
        values_t = values[:, pair_lanes(pair)].T
        for half in range(2):
            head = 2 * pair + half
            low = phi[half].astype(LOW)
            state_ref[:, head_lanes(head)] = low
            left = jnp.concatenate([values_t[half * 64 : half * 64 + 64], ones], axis=0)
            got = dot(left, low)
            put_sums(sums_ref, head, got[:64], got[64:65])


def front_phase(x, upstream, mask, gain_one, gain_two, sums_ref, weights, forms_ref, spread_ref, state_ref, out_ref, n2_ref, dy_ref, scale_ref):
    spread_sums(sums_ref, spread_ref)
    unit, _ = normalize(x)
    queries = dot((unit * gain_one).astype(LOW), weights[QUERY])
    state_ref[:, 2048:2560] = queries.astype(LOW)
    for pair in range(PAIRS):
        phi0, phi1 = feature_pair(queries[:, pair_lanes(pair)], forms_ref)
        low0, low1 = phi0.astype(LOW), phi1.astype(LOW)
        state_ref[:, head_lanes(2 * pair)] = low0
        state_ref[:, head_lanes(2 * pair + 1)] = low1
        both = dot_nt(low0, spread_ref[2 * pair]) + dot_nt(low1, spread_ref[2 * pair + 1])
        reciprocal = 1.0 / both[:, 128:]
        state_ref[:, pair_lanes(pair, 2560)] = (both[:, :128] * reciprocal).astype(LOW)
        state_ref[:, pair_lanes(pair, 3072)] = reciprocal.astype(LOW)
    mid = x + dot(state_ref[:, 2560:3072], weights[OUT])
    unit, scale = normalize(mid)
    n2_ref[...] = (unit * gain_two).astype(LOW)
    scale_ref[...] = jnp.broadcast_to(scale, scale_ref.shape)
    out_ref[...] = mid
    lanes = mask.shape[1]
    for at in range(0, D, lanes):
        dy_ref[:, at : at + lanes] = (upstream[:, at : at + lanes] * mask).astype(LOW)


def ffn_phase(first, n2, dy, w_up, w_down, out_ref, dn2_ref, up_grad_ref, down_grad_ref):
    hidden = dot(n2, w_up)
    cumulative = 0.5 * (1.0 + lax.erf(hidden * (1.0 / math.sqrt(2.0))))
    density = jnp.exp2(hidden * hidden * (-0.5 * LOG2E)) * (1.0 / math.sqrt(2.0 * math.pi))
    act = (hidden * cumulative).astype(LOW)
    du = (dot_nt(dy, w_down) * (cumulative + hidden * density)).astype(LOW)
    out_ref[...] += dot(act, w_down)
    down_grad_ref[...] += dot_tn(act, dy)
    dn2 = dot_nt(du, w_up)
    if first:
        dn2_ref[...] = dn2
    else:
        dn2_ref[...] += dn2
    up_grad_ref[...] += dot_tn(n2, du)


def attention_grad_phase(dy, dn2, n2, scale, gain, sums_ref, weights, back_ref, state_ref, spread_ref, gain_grad_ref, w_out_grad_ref, da_ref, dq_ref, grad_sums_ref):
    spread_sums(sums_ref, spread_ref)
    unit = n2.astype(F32) * (1.0 / gain)
    gain_grad_ref[...] += jnp.sum(dn2 * unit, axis=0, keepdims=True)
    da = (dy.astype(F32) + norm_grad(dn2, unit, scale, gain)).astype(LOW)
    da_ref[...] = da
    w_out_grad_ref[...] += dot_tn(state_ref[:, 2560:3072], da)
    datt = dot_nt(da, weights[OUT])
    for pair in range(PAIRS):
        dnumer = datt[:, pair_lanes(pair)] * state_ref[:, pair_lanes(pair, 3072)].astype(F32)
        weighted = -dnumer * state_ref[:, pair_lanes(pair, 2560)].astype(F32)
        left = jnp.concatenate([dnumer.astype(LOW), weighted.astype(LOW)], axis=1)
        left_t = left.T
        parts = []
        for half in range(2):
            head, own = 2 * pair + half, half * 64
            pq = state_ref[:, head_lanes(head)]
            dden = jnp.sum(left_t[128 + own : 192 + own].astype(F32), axis=0, keepdims=True)
            rows = jnp.concatenate(
                [left_t[own : own + 64], jnp.broadcast_to(dden, (16, dden.shape[1])).astype(LOW)], axis=0
            )
            got = dot(rows, pq)
            put_sums(grad_sums_ref, head, got[:64], got[64:65])
            parts.append((dot(left, spread_ref[head]) * pq.astype(F32)).astype(LOW))
        grads = dot(parts[0], back_ref[:256]) + dot(parts[1], back_ref[256:])
        q = state_ref[:, pair_lanes(pair, 2048)].astype(F32)
        dq_ref[:, pair_lanes(pair)] = (grads[:, :128] - grads[:, 128:] * q * 0.125).astype(LOW)


def keys_grad_phase(sums_ref, back_ref, state_ref, spread_ref, dq_ref, dk_ref, dv_ref, att_grad_ref):
    spread_grads(sums_ref, spread_ref)
    ones = jnp.ones((dk_ref.shape[0], 128), LOW)
    for pair in range(PAIRS):
        left = jnp.concatenate([state_ref[:, pair_lanes(pair, 2560)], ones], axis=1)
        parts = []
        dv = None
        for half in range(2):
            head = 2 * pair + half
            pk = state_ref[:, head_lanes(head)]
            parts.append((dot(left, spread_ref[head]) * pk.astype(F32)).astype(LOW))
            piece = dot_nt(pk, spread_ref[head, :128])
            dv = piece if dv is None else dv + piece
        dv_ref[:, pair_lanes(pair)] = dv.astype(LOW)
        grads = dot(parts[0], back_ref[:256]) + dot(parts[1], back_ref[256:])
        k = state_ref[:, pair_lanes(pair, 2048)].astype(F32)
        dk_ref[:, pair_lanes(pair)] = (grads[:, :128] - grads[:, 128:] * k * 0.125).astype(LOW)
    normed = state_ref[:, 3072:3584]
    att_grad_ref[KEY] += dot_tn(normed, dk_ref[...])
    att_grad_ref[VALUE] += dot_tn(normed, dv_ref[...])
    att_grad_ref[QUERY] += dot_tn(normed, dq_ref[...])


def input_grad_phase(x, da, dq, dk, dv, gain, weights, gain_grad_ref, input_grad_ref):
    dn1 = dot_nt(dq, weights[QUERY]) + dot_nt(dk, weights[KEY]) + dot_nt(dv, weights[VALUE])
    unit, scale = normalize(x)
    gain_grad_ref[...] += jnp.sum(dn1 * unit, axis=0, keepdims=True)
    input_grad_ref[...] = da.astype(F32) + norm_grad(dn1, unit, scale, gain)


class Place:
    def __init__(self, n_dp, n_seq):
        self.n_dp, self.n_seq, self.n_z = n_dp, n_seq, n_dp // 2
        self.dp, self.seq = lax.axis_index("dp"), lax.axis_index("seq")
        self.z, self.core = self.dp // 2, lax.rem(self.dp, 2)

    def up_z(self, step):
        return lax.rem(self.z + step, self.n_z)

    def up_seq(self, step):
        return lax.rem(self.seq + step, self.n_seq)

    def down_z(self, step):
        return lax.rem(self.z + (self.n_z - step), self.n_z)

    def owner(self, z):
        return z * 2 + self.core

    def other_core(self):
        return (self.z * 2 + 1 - self.core, self.seq)

    def meet(self):
        barrier = pltpu.get_barrier_semaphore()
        for step in range(1, self.n_dp):
            other = lax.rem(self.dp + step, self.n_dp)
            pl.semaphore_signal(barrier, inc=1, device_id=(other, self.seq), device_id_type=MESH)
        for step in range(1, self.n_seq):
            pl.semaphore_signal(barrier, inc=1, device_id=(self.dp, self.up_seq(step)), device_id_type=MESH)
        pl.semaphore_wait(barrier, self.n_dp - 1 + self.n_seq - 1)


def remote(source, target, sems, at, device):
    return pltpu.make_async_remote_copy(
        src_ref=source, dst_ref=target, send_sem=sems[0].at[at], recv_sem=sems[1].at[at],
        device_id=device, device_id_type=MESH,
    )


def semaphores(*shape):
    return [pltpu.SemaphoreType.DMA(shape), pltpu.SemaphoreType.DMA(shape)]


class Gather:
    def __init__(self, place, weights, first, count, index, sems):
        self.place, self.weights, self.first, self.count, self.index = place, weights, first, count, index
        self.own = D // place.n_dp
        self.across = min(place.n_seq, D // 128)
        self.units = count // (place.n_seq // self.across)
        self.z_sems, self.plane_sems, self.core_sems = sems

    def rows(self, owner):
        return pl.ds(pl.multiple_of(owner * self.own, self.own), self.own)

    def piece(self, owner, part):
        columns = D // self.across
        first = self.first + (part // self.across) * self.units
        left = pl.multiple_of(lax.rem(part, self.across) * columns, 128)
        return self.weights.at[pl.ds(first, self.units), self.rows(owner), pl.ds(left, columns)]

    def shard(self, owner):
        return self.weights.at[pl.ds(self.first, self.count), self.rows(owner)]

    def z_copy(self, step):
        place = self.place
        piece = self.piece(place.dp, place.seq)
        return remote(piece, piece, self.z_sems, (self.index, step - 1), (place.owner(place.up_z(step)), place.seq))

    def plane_copy(self, step, to):
        place = self.place
        piece = self.piece(place.owner(place.down_z(step)), place.seq)
        return remote(piece, piece, self.plane_sems, (self.index, step - 1, to - 1), (place.dp, place.up_seq(to)))

    def core_copy(self, step):
        shard = self.shard(self.place.owner(self.place.down_z(step)))
        return remote(shard, shard, self.core_sems, (self.index, step), self.place.other_core())

    def start(self):
        for step in range(1, self.place.n_z):
            self.z_copy(step).start()
        self.core_copy(0).start()

    def to_plane(self):
        for step in range(1, self.place.n_z):
            self.z_copy(step).wait_recv()
            for to in range(1, self.place.n_seq):
                self.plane_copy(step, to).start()

    def to_core(self):
        for step in range(1, self.place.n_z):
            for to in range(1, self.place.n_seq):
                self.plane_copy(step, to).wait_recv()
            self.core_copy(step).start()

    def finish(self):
        for step in range(self.place.n_z):
            self.core_copy(step).wait_recv()

    def drain(self):
        for step in range(1, self.place.n_z):
            self.z_copy(step).wait_send()
            for to in range(1, self.place.n_seq):
                self.plane_copy(step, to).wait_send()
        for step in range(self.place.n_z):
            self.core_copy(step).wait_send()


class Sums:
    def __init__(self, place, local, arrived, full, add_sems, full_sems):
        self.place, self.local, self.arrived, self.full = place, local, arrived, full
        self.add_sems, self.full_sems = add_sems, full_sems

    def add_copy(self, slot, index, to):
        other = self.place.up_seq(to)
        return remote(
            self.local.at[slot, other], self.arrived.at[index, to - 1], self.add_sems, (index, to - 1),
            (self.place.dp, other),
        )

    def full_copy(self, index, to):
        place = self.place
        mine = self.full.at[index, place.seq]
        return remote(mine, mine, self.full_sems, (index, to - 1), (place.dp, place.up_seq(to)))

    def start(self, slot, index):
        for to in range(1, self.place.n_seq):
            self.add_copy(slot, index, to).start()

    def add(self, slot, index):
        place = self.place
        total = self.local[slot, place.seq].astype(F32)
        for to in range(1, place.n_seq):
            self.add_copy(slot, index, to).wait_recv()
            total = total + self.arrived[index, to - 1].astype(F32)
        self.full[index, place.seq] = total.astype(LOW)
        for to in range(1, place.n_seq):
            self.full_copy(index, to).start()
        for to in range(1, place.n_seq):
            self.add_copy(slot, index, to).wait_send()

    def finish(self, index):
        for to in range(1, self.place.n_seq):
            self.full_copy(index, to).wait_recv()

    def drain(self, index):
        for to in range(1, self.place.n_seq):
            self.full_copy(index, to).wait_send()


OUT_SLOTS = 4


class Scatter:
    def __init__(self, place, index, refs, kept=None):
        self.place, self.index, self.slot, self.kept = place, index, index % OUT_SLOTS, kept
        self.out, self.mine, self.arrived, self.plane, self.column, self.final = refs[:6]
        self.core_sems, self.plane_sems, self.z_sems, self.full_sems = refs[6:8], refs[8:10], refs[10:12], refs[12:14]
        self.own = D // place.n_dp
        self.across = min(place.n_seq, D // 128)
        self.lanes = D // self.across

    @staticmethod
    def shapes(n_dp, n_seq, items, held):
        own, n_z = D // n_dp, n_dp // 2
        part = (own, D // min(n_seq, D // 128))
        return [
            pltpu.VMEM((OUT_SLOTS, n_seq, n_z) + part, LOW), pltpu.VMEM((held, n_seq, n_z) + part, LOW),
            pltpu.VMEM((items, n_seq, n_z) + part, LOW), pltpu.VMEM((items, n_seq - 1, n_z) + part, LOW),
            pltpu.VMEM((items, 2 * n_z - 1) + part, LOW), pltpu.VMEM((items, n_seq) + part, LOW),
            *semaphores(items), *semaphores(items, n_seq - 1), *semaphores(items, n_z - 1), *semaphores(items, n_seq - 1),
        ]

    def block(self, grads, owner, lane_part):
        rows = pl.ds(pl.multiple_of(owner * self.own, self.own), self.own)
        return grads[rows, lane_part * self.lanes : lane_part * self.lanes + self.lanes]

    def core_copy(self):
        return remote(
            self.out.at[self.slot], self.arrived.at[self.index], self.core_sems, self.index, self.place.other_core()
        )

    def plane_copy(self, to):
        other = self.place.up_seq(to)
        return remote(
            self.arrived.at[self.index, other], self.plane.at[self.index, to - 1], self.plane_sems,
            (self.index, to - 1), (self.place.dp, other),
        )

    def z_copy(self, step):
        place = self.place
        other = place.up_z(step)
        return remote(
            self.column.at[self.index, other], self.column.at[self.index, place.n_z + step - 1], self.z_sems,
            (self.index, step - 1), (place.owner(other), place.seq),
        )

    def full_copy(self, to):
        place = self.place
        mine = self.final.at[self.index, place.seq]
        return remote(mine, mine, self.full_sems, (self.index, to - 1), (place.dp, place.up_seq(to)))

    def put(self, unit, grads):
        place = self.place
        for lane_part in range(self.across):
            part = unit * self.across + lane_part
            for z in range(place.n_z):
                self.out[self.slot, part, z] = self.block(grads, z * 2 + 1 - place.core, lane_part).astype(LOW)
                if self.kept is None:
                    self.mine[self.index, part, z] = self.block(grads, place.owner(z), lane_part).astype(LOW)

    def start(self):
        self.core_copy().start()

    def to_plane(self):
        place = self.place
        self.core_copy().wait_recv()
        for part in range(place.n_seq):
            for z in range(place.n_z):
                if self.kept is None:
                    mine = self.mine[self.index, part, z].astype(F32)
                else:
                    mine = self.block(self.kept[part // self.across], place.owner(z), part % self.across)
                self.arrived[self.index, part, z] = (mine + self.arrived[self.index, part, z].astype(F32)).astype(LOW)
        for to in range(1, place.n_seq):
            self.plane_copy(to).start()

    def to_z(self):
        place = self.place
        for to in range(1, place.n_seq):
            self.plane_copy(to).wait_recv()
        for z in range(place.n_z):
            total = self.arrived[self.index, place.seq, z].astype(F32)
            for to in range(1, place.n_seq):
                total = total + self.plane[self.index, to - 1, z].astype(F32)
            self.column[self.index, z] = total.astype(LOW)
        for step in range(1, place.n_z):
            self.z_copy(step).start()

    def to_copies(self):
        place = self.place
        total = self.column[self.index, place.z].astype(F32)
        for step in range(1, place.n_z):
            self.z_copy(step).wait_recv()
            total = total + self.column[self.index, place.n_z + step - 1].astype(F32)
        self.final[self.index, place.seq] = total.astype(LOW)
        for to in range(1, place.n_seq):
            self.full_copy(to).start()

    def finish(self):
        for to in range(1, self.place.n_seq):
            self.full_copy(to).wait_recv()

    def result(self, unit):
        parts = [self.final[self.index, unit * self.across + at] for at in range(self.across)]
        return jnp.concatenate(parts, axis=1).astype(F32)

    def drain(self, core=True):
        place = self.place
        if core:
            self.core_copy().wait_send()
        for to in range(1, place.n_seq):
            self.plane_copy(to).wait_send()
            self.full_copy(to).wait_send()
        for step in range(1, place.n_z):
            self.z_copy(step).wait_send()


STATE = 2048 + 3 * D


def layer_kernel(
    sizes, x_hbm, cot_hbm, mask_ref, gains_own, wq, wk, wv, wo, wu, wd, forms_ref, back_ref,
    out_hbm, grad_hbm, gain_grads_ref, att_ref, up_ref, down_ref, state_hbm,
    weights, gain_buf, gains, att_grad, up_grad, down_grad, gain_sums, gain_mail,
    local, arrived, full, state, spread, n2_buf, dy_buf, da_buf, dq_buf, out_buf, pool, scale_buf,
    x_sems, cot_sems, write_sems, read_sems, out_sems, grad_sems, *rest,
):
    n_dp, n_seq = sizes
    count = x_hbm.shape[0]
    own = D // n_dp
    place = Place(n_dp, n_seq)
    group = max(1, n_seq // (D // 128))
    gather_sems = (rest[0:2], rest[2:4], rest[4:6])
    gain_sems, mail_sems = rest[6:8], rest[8:10]
    sums_refs = (place, local, arrived, full, rest[10:12], rest[12:14])
    scatter_refs = rest[14:]

    my_rows = pl.ds(pl.multiple_of(place.dp * own, own), own)

    def x_copy(step):
        slot = lax.rem(step, 2)
        return pltpu.make_async_copy(x_hbm.at[lax.rem(step, count)], pool.at[slot], x_sems.at[slot])

    def cot_copy(index):
        slot = lax.rem(index, 2)
        return pltpu.make_async_copy(cot_hbm.at[index], pool.at[2 + slot], cot_sems.at[slot])

    def write_copy(step):
        slot = lax.rem(step, 2)
        return pltpu.make_async_copy(state.at[slot], state_hbm.at[step], write_sems.at[slot])

    def read_copy(event):
        slot = lax.rem(event, 2)
        return pltpu.make_async_copy(
            state_hbm.at[lax.rem(count + event, 2 * count)], state.at[slot], read_sems.at[slot]
        )

    def out_copy(index):
        return pltpu.make_async_copy(out_buf.at[index], out_hbm.at[index], out_sems.at[index])

    def grad_copy(index):
        slot = lax.rem(index, 2)
        return pltpu.make_async_copy(pool.at[2 + slot], grad_hbm.at[index], grad_sems.at[slot])

    x_copy(0).start()
    cot_copy(0).start()
    for unit, ref in ((KEY, wk), (VALUE, wv), (QUERY, wq), (OUT, wo)):
        weights[unit, my_rows] = ref[...].astype(LOW)
    for chunk in range(CHUNKS):
        columns = [wu[:, (r * CHUNKS + chunk) * own : (r * CHUNKS + chunk + 1) * own] for r in range(n_dp)]
        weights[UP + chunk, my_rows] = jnp.concatenate(columns, axis=1).astype(LOW)
        weights[DOWN + chunk, my_rows] = wd[chunk * own : chunk * own + own].astype(LOW)
    gain_buf[my_rows] = gains_own[...]
    place.meet()

    runs = [(KEY, 2), (QUERY, 2), (UP, 4), (DOWN, 4)] if group == 1 else [(KEY, 4), (UP, 4), (DOWN, 4)]
    gathers = [Gather(place, weights, first, units, at, gather_sems) for at, (first, units) in enumerate(runs)]

    def gain_copy(step):
        mine = gain_buf.at[my_rows]
        other = lax.rem(place.dp + step, n_dp)
        return remote(mine, mine, gain_sems, step - 1, (other, place.seq))

    for step in range(1, n_dp):
        gain_copy(step).start()
    for item in gathers:
        item.start()
    gathers[0].to_plane()
    gathers[0].to_core()
    att_grad[...] = jnp.zeros_like(att_grad)
    gain_sums[...] = jnp.zeros_like(gain_sums)
    for step in range(1, n_dp):
        gain_copy(step).wait_recv()
    gains[...] = gain_buf[...].astype(F32).T[:8]
    gathers[0].finish()
    for item in gathers[1:]:
        item.to_plane()
    att_gathers, up_gather, down_gather = gathers[1:-2], gathers[-2], gathers[-1]

    sums = Sums(*sums_refs)

    def keys_step(index, carry):
        slot = lax.rem(index, 2)
        x_copy(index + 1).start()

        @pl.when(index >= 2)
        def _():
            write_copy(index - 2).wait()

        x_copy(index).wait()
        keys_phase(pool[slot], gains[0:1], weights, forms_ref, state.at[slot], local.at[slot])
        sums.start(slot, index)
        write_copy(index).start()

        @pl.when(index > 0)
        def _():
            sums.add(1 - slot, index - 1)

        return carry

    lax.fori_loop(0, count, keys_step, 0)
    for item in att_gathers:
        item.to_core()
    for item in att_gathers:
        item.finish()

    def front_step(index, carry):
        step = count + index
        slot = lax.rem(step, 2)

        @pl.when(index + 1 < count)
        def _():
            x_copy(step + 1).start()
            cot_copy(index + 1).start()

        write_copy(step - 2).wait()
        x_copy(step).wait()
        cot_copy(index).wait()
        sums.finish(index)
        mask = jnp.broadcast_to(mask_ref[pl.ds(index, 1)].astype(F32), (128, mask_ref.shape[1])).T
        front_phase(
            pool[slot], pool[2 + lax.rem(index, 2)], mask, gains[0:1], gains[1:2], full.at[index], weights, forms_ref,
            spread, state.at[slot], out_buf.at[index], n2_buf.at[index], dy_buf.at[index], scale_buf.at[index],
        )
        write_copy(step).start()

        @pl.when(index == 0)
        def _():
            sums.add((count - 1) % 2, count - 1)

        @pl.when(index == 1)
        def _():
            up_gather.to_core()

        @pl.when(index == 2)
        def _():
            down_gather.to_core()

        return carry

    lax.fori_loop(0, count, front_step, 0)
    up_gather.finish()
    down_gather.finish()
    for step in (2 * count - 2, 2 * count - 1):
        write_copy(step).wait()
    read_copy(0).start()
    read_copy(1).start()

    n_ffn = 2 * CHUNKS // group
    ffn_items = [Scatter(place, at, scatter_refs) for at in range(n_ffn)]
    if group == 1:
        items = ffn_items + [
            Scatter(place, n_ffn + at, scatter_refs, [att_grad.at[unit]])
            for at, unit in enumerate((OUT, KEY, VALUE, QUERY))
        ]
        early, late = [(items[n_ffn], [OUT])], [(items[n_ffn + 1 + at], [unit]) for at, unit in enumerate((KEY, VALUE, QUERY))]
    else:
        whole = Scatter(place, n_ffn, scatter_refs, [att_grad.at[unit] for unit in range(4)])
        items = ffn_items + [whole]
        early, late = [], [(whole, [KEY, VALUE, QUERY, OUT])]

    def put(item, unit, grads):
        if unit == 0 and item.index >= OUT_SLOTS:
            items[item.index - OUT_SLOTS].core_copy().wait_send()
        item.put(unit, grads)

    def whole_at(chunk):
        if chunk < 0 or chunk >= CHUNKS or (chunk + 1) % group:
            return []
        at = (chunk + 1) // group - 1
        return ffn_items[2 * at : 2 * at + 2]

    for chunk in range(CHUNKS):
        up_grad[...] = jnp.zeros_like(up_grad)
        down_grad[...] = jnp.zeros_like(down_grad)

        def ffn_step(index, carry, chunk=chunk):
            ffn_phase(
                chunk == 0, n2_buf[index], dy_buf[index], weights[UP + chunk], weights[DOWN + chunk], out_buf.at[index],
                pool.at[index], up_grad, down_grad,
            )
            if chunk == CHUNKS - 1:
                out_copy(index).start()

            @pl.when(index == 0)
            def _():
                for item in whole_at(chunk - 1):
                    item.to_plane()

            @pl.when(index == 1)
            def _():
                for item in whole_at(chunk - 2):
                    item.to_copies()

            @pl.when(index == count - 1)
            def _():
                for item in whole_at(chunk - 1):
                    item.to_z()

            return carry

        lax.fori_loop(0, count, ffn_step, 0)
        pair = ffn_items[2 * (chunk // group) : 2 * (chunk // group) + 2]
        put(pair[0], chunk % group, up_grad)
        put(pair[1], chunk % group, down_grad)
        for item in whole_at(chunk):
            item.start()

    grad_sums = Sums(place, local, arrived.at[pl.ds(count, count)], full.at[pl.ds(count, count)], rest[10:12], rest[12:14])
    grad_sums.add_sems = [ref.at[pl.ds(count, count)] for ref in rest[10:12]]
    grad_sums.full_sems = [ref.at[pl.ds(count, count)] for ref in rest[12:14]]

    def attention_step(index, carry):
        slot = lax.rem(index, 2)
        read_copy(index).wait()
        attention_grad_phase(
            dy_buf[index], pool[index], n2_buf[index], scale_buf[index][:, :1], gains[1:2], full.at[index], weights,
            back_ref, state.at[slot], spread, gain_sums.at[1:2], att_grad.at[OUT], da_buf.at[index],
            dq_buf.at[index], local.at[slot],
        )
        grad_sums.start(slot, index)
        read_copy(index + 2).start()

        @pl.when(index > 0)
        def _():
            grad_sums.add(1 - slot, index - 1)

        @pl.when(index == 0)
        def _():
            for item in whole_at(CHUNKS - 1):
                item.to_plane()
            for item in whole_at(CHUNKS - 2):
                item.to_copies()

        @pl.when(index == 2)
        def _():
            for item in whole_at(CHUNKS - 1):
                item.to_z()

        @pl.when(index == count - 1)
        def _():
            for item in whole_at(CHUNKS - 1):
                item.to_copies()

        return carry

    lax.fori_loop(0, count, attention_step, 0)
    for item, units in early:
        for at, unit in enumerate(units):
            put(item, at, att_grad.at[unit])
        item.start()
    x_copy(0).start()

    dk_buf, dv_buf = n2_buf, dy_buf

    def keys_grad_step(index, carry):
        event = count + index
        slot = lax.rem(event, 2)
        read_copy(event).wait()
        grad_sums.finish(index)
        keys_grad_phase(
            full.at[count + index], back_ref, state.at[slot], spread, dq_buf.at[index], dk_buf.at[index],
            dv_buf.at[index], att_grad,
        )

        @pl.when(index + 2 < count)
        def _():
            read_copy(event + 2).start()

        @pl.when(index == 0)
        def _():
            grad_sums.add((count - 1) % 2, count - 1)
            for item, _ in early:
                item.to_plane()

        @pl.when(index == 2)
        def _():
            for item, _ in early:
                item.to_z()

        return carry

    lax.fori_loop(0, count, keys_grad_step, 0)
    for item, units in late:
        for at, unit in enumerate(units):
            put(item, at, att_grad.at[unit])
        item.start()

    def input_grad_step(index, carry):
        slot = lax.rem(index, 2)

        @pl.when(index + 1 < count)
        def _():
            x_copy(index + 1).start()

        x_copy(index).wait()

        @pl.when(index >= 2)
        def _():
            grad_copy(index - 2).wait()

        input_grad_phase(
            pool[slot], da_buf[index], dq_buf[index], dk_buf[index], dv_buf[index], gains[0:1], weights,
            gain_sums.at[0:1], pool.at[2 + slot],
        )
        grad_copy(index).start()

        @pl.when(index == 0)
        def _():
            for item, _ in late:
                item.to_plane()
            for item, _ in early:
                item.to_copies()

        return carry

    lax.fori_loop(0, count, input_grad_step, 0)

    def mail_plane(step):
        mine = gain_mail.at[place.seq]
        return remote(mine, mine, mail_sems, step - 1, (place.dp, place.up_seq(step)))

    def mail_dp(step):
        mine = gain_mail.at[n_seq + place.dp]
        other = lax.rem(place.dp + step, n_dp)
        return remote(mine, mine, mail_sems, n_seq - 2 + step, (other, place.seq))

    gain_mail[place.seq] = gain_sums[...]
    for step in range(1, n_seq):
        mail_plane(step).start()
    for item, _ in late:
        item.to_z()
    for step in range(1, n_seq):
        mail_plane(step).wait_recv()
    total = gain_mail[0]
    for at in range(1, n_seq):
        total = total + gain_mail[at]
    gain_mail[n_seq + place.dp] = total
    for step in range(1, n_dp):
        mail_dp(step).start()
    for item, _ in late:
        item.to_copies()

    def ffn_results(at):
        return [ffn_items[2 * (chunk // group) + at].result(chunk % group) for chunk in range(CHUNKS)]

    for item in ffn_items:
        item.finish()
    up_rows = ffn_results(0)
    for r in range(n_dp):
        columns = [rows[:, r * own : r * own + own] for rows in up_rows]
        up_ref[:, r * CHUNKS * own : (r + 1) * CHUNKS * own] = jnp.concatenate(columns, axis=1)
    for chunk, rows in enumerate(ffn_results(1)):
        down_ref[chunk * own : chunk * own + own] = rows
    for step in range(1, n_dp):
        mail_dp(step).wait_recv()
    total = gain_mail[n_seq]
    for at in range(1, n_dp):
        total = total + gain_mail[n_seq + at]
    gain_grads_ref[...] = total
    for item, units in early + late:
        item.finish()
        for at, unit in enumerate(units):
            att_ref[unit] = item.result(at)

    for item in items:
        item.drain(core=item.index + OUT_SLOTS >= len(items))
    for step in range(1, n_seq):
        mail_plane(step).wait_send()
    for step in range(1, n_dp):
        mail_dp(step).wait_send()
        gain_copy(step).wait_send()
    for item in gathers:
        item.drain()
    for index in range(count):
        sums.drain(index)
        grad_sums.drain(index)
        out_copy(index).wait()
    for index in (count - 2, count - 1):
        grad_copy(index).wait()


def on_device(sizes, inputs, cotangent, masked, proj_seed, gain_attn, w_query, w_key, w_value, w_out, gain_ffn, w_up, w_down):
    n_dp, n_seq = sizes
    count, length = inputs.shape[0], inputs.shape[1]
    own, own_ff = D // n_dp, FF // n_dp
    group = max(1, n_seq // (D // 128))
    n_gathers = 4 if group == 1 else 3
    n_ffn = 2 * CHUNKS // group
    n_items = n_ffn + 4 // group
    part_rows = HEADS * HEAD_DIM // n_seq + 16
    forms, back = feature_forms(proj_seed[0])
    gains = jnp.pad(jnp.stack([gain_attn, gain_ffn], axis=1).astype(LOW), ((0, 0), (0, 126)))
    sd = jax.ShapeDtypeStruct
    vmem = pl.BlockSpec(memory_space=pltpu.VMEM)
    anywhere = pl.BlockSpec(memory_space=pl.ANY)
    outputs, input_grad, gain_grads, att, up, down, _ = pl.pallas_call(
        functools.partial(layer_kernel, sizes),
        in_specs=[anywhere, anywhere] + [vmem] * 10,
        out_specs=[anywhere, anywhere] + [vmem] * 4 + [anywhere],
        out_shape=[
            sd((count, length, D), F32), sd((count, length, D), F32), sd((8, D), F32), sd((4, own, D), F32),
            sd((own, FF), F32), sd((own_ff, D), F32), sd((2 * count, length, STATE), LOW),
        ],
        scratch_shapes=[
            pltpu.VMEM((UNITS, D, D), LOW), pltpu.VMEM((D, 128), LOW), pltpu.VMEM((8, D), F32),
            pltpu.VMEM((4, D, D), F32), pltpu.VMEM((D, D), F32), pltpu.VMEM((D, D), F32),
            pltpu.VMEM((8, D), F32), pltpu.VMEM((n_seq + n_dp, 8, D), F32),
            pltpu.VMEM((2, n_seq, part_rows, 256), LOW), pltpu.VMEM((2 * count, n_seq - 1, part_rows, 256), LOW),
            pltpu.VMEM((2 * count, n_seq, part_rows, 256), LOW),
            pltpu.VMEM((2, length, STATE), LOW), pltpu.VMEM((HEADS, 256, 256), LOW),
            pltpu.VMEM((count, length, D), LOW), pltpu.VMEM((count, length, D), LOW),
            pltpu.VMEM((count, length, D), LOW), pltpu.VMEM((count, length, D), LOW),
            pltpu.VMEM((count, length, D), F32), pltpu.VMEM((max(count, 4), length, D), F32),
            pltpu.VMEM((count, length, 128), F32),
            *[pltpu.SemaphoreType.DMA((2,)) for _ in range(4)],
            pltpu.SemaphoreType.DMA((count,)), pltpu.SemaphoreType.DMA((2,)),
            *semaphores(n_gathers, n_dp // 2 - 1), *semaphores(n_gathers, n_dp // 2 - 1, n_seq - 1),
            *semaphores(n_gathers, n_dp // 2),
            *semaphores(n_dp - 1), *semaphores(n_seq + n_dp - 2),
            *semaphores(2 * count, n_seq - 1), *semaphores(2 * count, n_seq - 1),
            *Scatter.shapes(n_dp, n_seq, n_items, n_ffn),
        ],
        compiler_params=pltpu.CompilerParams(
            vmem_limit_bytes=63 * 2**20, collective_id=0, has_side_effects=True
        ),
        name="layer",
    )(inputs, cotangent, masked, gains, w_query, w_key, w_value, w_out, w_up, w_down, forms, back)
    gain_grads = lax.dynamic_slice(gain_grads, (0, lax.axis_index("dp") * own), (2, own))
    return (
        outputs, input_grad, gain_grads[0], att[QUERY], att[KEY], att[VALUE], att[OUT], gain_grads[1], up, down,
    )


def solution(mesh):
    in_specs = (
        P("dp", "seq", None),
        P("dp", "seq", None),
        P("dp", "seq"),
        P(),
        P("dp"),
        P("dp", None),
        P("dp", None),
        P("dp", None),
        P("dp", None),
        P("dp"),
        P("dp", None),
        P("dp", None),
    )
    out_specs = (
        P("dp", "seq", None),
        P("dp", "seq", None),
        P("dp"),
        P("dp", None),
        P("dp", None),
        P("dp", None),
        P("dp", None),
        P("dp"),
        P("dp", None),
        P("dp", None),
    )
    sizes = (mesh.shape["dp"], mesh.shape["seq"])
    return jax.shard_map(functools.partial(on_device, sizes), mesh=mesh, in_specs=in_specs, out_specs=out_specs, check_vma=False)
```

```python
import functools
import math

import jax
import jax.numpy as jnp
from jax import lax
from jax.experimental import pallas as pl
from jax.experimental.pallas import tpu as pltpu
from jax.sharding import PartitionSpec as P

D = 512
HEADS = 8
PAIRS = 4
HEAD_DIM = 64
FEATURES = 256
FF = 2048
CHUNKS = 4
KEY, VALUE, QUERY, OUT, UP, DOWN, UNITS = 0, 1, 2, 3, 4, 5, 12

epsilon = 1e-05
LOG2E = math.log2(math.e)
LOW = jnp.bfloat16
F32 = jnp.float32
MESH = pl.DeviceIdType.MESH


def scramble(hashed):
    return jnp.bitwise_xor(hashed, lax.shift_right_logical(hashed, jnp.full_like(hashed, 16)))


def uniform_entries(counter, seed):
    hashed = counter * 1664525 + seed * 22695477 + 1013904223
    hashed = scramble(hashed) * 73244475
    hashed = scramble(hashed) * 73244475
    hashed = scramble(hashed)
    low_bits = jnp.bitwise_and(hashed, 8388607)
    return (low_bits.astype(F32) + 0.5) * (1.0 / 8388608.0)


def direction_entries(index, seed):
    radius = jnp.sqrt(-2.0 * jnp.log(uniform_entries(index, seed)))
    turn = uniform_entries(index + FEATURES * HEAD_DIM, seed)
    return radius * jnp.cos(2.0 * math.pi * turn)


def feature_forms(seed, forms_ref, back_ref):
    col = lax.broadcasted_iota(jnp.int32, (HEAD_DIM, FEATURES), 1)
    row = lax.broadcasted_iota(jnp.int32, (HEAD_DIM, FEATURES), 0)
    dirs_t = direction_entries(col * HEAD_DIM + row, seed) * HEAD_DIM ** (-0.25)
    scaled = dirs_t * LOG2E
    high = scaled.astype(LOW)
    rest = (scaled - high.astype(F32)).astype(LOW)
    minus = jnp.full((HEAD_DIM, FEATURES), -1.0, LOW)
    for half, pieces in enumerate(((high, high, rest, minus), (high, high, minus, rest))):
        for at, piece in enumerate(pieces):
            forms_ref[half, at * HEAD_DIM : at * HEAD_DIM + HEAD_DIM] = piece
    one, zero = jnp.ones((FEATURES, HEAD_DIM), F32), jnp.zeros((FEATURES, HEAD_DIM), F32)
    back = dirs_t.T
    back_ref[:FEATURES] = jnp.concatenate([back, zero, one, zero], axis=1).astype(LOW)
    back_ref[FEATURES:] = jnp.concatenate([zero, back, zero, one], axis=1).astype(LOW)


def dot(left, right):
    return jnp.dot(left, right, preferred_element_type=F32)


def dot_nt(left, right):
    return lax.dot_general(left, right, (((1,), (1,)), ((), ())), preferred_element_type=F32)


def dot_tn(left, right):
    return lax.dot_general(left, right, (((0,), (0,)), ((), ())), preferred_element_type=F32)


def normalize(values):
    centred = values - jnp.mean(values, axis=-1, keepdims=True)
    scale = lax.rsqrt(jnp.mean(centred * centred, axis=-1, keepdims=True) + epsilon)
    return centred * scale, scale


def norm_grad(grad_normed, unit_rows, scale, gain):
    scaled_grad = grad_normed * gain
    first = jnp.mean(scaled_grad, axis=-1, keepdims=True)
    second = jnp.mean(scaled_grad * unit_rows, axis=-1, keepdims=True)
    return scale * (scaled_grad - first - unit_rows * second)


def pair_lanes(pair, base=0):
    return slice(base + pair * 128, base + pair * 128 + 128)


def head_lanes(head):
    return slice(head * 256, head * 256 + 256)


def feature_pair(rows, forms_ref):
    high = rows.astype(LOW)
    rest = (rows - high.astype(F32)).astype(LOW)
    square = (rows * rows * (LOG2E / 16.0) + 1.0 / 16.0).astype(LOW)
    h0, h1 = high[:, :64], high[:, 64:]
    r0, r1 = rest[:, :64], rest[:, 64:]
    s0, s1 = square[:, :64], square[:, 64:]
    left0 = jnp.concatenate([r0, h0, h0, s0], axis=1)
    left1 = jnp.concatenate([h1, r1, s1, h1], axis=1)
    return jnp.exp2(dot(left0, forms_ref[0])), jnp.exp2(dot(left1, forms_ref[1]))


def sums_place(parts, head):
    step = HEADS * HEAD_DIM // parts
    block = min(step, HEAD_DIM)
    runs = [divmod(head * HEAD_DIM + at, step) + (at, block) for at in range(0, HEAD_DIM, block)]
    part = head * HEAD_DIM // step
    return runs, part, step + head - -(-part * step // HEAD_DIM)


def put_sums(sums_ref, head, rows, totals):
    runs, part, row = sums_place(sums_ref.shape[0], head)
    for run_part, run_row, at, block in runs:
        sums_ref[run_part, run_row : run_row + block] = rows[at : at + block].astype(LOW)
    sums_ref[part, row : row + 1] = totals.astype(LOW)


def get_sums(sums_ref, head):
    runs, part, row = sums_place(sums_ref.shape[0], head)
    rows = [sums_ref[run_part, run_row : run_row + block] for run_part, run_row, _, block in runs]
    rows = rows[0] if len(rows) == 1 else jnp.concatenate(rows, axis=0)
    return rows, sums_ref[part, row : row + 1].astype(F32)


def spread_sums(sums_ref, spread_ref):
    for head in range(HEADS):
        own, other = (head % 2) * 64, 64 - (head % 2) * 64
        rows, totals = get_sums(sums_ref, head)
        spread_ref[head, own : own + 64] = rows
        spread_ref[head, 128 + own : 192 + own] = jnp.broadcast_to(totals, (64, 256)).astype(LOW)
        spread_ref[head, other : other + 64] = jnp.zeros((64, 256), LOW)
        spread_ref[head, 128 + other : 192 + other] = jnp.zeros((64, 256), LOW)


def spread_grads(sums_ref, spread_ref):
    for head in range(HEADS):
        own, other = (head % 2) * 64, 64 - (head % 2) * 64
        rows, totals = get_sums(sums_ref, head)
        spread_ref[head, own : own + 64] = rows
        spread_ref[head, other : other + 64] = jnp.zeros((64, 256), LOW)
        row = lax.broadcasted_iota(jnp.int32, (128, 256), 0)
        spread_ref[head, 128:] = jnp.where(row == 0, jnp.broadcast_to(totals, (128, 256)), 0.0).astype(LOW)


def keys_phase(x, gain, weights, forms_ref, state_ref, sums_ref):
    unit, _ = normalize(x)
    normed = (unit * gain).astype(LOW)
    state_ref[:, 3072:3584] = normed
    values = dot(normed, weights[VALUE]).astype(LOW)
    state_ref[:, 2560:3072] = values
    keys = dot(normed, weights[KEY])
    state_ref[:, 2048:2560] = keys.astype(LOW)
    ones = jnp.ones((16, x.shape[0]), LOW)
    for pair in range(PAIRS):
        phi = feature_pair(keys[:, pair_lanes(pair)], forms_ref)
        values_t = values[:, pair_lanes(pair)].T
        for half in range(2):
            head = 2 * pair + half
            low = phi[half].astype(LOW)
            state_ref[:, head_lanes(head)] = low
            left = jnp.concatenate([values_t[half * 64 : half * 64 + 64], ones], axis=0)
            got = dot(left, low)
            put_sums(sums_ref, head, got[:64], got[64:65])


def front_phase(x, upstream, mask, gain_one, gain_two, sums_arrive, sums_ref, weights, forms_ref, spread_ref, state_ref, out_ref, n2_ref, dy_ref, scale_ref):
    unit, _ = normalize(x)
    queries = dot((unit * gain_one).astype(LOW), weights[QUERY])
    state_ref[:, 2048:2560] = queries.astype(LOW)
    for pair in range(PAIRS):
        phi0, phi1 = feature_pair(queries[:, pair_lanes(pair)], forms_ref)
        state_ref[:, head_lanes(2 * pair)] = phi0.astype(LOW)
        state_ref[:, head_lanes(2 * pair + 1)] = phi1.astype(LOW)
    lanes = mask.shape[1]
    for at in range(0, D, lanes):
        dy_ref[:, at : at + lanes] = (upstream[:, at : at + lanes] * mask).astype(LOW)
    sums_arrive()
    spread_sums(sums_ref, spread_ref)
    for pair in range(PAIRS):
        low0, low1 = state_ref[:, head_lanes(2 * pair)], state_ref[:, head_lanes(2 * pair + 1)]
        both = dot_nt(low0, spread_ref[2 * pair]) + dot_nt(low1, spread_ref[2 * pair + 1])
        reciprocal = 1.0 / both[:, 128:]
        state_ref[:, pair_lanes(pair, 2560)] = (both[:, :128] * reciprocal).astype(LOW)
        state_ref[:, pair_lanes(pair, 3072)] = reciprocal.astype(LOW)
    mid = x + dot(state_ref[:, 2560:3072], weights[OUT])
    unit, scale = normalize(mid)
    n2_ref[...] = (unit * gain_two).astype(LOW)
    scale_ref[...] = jnp.broadcast_to(scale, scale_ref.shape)
    out_ref[...] = mid


def ffn_phase(first, n2, dy, w_up, w_down, out_ref, low_out_ref, dn2_ref, up_grad_ref, down_grad_ref):
    hidden = dot(n2, w_up)
    cumulative = 0.5 * (1.0 + lax.erf(hidden * (1.0 / math.sqrt(2.0))))
    density = jnp.exp2(hidden * hidden * (-0.5 * LOG2E)) * (1.0 / math.sqrt(2.0 * math.pi))
    act = (hidden * cumulative).astype(LOW)
    du = (dot_nt(dy, w_down) * (cumulative + hidden * density)).astype(LOW)
    if low_out_ref is None:
        out_ref[...] += dot(act, w_down)
    else:
        low_out_ref[...] = (out_ref[...] + dot(act, w_down)).astype(LOW)
    down_grad_ref[...] += dot_tn(act, dy)
    dn2 = dot_nt(du, w_up)
    if first:
        dn2_ref[...] = dn2
    else:
        dn2_ref[...] += dn2
    up_grad_ref[...] += dot_tn(n2, du)


def attention_grad_phase(dy, dn2, n2, scale, gain, sums_ref, weights, back_ref, state_ref, spread_ref, gain_grad_ref, w_out_grad_ref, da_ref, dq_ref, grad_sums_ref):
    spread_sums(sums_ref, spread_ref)
    unit = n2.astype(F32) * (1.0 / gain)
    gain_grad_ref[...] += jnp.sum(dn2 * unit, axis=0, keepdims=True)
    da = (dy.astype(F32) + norm_grad(dn2, unit, scale, gain)).astype(LOW)
    da_ref[...] = da
    w_out_grad_ref[...] += dot_tn(state_ref[:, 2560:3072], da)
    datt = dot_nt(da, weights[OUT])
    for pair in range(PAIRS):
        dnumer = datt[:, pair_lanes(pair)] * state_ref[:, pair_lanes(pair, 3072)].astype(F32)
        weighted = -dnumer * state_ref[:, pair_lanes(pair, 2560)].astype(F32)
        left = jnp.concatenate([dnumer.astype(LOW), weighted.astype(LOW)], axis=1)
        left_t = left.T
        parts = []
        for half in range(2):
            head, own = 2 * pair + half, half * 64
            pq = state_ref[:, head_lanes(head)]
            dden = jnp.sum(left_t[128 + own : 192 + own].astype(F32), axis=0, keepdims=True)
            rows = jnp.concatenate(
                [left_t[own : own + 64], jnp.broadcast_to(dden, (16, dden.shape[1])).astype(LOW)], axis=0
            )
            got = dot(rows, pq)
            put_sums(grad_sums_ref, head, got[:64], got[64:65])
            parts.append((dot(left, spread_ref[head]) * pq.astype(F32)).astype(LOW))
        grads = dot(parts[0], back_ref[:256]) + dot(parts[1], back_ref[256:])
        q = state_ref[:, pair_lanes(pair, 2048)].astype(F32)
        dq_ref[:, pair_lanes(pair)] = (grads[:, :128] - grads[:, 128:] * q * 0.125).astype(LOW)


def keys_grad_phase(sums_ref, back_ref, state_ref, spread_ref, dq_ref, dk_ref, dv_ref, att_grad_ref):
    spread_grads(sums_ref, spread_ref)
    ones = jnp.ones((dk_ref.shape[0], 128), LOW)
    for pair in range(PAIRS):
        left = jnp.concatenate([state_ref[:, pair_lanes(pair, 2560)], ones], axis=1)
        parts = []
        dv = None
        for half in range(2):
            head = 2 * pair + half
            pk = state_ref[:, head_lanes(head)]
            parts.append((dot(left, spread_ref[head]) * pk.astype(F32)).astype(LOW))
            piece = dot_nt(pk, spread_ref[head, :128])
            dv = piece if dv is None else dv + piece
        dv_ref[:, pair_lanes(pair)] = dv.astype(LOW)
        grads = dot(parts[0], back_ref[:256]) + dot(parts[1], back_ref[256:])
        k = state_ref[:, pair_lanes(pair, 2048)].astype(F32)
        dk_ref[:, pair_lanes(pair)] = (grads[:, :128] - grads[:, 128:] * k * 0.125).astype(LOW)
    normed = state_ref[:, 3072:3584]
    att_grad_ref[KEY] += dot_tn(normed, dk_ref[...])
    att_grad_ref[VALUE] += dot_tn(normed, dv_ref[...])
    att_grad_ref[QUERY] += dot_tn(normed, dq_ref[...])


def input_grad_phase(x, da_ref, dq, dk, dv, gain, weights, gain_grad_ref):
    dn1 = dot_nt(dq, weights[QUERY]) + dot_nt(dk, weights[KEY]) + dot_nt(dv, weights[VALUE])
    unit, scale = normalize(x)
    gain_grad_ref[...] += jnp.sum(dn1 * unit, axis=0, keepdims=True)
    da_ref[...] = (da_ref[...].astype(F32) + norm_grad(dn1, unit, scale, gain)).astype(LOW)


class Place:
    def __init__(self, n_dp, n_seq):
        self.n_dp, self.n_seq, self.n_z = n_dp, n_seq, n_dp // 2
        self.dp, self.seq = lax.axis_index("dp"), lax.axis_index("seq")
        self.z, self.core = self.dp // 2, lax.rem(self.dp, 2)

    def up_z(self, step):
        return lax.rem(self.z + step, self.n_z)

    def up_seq(self, step):
        return lax.rem(self.seq + step, self.n_seq)

    def down_z(self, step):
        return lax.rem(self.z + (self.n_z - step), self.n_z)

    def owner(self, z):
        return z * 2 + self.core

    def other_core(self):
        return (self.z * 2 + 1 - self.core, self.seq)

    def arrive(self):
        barrier = pltpu.get_barrier_semaphore()
        for step in range(1, self.n_dp):
            other = lax.rem(self.dp + step, self.n_dp)
            pl.semaphore_signal(barrier, inc=1, device_id=(other, self.seq), device_id_type=MESH)
        for step in range(1, self.n_seq):
            pl.semaphore_signal(barrier, inc=1, device_id=(self.dp, self.up_seq(step)), device_id_type=MESH)

    def meet(self):
        pl.semaphore_wait(pltpu.get_barrier_semaphore(), self.n_dp - 1 + self.n_seq - 1)


def remote(source, target, sems, at, device):
    return pltpu.make_async_remote_copy(
        src_ref=source, dst_ref=target, send_sem=sems[0].at[at], recv_sem=sems[1].at[at],
        device_id=device, device_id_type=MESH,
    )


def semaphores(*shape):
    return [pltpu.SemaphoreType.DMA(shape), pltpu.SemaphoreType.DMA(shape)]


class Gather:
    def __init__(self, place, weights, first, count, index, sems, line=False):
        self.place, self.weights, self.first, self.count, self.index = place, weights, first, count, index
        self.line = line
        self.own = D // place.n_dp
        self.across = min(place.n_seq, D // 128)
        self.units = count // (place.n_seq // self.across)
        self.z_sems, self.plane_sems, self.core_sems = sems

    def rows(self, owner):
        return pl.ds(pl.multiple_of(owner * self.own, self.own), self.own)

    def piece(self, owner, part):
        columns = D // self.across
        first = self.first + (part // self.across) * self.units
        left = pl.multiple_of(lax.rem(part, self.across) * columns, 128)
        return self.weights.at[pl.ds(first, self.units), self.rows(owner), pl.ds(left, columns)]

    def shard(self, owner):
        return self.weights.at[pl.ds(self.first, self.count), self.rows(owner)]

    def z_copy(self, step):
        place = self.place
        piece = self.shard(place.dp) if self.line else self.piece(place.dp, place.seq)
        return remote(piece, piece, self.z_sems, (self.index, step - 1), (place.owner(place.up_z(step)), place.seq))

    def plane_copy(self, step, to):
        place = self.place
        piece = self.piece(place.owner(place.down_z(step)), place.seq)
        return remote(piece, piece, self.plane_sems, (self.index, step - 1, to - 1), (place.dp, place.up_seq(to)))

    def core_copy(self, step):
        shard = self.shard(self.place.owner(self.place.down_z(step)))
        return remote(shard, shard, self.core_sems, (self.index, step), self.place.other_core())

    def start(self):
        for step in range(1, self.place.n_z):
            self.z_copy(step).start()
        self.core_copy(0).start()

    def to_plane(self):
        for step in range(1, self.place.n_z):
            self.z_copy(step).wait_recv()
            for to in range(1, self.place.n_seq):
                self.plane_copy(step, to).start()

    def to_core(self):
        for step in range(1, self.place.n_z):
            if self.line:
                self.z_copy(step).wait_recv()
            else:
                for to in range(1, self.place.n_seq):
                    self.plane_copy(step, to).wait_recv()
            self.core_copy(step).start()

    def finish(self):
        for step in range(self.place.n_z):
            self.core_copy(step).wait_recv()

    def drain(self):
        for step in range(1, self.place.n_z):
            self.z_copy(step).wait_send()
            if not self.line:
                for to in range(1, self.place.n_seq):
                    self.plane_copy(step, to).wait_send()
        for step in range(self.place.n_z):
            self.core_copy(step).wait_send()


class Sums:
    def __init__(self, place, local, arrived, full, add_sems, full_sems):
        self.place, self.local, self.arrived, self.full = place, local, arrived, full
        self.add_sems, self.full_sems = add_sems, full_sems

    def add_copy(self, slot, index, to):
        other = self.place.up_seq(to)
        return remote(
            self.local.at[slot, other], self.arrived.at[index, to - 1], self.add_sems, (index, to - 1),
            (self.place.dp, other),
        )

    def full_copy(self, index, to):
        place = self.place
        mine = self.full.at[index, place.seq]
        return remote(mine, mine, self.full_sems, (index, to - 1), (place.dp, place.up_seq(to)))

    def start(self, slot, index):
        for to in range(1, self.place.n_seq):
            self.add_copy(slot, index, to).start()

    def add(self, slot, index):
        place = self.place
        total = self.local[slot, place.seq].astype(F32)
        for to in range(1, place.n_seq):
            self.add_copy(slot, index, to).wait_recv()
            total = total + self.arrived[index, to - 1].astype(F32)
        self.full[index, place.seq] = total.astype(LOW)
        for to in range(1, place.n_seq):
            self.full_copy(index, to).start()
        for to in range(1, place.n_seq):
            self.add_copy(slot, index, to).wait_send()

    def finish(self, index):
        for to in range(1, self.place.n_seq):
            self.full_copy(index, to).wait_recv()

    def drain(self, index):
        for to in range(1, self.place.n_seq):
            self.full_copy(index, to).wait_send()


OUT_SLOTS = 4


class Scatter:
    def __init__(self, place, index, refs, kept=None, z_first=False):
        self.place, self.index, self.slot, self.kept = place, index, index % OUT_SLOTS, kept
        self.z_first = z_first
        self.out, self.mine, self.arrived, self.first, self.second, self.final = refs[:6]
        self.core_sems, self.plane_sems, self.z_sems, self.full_sems = refs[6:8], refs[8:10], refs[10:12], refs[12:14]
        self.own = D // place.n_dp
        self.across = min(place.n_seq, D // 128)
        self.lanes = D // self.across
        self.n_first, self.n_second = (place.n_z, place.n_seq) if z_first else (place.n_seq, place.n_z)

    @staticmethod
    def shapes(n_dp, n_seq, items, held):
        own, n_z = D // n_dp, n_dp // 2
        part = (own, D // min(n_seq, D // 128))
        return [
            pltpu.VMEM((OUT_SLOTS, n_seq, n_z) + part, LOW), pltpu.VMEM((held, n_seq, n_z) + part, LOW),
            pltpu.VMEM((items, n_seq, n_z) + part, LOW),
            pltpu.VMEM((items, max((n_seq - 1) * n_z, (n_z - 1) * n_seq)) + part, LOW),
            pltpu.VMEM((items, 2 * max(n_z, n_seq) - 1) + part, LOW), pltpu.VMEM((items, n_seq) + part, LOW),
            *semaphores(items), *semaphores(items, n_seq - 1), *semaphores(items, n_z - 1), *semaphores(items, n_seq - 1),
        ]

    def block(self, grads, owner, lane_part):
        rows = pl.ds(pl.multiple_of(owner * self.own, self.own), self.own)
        return grads[rows, lane_part * self.lanes : lane_part * self.lanes + self.lanes]

    def core_copy(self):
        return remote(
            self.out.at[self.slot], self.arrived.at[self.index], self.core_sems, self.index, self.place.other_core()
        )

    def axis_copy(self, along_z, step, source, target):
        place = self.place
        if along_z:
            return remote(
                source, target, self.z_sems, (self.index, step - 1), (place.owner(place.up_z(step)), place.seq)
            )
        return remote(source, target, self.plane_sems, (self.index, step - 1), (place.dp, place.up_seq(step)))

    def first_copy(self, step):
        place = self.place
        arrived = self.arrived.at[self.index]
        source = arrived.at[:, place.up_z(step)] if self.z_first else arrived.at[place.up_seq(step)]
        target = self.first.at[self.index, pl.ds((step - 1) * self.n_second, self.n_second)]
        return self.axis_copy(self.z_first, step, source, target)

    def second_copy(self, step):
        place = self.place
        other = place.up_seq(step) if self.z_first else place.up_z(step)
        return self.axis_copy(
            not self.z_first, step, self.second.at[self.index, other],
            self.second.at[self.index, self.n_second + step - 1],
        )

    def full_copy(self, to):
        place = self.place
        mine = self.final.at[self.index, place.seq]
        return remote(mine, mine, self.full_sems, (self.index, to - 1), (place.dp, place.up_seq(to)))

    def put(self, unit, grads):
        place = self.place
        for lane_part in range(self.across):
            part = unit * self.across + lane_part
            for z in range(place.n_z):
                self.out[self.slot, part, z] = self.block(grads, z * 2 + 1 - place.core, lane_part).astype(LOW)
                if self.kept is None:
                    self.mine[self.index, part, z] = self.block(grads, place.owner(z), lane_part).astype(LOW)

    def start(self):
        self.core_copy().start()

    def to_first(self):
        place = self.place
        self.core_copy().wait_recv()
        for part in range(place.n_seq):
            for z in range(place.n_z):
                if self.kept is None:
                    mine = self.mine[self.index, part, z].astype(F32)
                else:
                    mine = self.block(self.kept[part // self.across], place.owner(z), part % self.across)
                self.arrived[self.index, part, z] = (mine + self.arrived[self.index, part, z].astype(F32)).astype(LOW)
        for step in range(1, self.n_first):
            self.first_copy(step).start()

    def to_second(self):
        place = self.place
        for step in range(1, self.n_first):
            self.first_copy(step).wait_recv()
        for at in range(self.n_second):
            total = self.arrived[self.index, at, place.z] if self.z_first else self.arrived[self.index, place.seq, at]
            total = total.astype(F32)
            for step in range(1, self.n_first):
                total = total + self.first[self.index, (step - 1) * self.n_second + at].astype(F32)
            self.second[self.index, at] = total.astype(LOW)
        for step in range(1, self.n_second):
            self.second_copy(step).start()

    def to_copies(self):
        place = self.place
        total = self.second[self.index, place.seq if self.z_first else place.z].astype(F32)
        for step in range(1, self.n_second):
            self.second_copy(step).wait_recv()
            total = total + self.second[self.index, self.n_second + step - 1].astype(F32)
        self.final[self.index, place.seq] = total.astype(LOW)
        for to in range(1, place.n_seq):
            self.full_copy(to).start()

    def finish(self):
        for to in range(1, self.place.n_seq):
            self.full_copy(to).wait_recv()

    def result(self, unit):
        parts = [self.final[self.index, unit * self.across + at] for at in range(self.across)]
        return jnp.concatenate(parts, axis=1)

    def drain(self, core=True):
        if core:
            self.core_copy().wait_send()
        for step in range(1, self.n_first):
            self.first_copy(step).wait_send()
        for step in range(1, self.n_second):
            self.second_copy(step).wait_send()
        for to in range(1, self.place.n_seq):
            self.full_copy(to).wait_send()


STATE = 2048 + 3 * D


def layer_kernel(
    sizes, x_hbm, cot_hbm, mask_ref, gains_own, wq, wk, wv, wo, wu, wd, seed_ref,
    out_hbm, grad_hbm, gain_grads_ref, dwk, dwv, dwq, dwo, up_ref, down_ref, state_hbm,
    weights, gain_buf, gains, att_grad, up_grad, down_grad, gain_sums, gain_mail,
    local, arrived, full, state, spread, n2_buf, dy_buf, da_buf, dq_buf, out_buf, pool, scale_buf,
    forms_ref, back_ref, x_sems, cot_sems, write_sems, read_sems, out_sems, grad_sems, *rest,
):
    n_dp, n_seq = sizes
    count = x_hbm.shape[0]
    own = D // n_dp
    place = Place(n_dp, n_seq)
    group = max(1, n_seq // (D // 128))
    gather_sems = (rest[0:2], rest[2:4], rest[4:6])
    gain_sems, mail_sems = rest[6:8], rest[8:10]
    sums_refs = (place, local, arrived, full, rest[10:12], rest[12:14])
    scatter_refs = rest[14:]

    my_rows = pl.ds(pl.multiple_of(place.dp * own, own), own)

    def x_copy(step):
        slot = lax.rem(step, 2)
        return pltpu.make_async_copy(x_hbm.at[lax.rem(step, count)], pool.at[slot], x_sems.at[slot])

    def cot_copy(index):
        slot = lax.rem(index, 2)
        return pltpu.make_async_copy(cot_hbm.at[index], pool.at[2 + slot], cot_sems.at[slot])

    def write_copy(step):
        slot = lax.rem(step, 2)
        return pltpu.make_async_copy(state.at[slot], state_hbm.at[step], write_sems.at[slot])

    def read_copy(event):
        slot = lax.rem(event, 2)
        return pltpu.make_async_copy(
            state_hbm.at[lax.rem(count + event, 2 * count)], state.at[slot], read_sems.at[slot]
        )

    def out_copy(index):
        return pltpu.make_async_copy(da_buf.at[index], out_hbm.at[index], out_sems.at[index])

    def grad_copy(index):
        return pltpu.make_async_copy(da_buf.at[index], grad_hbm.at[index], grad_sems.at[index])

    place.arrive()
    x_copy(0).start()
    cot_copy(0).start()
    for unit, ref in ((KEY, wk), (VALUE, wv), (QUERY, wq), (OUT, wo)):
        weights[unit, my_rows] = ref[...].astype(LOW)
    for chunk in range(CHUNKS):
        columns = [wu[:, (r * CHUNKS + chunk) * own : (r * CHUNKS + chunk + 1) * own] for r in range(n_dp)]
        weights[UP + 2 * chunk, my_rows] = jnp.concatenate(columns, axis=1).astype(LOW)
        weights[DOWN + 2 * chunk, my_rows] = wd[chunk * own : chunk * own + own].astype(LOW)
    gain_buf[my_rows] = gains_own[...]
    place.meet()

    runs = [(KEY, 2), (QUERY, 2)] if group == 1 else [(KEY, 4)]
    gathers = [Gather(place, weights, first, units, at, gather_sems, line=at > 0) for at, (first, units) in enumerate(runs)]
    keys_gathers, att_gathers = gathers[:1], gathers[1:]
    ffn_gathers = [
        Gather(place, weights, UP + 2 * chunk, 2, len(runs) + chunk, gather_sems, line=True) for chunk in range(CHUNKS)
    ]
    gathers = gathers + ffn_gathers

    def gain_copy(step):
        mine = gain_buf.at[my_rows]
        other = lax.rem(place.dp + step, n_dp)
        return remote(mine, mine, gain_sems, step - 1, (other, place.seq))

    for step in range(1, n_dp):
        gain_copy(step).start()
    for item in keys_gathers:
        item.start()
    feature_forms(seed_ref[0], forms_ref, back_ref)
    gathers[0].to_plane()
    att_grad[...] = jnp.zeros_like(att_grad)
    gain_sums[...] = jnp.zeros_like(gain_sums)
    for item in keys_gathers[1:]:
        item.to_core()
    for item in att_gathers + ffn_gathers[:1]:
        item.start()
    gathers[0].to_core()
    for step in range(1, n_dp):
        gain_copy(step).wait_recv()
    gains[...] = gain_buf[...].astype(F32).T[:8]
    for item in keys_gathers:
        item.finish()

    sums = Sums(*sums_refs)

    def keys_step(index, carry):
        slot = lax.rem(index, 2)
        x_copy(index + 1).start()

        @pl.when(index >= 2)
        def _():
            write_copy(index - 2).wait()

        x_copy(index).wait()
        keys_phase(pool[slot], gains[0:1], weights, forms_ref, state.at[slot], local.at[slot])
        sums.start(slot, index)
        write_copy(index).start()

        @pl.when(index > 0)
        def _():
            sums.add(1 - slot, index - 1)

        @pl.when(index == 2)
        def _():
            for item in att_gathers:
                item.to_core()
            ffn_gathers[1].start()

        return carry

    lax.fori_loop(0, count, keys_step, 0)
    for item in att_gathers:
        item.finish()

    def front_step(index, carry):
        step = count + index
        slot = lax.rem(step, 2)

        @pl.when(index + 1 < count)
        def _():
            x_copy(step + 1).start()
            cot_copy(index + 1).start()

        write_copy(step - 2).wait()
        x_copy(step).wait()
        cot_copy(index).wait()

        def sums_arrive():
            @pl.when(index == 0)
            def _():
                sums.add((count - 1) % 2, count - 1)

            sums.finish(index)

        mask = jnp.broadcast_to(mask_ref[pl.ds(index, 1)].astype(F32), (128, mask_ref.shape[1])).T
        front_phase(
            pool[slot], pool[2 + lax.rem(index, 2)], mask, gains[0:1], gains[1:2], sums_arrive, full.at[index], weights, forms_ref,
            spread, state.at[slot], out_buf.at[index], n2_buf.at[index], dy_buf.at[index], scale_buf.at[index],
        )
        write_copy(step).start()

        @pl.when(index == 1)
        def _():
            ffn_gathers[0].to_core()
            ffn_gathers[2].start()

        @pl.when(index == count - 1)
        def _():
            ffn_gathers[1].to_core()
            ffn_gathers[3].start()

        return carry

    lax.fori_loop(0, count, front_step, 0)
    for step in (2 * count - 2, 2 * count - 1):
        write_copy(step).wait()
    read_copy(0).start()
    read_copy(1).start()

    n_ffn = 2 * CHUNKS // group
    ffn_items = [Scatter(place, at, scatter_refs, z_first=at >= n_ffn - 2) for at in range(n_ffn)]
    if group == 1:
        items = ffn_items + [
            Scatter(place, n_ffn + at, scatter_refs, [att_grad.at[unit]], z_first=at < 2)
            for at, unit in enumerate((OUT, KEY, VALUE, QUERY))
        ]
        early, late = [(items[n_ffn], [OUT])], [(items[n_ffn + 1 + at], [unit]) for at, unit in enumerate((KEY, VALUE, QUERY))]
    else:
        whole = Scatter(place, n_ffn, scatter_refs, [att_grad.at[unit] for unit in range(4)])
        items = ffn_items + [whole]
        early, late = [], [(whole, [KEY, VALUE, QUERY, OUT])]

    def put(item, unit, grads):
        if unit == 0 and item.index >= OUT_SLOTS:
            items[item.index - OUT_SLOTS].core_copy().wait_send()
        item.put(unit, grads)

    def whole_at(chunk):
        if chunk < 0 or chunk >= CHUNKS or (chunk + 1) % group:
            return []
        at = (chunk + 1) // group - 1
        return ffn_items[2 * at : 2 * at + 2]

    for chunk in range(CHUNKS):
        ffn_gathers[chunk].finish()
        up_grad[...] = jnp.zeros_like(up_grad)
        down_grad[...] = jnp.zeros_like(down_grad)

        def ffn_step(index, carry, chunk=chunk):
            ffn_phase(
                chunk == 0, n2_buf[index], dy_buf[index], weights[UP + 2 * chunk], weights[DOWN + 2 * chunk],
                out_buf.at[index], da_buf.at[index] if chunk == CHUNKS - 1 else None, pool.at[index], up_grad, down_grad,
            )
            if chunk == CHUNKS - 1:
                out_copy(index).start()

            @pl.when(index == 0)
            def _():
                for item in whole_at(chunk - 1):
                    item.to_first()
                for item in whole_at(chunk - 2):
                    item.to_second()

            @pl.when(index == count - 1)
            def _():
                for item in whole_at(chunk - 2):
                    item.to_copies()
                if chunk < 2:
                    ffn_gathers[chunk + 2].to_core()

            return carry

        lax.fori_loop(0, count, ffn_step, 0)
        pair = ffn_items[2 * (chunk // group) : 2 * (chunk // group) + 2]
        put(pair[0], chunk % group, up_grad)
        put(pair[1], chunk % group, down_grad)
        for item in whole_at(chunk):
            item.start()

    grad_sums = Sums(place, local, arrived.at[pl.ds(count, count)], full.at[pl.ds(count, count)], rest[10:12], rest[12:14])
    grad_sums.add_sems = [ref.at[pl.ds(count, count)] for ref in rest[10:12]]
    grad_sums.full_sems = [ref.at[pl.ds(count, count)] for ref in rest[12:14]]

    def attention_step(index, carry):
        slot = lax.rem(index, 2)
        read_copy(index).wait()
        out_copy(index).wait()
        attention_grad_phase(
            dy_buf[index], pool[index], n2_buf[index], scale_buf[index][:, :1], gains[1:2], full.at[index], weights,
            back_ref, state.at[slot], spread, gain_sums.at[1:2], att_grad.at[OUT], da_buf.at[index],
            dq_buf.at[index], local.at[slot],
        )
        grad_sums.start(slot, index)
        read_copy(index + 2).start()

        @pl.when(index > 0)
        def _():
            grad_sums.add(1 - slot, index - 1)

        @pl.when(index == 0)
        def _():
            for item in whole_at(CHUNKS - 1):
                item.to_first()

        @pl.when(index == 1)
        def _():
            for item in whole_at(CHUNKS - 2):
                item.to_second()

        @pl.when(index == count - 1)
        def _():
            for item in whole_at(CHUNKS - 2):
                item.to_copies()
            for item in whole_at(CHUNKS - 1):
                item.to_second()

        return carry

    lax.fori_loop(0, count, attention_step, 0)
    for item, units in early:
        for at, unit in enumerate(units):
            put(item, at, att_grad.at[unit])
        item.start()
    x_copy(0).start()

    dk_buf, dv_buf = n2_buf, dy_buf

    def keys_grad_step(index, carry):
        event = count + index
        slot = lax.rem(event, 2)
        read_copy(event).wait()
        grad_sums.finish(index)
        keys_grad_phase(
            full.at[count + index], back_ref, state.at[slot], spread, dq_buf.at[index], dk_buf.at[index],
            dv_buf.at[index], att_grad,
        )

        @pl.when(index + 2 < count)
        def _():
            read_copy(event + 2).start()

        @pl.when(index == 0)
        def _():
            grad_sums.add((count - 1) % 2, count - 1)
            for item, _ in early:
                item.to_first()

        @pl.when(index == 2)
        def _():
            for item in whole_at(CHUNKS - 1):
                item.to_copies()

        @pl.when(index == count - 1)
        def _():
            for item, _ in early:
                item.to_second()

        return carry

    lax.fori_loop(0, count, keys_grad_step, 0)
    for item, units in late:
        for at, unit in enumerate(units):
            put(item, at, att_grad.at[unit])
        item.start()

    def input_grad_step(index, carry):
        slot = lax.rem(index, 2)

        @pl.when(index + 1 < count)
        def _():
            x_copy(index + 1).start()

        x_copy(index).wait()

        input_grad_phase(
            pool[slot], da_buf.at[index], dq_buf[index], dk_buf[index], dv_buf[index], gains[0:1], weights,
            gain_sums.at[0:1],
        )
        grad_copy(index).start()

        @pl.when(index == 0)
        def _():
            for item, _ in late:
                item.to_first()

        @pl.when(index == 1)
        def _():
            for item, _ in early:
                item.to_copies()


        return carry

    lax.fori_loop(0, count, input_grad_step, 0)

    def mail_plane(step):
        mine = gain_mail.at[place.seq]
        return remote(mine, mine, mail_sems, step - 1, (place.dp, place.up_seq(step)))

    def mail_dp(step):
        mine = gain_mail.at[n_seq + place.dp]
        other = lax.rem(place.dp + step, n_dp)
        return remote(mine, mine, mail_sems, n_seq - 2 + step, (other, place.seq))

    gain_mail[place.seq] = gain_sums[...]
    for step in range(1, n_seq):
        mail_plane(step).start()
    for item, _ in late:
        item.to_second()
    for item, _ in late:
        item.to_copies()
    for step in range(1, n_seq):
        mail_plane(step).wait_recv()
    total = gain_mail[0]
    for at in range(1, n_seq):
        total = total + gain_mail[at]
    gain_mail[n_seq + place.dp] = total
    for step in range(1, n_dp):
        mail_dp(step).start()

    def ffn_results(at):
        return [ffn_items[2 * (chunk // group) + at].result(chunk % group) for chunk in range(CHUNKS)]

    for item in ffn_items:
        item.finish()
    up_rows = ffn_results(0)
    for r in range(n_dp):
        columns = [rows[:, r * own : r * own + own] for rows in up_rows]
        up_ref[:, r * CHUNKS * own : (r + 1) * CHUNKS * own] = jnp.concatenate(columns, axis=1)
    for chunk, rows in enumerate(ffn_results(1)):
        down_ref[chunk * own : chunk * own + own] = rows
    for step in range(1, n_dp):
        mail_dp(step).wait_recv()
    total = gain_mail[n_seq]
    for at in range(1, n_dp):
        total = total + gain_mail[n_seq + at]
    own_gains = jnp.zeros((8, own), F32)
    for r in range(n_dp):
        own_gains = jnp.where(place.dp == r, total[:, r * own : r * own + own], own_gains)
    gain_grads_ref[...] = own_gains
    for item, units in early + late:
        item.finish()
        for at, unit in enumerate(units):
            (dwk, dwv, dwq, dwo)[unit][...] = item.result(at)

    for item in items:
        item.drain(core=item.index + OUT_SLOTS >= len(items))
    for step in range(1, n_seq):
        mail_plane(step).wait_send()
    for step in range(1, n_dp):
        mail_dp(step).wait_send()
        gain_copy(step).wait_send()
    for item in gathers:
        item.drain()
    for index in range(count):
        sums.drain(index)
        grad_sums.drain(index)
        grad_copy(index).wait()


def on_device(sizes, inputs, cotangent, masked, proj_seed, gain_attn, w_query, w_key, w_value, w_out, gain_ffn, w_up, w_down):
    n_dp, n_seq = sizes
    count, length = inputs.shape[0], inputs.shape[1]
    own, own_ff = D // n_dp, FF // n_dp
    group = max(1, n_seq // (D // 128))
    n_gathers = CHUNKS + (2 if group == 1 else 1)
    n_ffn = 2 * CHUNKS // group
    n_items = n_ffn + 4 // group
    part_rows = HEADS * HEAD_DIM // n_seq + 16
    gains = jnp.pad(jnp.stack([gain_attn, gain_ffn], axis=1).astype(LOW), ((0, 0), (0, 126)))
    sd = jax.ShapeDtypeStruct
    vmem = pl.BlockSpec(memory_space=pltpu.VMEM)
    anywhere = pl.BlockSpec(memory_space=pl.ANY)
    outputs, input_grad, gain_grads, dwk, dwv, dwq, dwo, up, down, _ = pl.pallas_call(
        functools.partial(layer_kernel, sizes),
        in_specs=[anywhere, anywhere] + [vmem] * 8 + [pl.BlockSpec(memory_space=pltpu.SMEM)],
        out_specs=[anywhere, anywhere] + [vmem] * 7 + [anywhere],
        out_shape=[
            sd((count, length, D), LOW), sd((count, length, D), LOW), sd((8, own), F32), *[sd((own, D), LOW)] * 4,
            sd((own, FF), LOW), sd((own_ff, D), LOW), sd((2 * count, length, STATE), LOW),
        ],
        scratch_shapes=[
            pltpu.VMEM((UNITS, D, D), LOW), pltpu.VMEM((D, 128), LOW), pltpu.VMEM((8, D), F32),
            pltpu.VMEM((4, D, D), F32), pltpu.VMEM((D, D), F32), pltpu.VMEM((D, D), F32),
            pltpu.VMEM((8, D), F32), pltpu.VMEM((n_seq + n_dp, 8, D), F32),
            pltpu.VMEM((2, n_seq, part_rows, 256), LOW), pltpu.VMEM((2 * count, n_seq - 1, part_rows, 256), LOW),
            pltpu.VMEM((2 * count, n_seq, part_rows, 256), LOW),
            pltpu.VMEM((2, length, STATE), LOW), pltpu.VMEM((HEADS, 256, 256), LOW),
            pltpu.VMEM((count, length, D), LOW), pltpu.VMEM((count, length, D), LOW),
            pltpu.VMEM((count, length, D), LOW), pltpu.VMEM((count, length, D), LOW),
            pltpu.VMEM((count, length, D), F32), pltpu.VMEM((max(count, 4), length, D), F32),
            pltpu.VMEM((count, length, 128), F32),
            pltpu.VMEM((2, 256, 256), LOW), pltpu.VMEM((512, 256), LOW),
            *[pltpu.SemaphoreType.DMA((2,)) for _ in range(4)],
            pltpu.SemaphoreType.DMA((count,)), pltpu.SemaphoreType.DMA((count,)),
            *semaphores(n_gathers, n_dp // 2 - 1), *semaphores(n_gathers, n_dp // 2 - 1, n_seq - 1),
            *semaphores(n_gathers, n_dp // 2),
            *semaphores(n_dp - 1), *semaphores(n_seq + n_dp - 2),
            *semaphores(2 * count, n_seq - 1), *semaphores(2 * count, n_seq - 1),
            *Scatter.shapes(n_dp, n_seq, n_items, n_ffn),
        ],
        compiler_params=pltpu.CompilerParams(
            vmem_limit_bytes=63 * 2**20, collective_id=0, has_side_effects=True
        ),
        name="layer",
    )(inputs, cotangent, masked, gains, w_query, w_key, w_value, w_out, w_up, w_down, proj_seed)
    grains = 2
    block = pl.BlockSpec((None, length // grains, D), lambda i: (i // grains, lax.rem(i, grains), 0))
    small = [(own, D)] * 4 + [(own, FF), (own_ff, D)]

    def fixed(shape):
        return pl.BlockSpec(shape, lambda i: (0, 0))

    def widen(out_ref, grad_ref, gains_ref, *refs):
        wide_out, wide_grad, gain_one, gain_two = refs[len(small) : len(small) + 4]
        wide_out[...] = out_ref[...].astype(F32)
        wide_grad[...] = grad_ref[...].astype(F32)

        @pl.when(pl.program_id(0) == 0)
        def _():
            gain_one[...] = gains_ref[0:1]
            gain_two[...] = gains_ref[1:2]
            for low_ref, wide_ref in zip(refs[: len(small)], refs[len(small) + 4 :]):
                wide_ref[...] = low_ref[...].astype(F32)

    outputs, input_grad, gain_one, gain_two, dwk, dwv, dwq, dwo, up, down = pl.pallas_call(
        widen,
        grid=(count * grains,),
        in_specs=[block, block, fixed((8, own))] + [fixed(shape) for shape in small],
        out_specs=[block, block, fixed((1, own)), fixed((1, own))] + [fixed(shape) for shape in small],
        out_shape=[sd((count, length, D), F32), sd((count, length, D), F32), sd((1, own), F32), sd((1, own), F32)]
        + [sd(shape, F32) for shape in small],
        compiler_params=pltpu.CompilerParams(vmem_limit_bytes=63 * 2**20),
        name="widen",
    )(outputs, input_grad, gain_grads, dwk, dwv, dwq, dwo, up, down)
    return (
        outputs, input_grad, gain_one.reshape(own), dwq, dwk, dwv, dwo, gain_two.reshape(own), up, down,
    )


def solution(mesh):
    in_specs = (
        P("dp", "seq", None),
        P("dp", "seq", None),
        P("dp", "seq"),
        P(),
        P("dp"),
        P("dp", None),
        P("dp", None),
        P("dp", None),
        P("dp", None),
        P("dp"),
        P("dp", None),
        P("dp", None),
    )
    out_specs = (
        P("dp", "seq", None),
        P("dp", "seq", None),
        P("dp"),
        P("dp", None),
        P("dp", None),
        P("dp", None),
        P("dp", None),
        P("dp"),
        P("dp", None),
        P("dp", None),
    )
    sizes = (mesh.shape["dp"], mesh.shape["seq"])
    return jax.shard_map(functools.partial(on_device, sizes), mesh=mesh, in_specs=in_specs, out_specs=out_specs, check_vma=False)
```

```python
import functools
import math

import jax
import jax.numpy as jnp
from jax import lax
from jax.experimental import pallas as pl
from jax.experimental.pallas import tpu as pltpu
from jax.sharding import PartitionSpec as P

D = 512
HEADS = 8
PAIRS = 4
HEAD_DIM = 64
FEATURES = 256
FF = 2048
CHUNKS = 4
KEY, VALUE, QUERY, OUT, UP, DOWN, UNITS = 0, 1, 2, 3, 4, 5, 12

epsilon = 1e-05
LOG2E = math.log2(math.e)
LOW = jnp.bfloat16
F32 = jnp.float32
MESH = pl.DeviceIdType.MESH


def scramble(hashed):
    return jnp.bitwise_xor(hashed, lax.shift_right_logical(hashed, jnp.full_like(hashed, 16)))


def uniform_entries(counter, seed):
    hashed = counter * 1664525 + seed * 22695477 + 1013904223
    hashed = scramble(hashed) * 73244475
    hashed = scramble(hashed) * 73244475
    hashed = scramble(hashed)
    low_bits = jnp.bitwise_and(hashed, 8388607)
    return (low_bits.astype(F32) + 0.5) * (1.0 / 8388608.0)


def direction_entries(index, seed):
    radius = jnp.sqrt(-2.0 * jnp.log(uniform_entries(index, seed)))
    turn = uniform_entries(index + FEATURES * HEAD_DIM, seed)
    return radius * jnp.cos(2.0 * math.pi * turn)


def feature_forms(seed, forms_ref, back_ref):
    col = lax.broadcasted_iota(jnp.int32, (HEAD_DIM, FEATURES), 1)
    row = lax.broadcasted_iota(jnp.int32, (HEAD_DIM, FEATURES), 0)
    dirs_t = direction_entries(col * HEAD_DIM + row, seed) * HEAD_DIM ** (-0.25)
    scaled = dirs_t * LOG2E
    high = scaled.astype(LOW)
    rest = (scaled - high.astype(F32)).astype(LOW)
    minus = jnp.full((HEAD_DIM, FEATURES), -1.0, LOW)
    for half, pieces in enumerate(((high, high, rest, minus), (high, high, minus, rest))):
        for at, piece in enumerate(pieces):
            forms_ref[half, at * HEAD_DIM : at * HEAD_DIM + HEAD_DIM] = piece
    one, zero = jnp.ones((FEATURES, HEAD_DIM), F32), jnp.zeros((FEATURES, HEAD_DIM), F32)
    back = dirs_t.T
    back_ref[:FEATURES] = jnp.concatenate([back, zero, one, zero], axis=1).astype(LOW)
    back_ref[FEATURES:] = jnp.concatenate([zero, back, zero, one], axis=1).astype(LOW)


def dot(left, right):
    return jnp.dot(left, right, preferred_element_type=F32)


def dot_nt(left, right):
    return lax.dot_general(left, right, (((1,), (1,)), ((), ())), preferred_element_type=F32)


def dot_tn(left, right):
    return lax.dot_general(left, right, (((0,), (0,)), ((), ())), preferred_element_type=F32)


def normalize(values):
    centred = values - jnp.mean(values, axis=-1, keepdims=True)
    scale = lax.rsqrt(jnp.mean(centred * centred, axis=-1, keepdims=True) + epsilon)
    return centred * scale, scale


def norm_grad(grad_normed, unit_rows, scale, gain):
    scaled_grad = grad_normed * gain
    first = jnp.mean(scaled_grad, axis=-1, keepdims=True)
    second = jnp.mean(scaled_grad * unit_rows, axis=-1, keepdims=True)
    return scale * (scaled_grad - first - unit_rows * second)


def unit_of(weights, unit):
    return weights[unit].reshape(D, D)


def pair_lanes(pair, base=0):
    return slice(base + pair * 128, base + pair * 128 + 128)


def head_lanes(head):
    return slice(head * 256, head * 256 + 256)


def feature_pair(rows, forms_ref):
    high = rows.astype(LOW)
    rest = (rows - high.astype(F32)).astype(LOW)
    square = (rows * rows * (LOG2E / 16.0) + 1.0 / 16.0).astype(LOW)
    h0, h1 = high[:, :64], high[:, 64:]
    r0, r1 = rest[:, :64], rest[:, 64:]
    s0, s1 = square[:, :64], square[:, 64:]
    left0 = jnp.concatenate([r0, h0, h0, s0], axis=1)
    left1 = jnp.concatenate([h1, r1, s1, h1], axis=1)
    return jnp.exp2(dot(left0, forms_ref[0])), jnp.exp2(dot(left1, forms_ref[1]))


def sums_place(parts, head):
    step = HEADS * HEAD_DIM // parts
    block = min(step, HEAD_DIM)
    runs = [divmod(head * HEAD_DIM + at, step) + (at, block) for at in range(0, HEAD_DIM, block)]
    part = head * HEAD_DIM // step
    return runs, part, step + head - -(-part * step // HEAD_DIM)


def put_sums(sums_ref, head, rows, totals):
    runs, part, row = sums_place(sums_ref.shape[0], head)
    for run_part, run_row, at, block in runs:
        sums_ref[run_part, run_row : run_row + block] = rows[at : at + block].astype(LOW)
    sums_ref[part, row : row + 1] = totals.astype(LOW)


def get_sums(sums_ref, head):
    runs, part, row = sums_place(sums_ref.shape[0], head)
    rows = [sums_ref[run_part, run_row : run_row + block] for run_part, run_row, _, block in runs]
    rows = rows[0] if len(rows) == 1 else jnp.concatenate(rows, axis=0)
    return rows, sums_ref[part, row : row + 1].astype(F32)


def spread_sums(sums_ref, spread_ref):
    for head in range(HEADS):
        own, other = (head % 2) * 64, 64 - (head % 2) * 64
        rows, totals = get_sums(sums_ref, head)
        spread_ref[head, own : own + 64] = rows
        spread_ref[head, 128 + own : 192 + own] = jnp.broadcast_to(totals, (64, 256)).astype(LOW)
        spread_ref[head, other : other + 64] = jnp.zeros((64, 256), LOW)
        spread_ref[head, 128 + other : 192 + other] = jnp.zeros((64, 256), LOW)


def spread_grads(sums_ref, spread_ref):
    for head in range(HEADS):
        own, other = (head % 2) * 64, 64 - (head % 2) * 64
        rows, totals = get_sums(sums_ref, head)
        spread_ref[head, own : own + 64] = rows
        spread_ref[head, other : other + 64] = jnp.zeros((64, 256), LOW)
        row = lax.broadcasted_iota(jnp.int32, (128, 256), 0)
        spread_ref[head, 128:] = jnp.where(row == 0, jnp.broadcast_to(totals, (128, 256)), 0.0).astype(LOW)


def keys_phase(x, gain, weights, forms_ref, state_ref, sums_ref):
    unit, _ = normalize(x)
    normed = (unit * gain).astype(LOW)
    state_ref[:, 3072:3584] = normed
    values = dot(normed, unit_of(weights, VALUE)).astype(LOW)
    state_ref[:, 2560:3072] = values
    keys = dot(normed, unit_of(weights, KEY))
    state_ref[:, 2048:2560] = keys.astype(LOW)
    ones = jnp.ones((16, x.shape[0]), LOW)
    for pair in range(PAIRS):
        phi = feature_pair(keys[:, pair_lanes(pair)], forms_ref)
        values_t = values[:, pair_lanes(pair)].T
        for half in range(2):
            head = 2 * pair + half
            low = phi[half].astype(LOW)
            state_ref[:, head_lanes(head)] = low
            left = jnp.concatenate([values_t[half * 64 : half * 64 + 64], ones], axis=0)
            got = dot(left, low)
            put_sums(sums_ref, head, got[:64], got[64:65])


def front_phase(x, upstream, mask, gain_one, gain_two, sums_arrive, sums_ref, weights, forms_ref, spread_ref, state_ref, out_ref, n2_ref, dy_ref, scale_ref):
    unit, _ = normalize(x)
    queries = dot((unit * gain_one).astype(LOW), unit_of(weights, QUERY))
    state_ref[:, 2048:2560] = queries.astype(LOW)
    for pair in range(PAIRS):
        phi0, phi1 = feature_pair(queries[:, pair_lanes(pair)], forms_ref)
        state_ref[:, head_lanes(2 * pair)] = phi0.astype(LOW)
        state_ref[:, head_lanes(2 * pair + 1)] = phi1.astype(LOW)
    lanes = mask.shape[1]
    for at in range(0, D, lanes):
        dy_ref[:, at : at + lanes] = (upstream[:, at : at + lanes] * mask).astype(LOW)
    sums_arrive()
    spread_sums(sums_ref, spread_ref)
    for pair in range(PAIRS):
        low0, low1 = state_ref[:, head_lanes(2 * pair)], state_ref[:, head_lanes(2 * pair + 1)]
        both = dot_nt(low0, spread_ref[2 * pair]) + dot_nt(low1, spread_ref[2 * pair + 1])
        reciprocal = 1.0 / both[:, 128:]
        state_ref[:, pair_lanes(pair, 2560)] = (both[:, :128] * reciprocal).astype(LOW)
        state_ref[:, pair_lanes(pair, 3072)] = reciprocal.astype(LOW)
    mid = x + dot(state_ref[:, 2560:3072], unit_of(weights, OUT))
    unit, scale = normalize(mid)
    n2_ref[...] = (unit * gain_two).astype(LOW)
    scale_ref[...] = jnp.broadcast_to(scale, scale_ref.shape)
    out_ref[...] = mid


def ffn_phase(first, n2, dy, w_up, w_down, out_ref, low_out_ref, dn2_ref, up_grad_ref, down_grad_ref):
    hidden = dot(n2, w_up)
    cumulative = 0.5 * (1.0 + lax.erf(hidden * (1.0 / math.sqrt(2.0))))
    density = jnp.exp2(hidden * hidden * (-0.5 * LOG2E)) * (1.0 / math.sqrt(2.0 * math.pi))
    act = (hidden * cumulative).astype(LOW)
    du = (dot_nt(dy, w_down) * (cumulative + hidden * density)).astype(LOW)
    if low_out_ref is None:
        out_ref[...] += dot(act, w_down)
    else:
        low_out_ref[...] = (out_ref[...] + dot(act, w_down)).astype(LOW)
    down_grad_ref[...] += dot_tn(act, dy)
    dn2 = dot_nt(du, w_up)
    if first:
        dn2_ref[...] = dn2
    else:
        dn2_ref[...] += dn2
    up_grad_ref[...] += dot_tn(n2, du)


def attention_grad_phase(dy, dn2, n2, scale, gain, sums_ref, weights, back_ref, state_ref, spread_ref, gain_grad_ref, w_out_grad_ref, da_ref, dq_ref, grad_sums_ref):
    spread_sums(sums_ref, spread_ref)
    unit = n2.astype(F32) * (1.0 / gain)
    gain_grad_ref[...] += jnp.sum(dn2 * unit, axis=0, keepdims=True)
    da = (dy.astype(F32) + norm_grad(dn2, unit, scale, gain)).astype(LOW)
    da_ref[...] = da
    w_out_grad_ref[...] += dot_tn(state_ref[:, 2560:3072], da)
    datt = dot_nt(da, unit_of(weights, OUT))
    for pair in range(PAIRS):
        dnumer = datt[:, pair_lanes(pair)] * state_ref[:, pair_lanes(pair, 3072)].astype(F32)
        weighted = -dnumer * state_ref[:, pair_lanes(pair, 2560)].astype(F32)
        left = jnp.concatenate([dnumer.astype(LOW), weighted.astype(LOW)], axis=1)
        left_t = left.T
        parts = []
        for half in range(2):
            head, own = 2 * pair + half, half * 64
            pq = state_ref[:, head_lanes(head)]
            dden = jnp.sum(left_t[128 + own : 192 + own].astype(F32), axis=0, keepdims=True)
            rows = jnp.concatenate(
                [left_t[own : own + 64], jnp.broadcast_to(dden, (16, dden.shape[1])).astype(LOW)], axis=0
            )
            got = dot(rows, pq)
            put_sums(grad_sums_ref, head, got[:64], got[64:65])
            parts.append((dot(left, spread_ref[head]) * pq.astype(F32)).astype(LOW))
        grads = dot(parts[0], back_ref[:256]) + dot(parts[1], back_ref[256:])
        q = state_ref[:, pair_lanes(pair, 2048)].astype(F32)
        dq_ref[:, pair_lanes(pair)] = (grads[:, :128] - grads[:, 128:] * q * 0.125).astype(LOW)


def keys_grad_phase(sums_ref, back_ref, state_ref, spread_ref, dq_ref, dk_ref, dv_ref, att_grad_ref):
    spread_grads(sums_ref, spread_ref)
    ones = jnp.ones((dk_ref.shape[0], 128), LOW)
    for pair in range(PAIRS):
        left = jnp.concatenate([state_ref[:, pair_lanes(pair, 2560)], ones], axis=1)
        parts = []
        dv = None
        for half in range(2):
            head = 2 * pair + half
            pk = state_ref[:, head_lanes(head)]
            parts.append((dot(left, spread_ref[head]) * pk.astype(F32)).astype(LOW))
            piece = dot_nt(pk, spread_ref[head, :128])
            dv = piece if dv is None else dv + piece
        dv_ref[:, pair_lanes(pair)] = dv.astype(LOW)
        grads = dot(parts[0], back_ref[:256]) + dot(parts[1], back_ref[256:])
        k = state_ref[:, pair_lanes(pair, 2048)].astype(F32)
        dk_ref[:, pair_lanes(pair)] = (grads[:, :128] - grads[:, 128:] * k * 0.125).astype(LOW)
    normed = state_ref[:, 3072:3584]
    att_grad_ref[KEY] += dot_tn(normed, dk_ref[...])
    att_grad_ref[VALUE] += dot_tn(normed, dv_ref[...])
    att_grad_ref[QUERY] += dot_tn(normed, dq_ref[...])


def input_grad_phase(x, da_ref, dq, dk, dv, gain, weights, gain_grad_ref):
    dn1 = dot_nt(dq, unit_of(weights, QUERY)) + dot_nt(dk, unit_of(weights, KEY)) + dot_nt(dv, unit_of(weights, VALUE))
    unit, scale = normalize(x)
    gain_grad_ref[...] += jnp.sum(dn1 * unit, axis=0, keepdims=True)
    da_ref[...] = (da_ref[...].astype(F32) + norm_grad(dn1, unit, scale, gain)).astype(LOW)


class Place:
    def __init__(self, n_dp, n_seq):
        self.n_dp, self.n_seq, self.n_z = n_dp, n_seq, n_dp // 2
        self.dp, self.seq = lax.axis_index("dp"), lax.axis_index("seq")
        self.z, self.core = self.dp // 2, lax.rem(self.dp, 2)

    def up_z(self, step):
        return lax.rem(self.z + step, self.n_z)

    def up_seq(self, step):
        return lax.rem(self.seq + step, self.n_seq)

    def down_z(self, step):
        return lax.rem(self.z + (self.n_z - step), self.n_z)

    def owner(self, z):
        return z * 2 + self.core

    def other_core(self):
        return (self.z * 2 + 1 - self.core, self.seq)

    def arrive(self):
        barrier = pltpu.get_barrier_semaphore()
        for step in range(1, self.n_dp):
            other = lax.rem(self.dp + step, self.n_dp)
            pl.semaphore_signal(barrier, inc=1, device_id=(other, self.seq), device_id_type=MESH)
        for step in range(1, self.n_seq):
            pl.semaphore_signal(barrier, inc=1, device_id=(self.dp, self.up_seq(step)), device_id_type=MESH)

    def meet(self):
        pl.semaphore_wait(pltpu.get_barrier_semaphore(), self.n_dp - 1 + self.n_seq - 1)


def remote(source, target, sems, at, device):
    return pltpu.make_async_remote_copy(
        src_ref=source, dst_ref=target, send_sem=sems[0].at[at], recv_sem=sems[1].at[at],
        device_id=device, device_id_type=MESH,
    )


def semaphores(*shape):
    return [pltpu.SemaphoreType.DMA(shape), pltpu.SemaphoreType.DMA(shape)]


class Gather:
    def __init__(self, place, weights, first, count, index, sems, line=False):
        self.place, self.weights, self.first, self.count, self.index = place, weights, first, count, index
        self.line = line
        self.own = D // place.n_dp
        self.across = min(place.n_seq, D // 128)
        self.units = count // (place.n_seq // self.across)
        self.z_sems, self.plane_sems, self.core_sems = sems

    def piece(self, z, part):
        columns = D // self.across
        first = self.first + (part // self.across) * self.units
        left = pl.multiple_of(lax.rem(part, self.across) * columns, 128)
        return self.weights.at[pl.ds(first, self.units), z, self.place.core, :, pl.ds(left, columns)]

    def shard(self, z):
        return self.weights.at[pl.ds(self.first, self.count), z, self.place.core]

    def z_copy(self, step):
        place = self.place
        piece = self.shard(place.z) if self.line else self.piece(place.z, place.seq)
        return remote(piece, piece, self.z_sems, (self.index, step - 1), (place.owner(place.up_z(step)), place.seq))

    def plane_copy(self, step, to):
        place = self.place
        piece = self.piece(place.down_z(step), place.seq)
        return remote(piece, piece, self.plane_sems, (self.index, step - 1, to - 1), (place.dp, place.up_seq(to)))

    def core_copy(self):
        shards = self.weights.at[pl.ds(self.first, self.count), :, self.place.core]
        return remote(shards, shards, self.core_sems, self.index, self.place.other_core())

    def start(self):
        for step in range(1, self.place.n_z):
            self.z_copy(step).start()

    def to_plane(self):
        for step in range(1, self.place.n_z):
            self.z_copy(step).wait_recv()
            for to in range(1, self.place.n_seq):
                self.plane_copy(step, to).start()

    def to_core(self):
        for step in range(1, self.place.n_z):
            if self.line:
                self.z_copy(step).wait_recv()
            else:
                for to in range(1, self.place.n_seq):
                    self.plane_copy(step, to).wait_recv()
        self.core_copy().start()

    def finish(self):
        self.core_copy().wait_recv()

    def drain(self):
        for step in range(1, self.place.n_z):
            self.z_copy(step).wait_send()
            if not self.line:
                for to in range(1, self.place.n_seq):
                    self.plane_copy(step, to).wait_send()
        self.core_copy().wait_send()


class Sums:
    def __init__(self, place, local, arrived, full, add_sems, full_sems):
        self.place, self.local, self.arrived, self.full = place, local, arrived, full
        self.add_sems, self.full_sems = add_sems, full_sems

    def add_copy(self, slot, index, to):
        other = self.place.up_seq(to)
        return remote(
            self.local.at[slot, other], self.arrived.at[index, to - 1], self.add_sems, (index, to - 1),
            (self.place.dp, other),
        )

    def full_copy(self, index, to):
        place = self.place
        mine = self.full.at[index, place.seq]
        return remote(mine, mine, self.full_sems, (index, to - 1), (place.dp, place.up_seq(to)))

    def start(self, slot, index):
        for to in range(1, self.place.n_seq):
            self.add_copy(slot, index, to).start()

    def add(self, slot, index):
        place = self.place
        total = self.local[slot, place.seq].astype(F32)
        for to in range(1, place.n_seq):
            self.add_copy(slot, index, to).wait_recv()
            total = total + self.arrived[index, to - 1].astype(F32)
        self.full[index, place.seq] = total.astype(LOW)
        for to in range(1, place.n_seq):
            self.full_copy(index, to).start()
        for to in range(1, place.n_seq):
            self.add_copy(slot, index, to).wait_send()

    def finish(self, index):
        for to in range(1, self.place.n_seq):
            self.full_copy(index, to).wait_recv()

    def drain(self, index):
        for to in range(1, self.place.n_seq):
            self.full_copy(index, to).wait_send()


class Scatter:
    REFS = 14

    def __init__(self, place, refs, z_first, kept=None):
        self.place, self.z_first, self.kept = place, z_first, kept
        self.out, self.mine, self.arrived, self.first, self.second, self.final = refs[:6]
        self.core_sems, self.plane_sems, self.z_sems, self.full_sems = refs[6:8], refs[8:10], refs[10:12], refs[12:14]
        self.own = D // place.n_dp
        self.across = min(place.n_seq, D // 128)
        self.lanes = D // self.across
        self.units = self.out.shape[2]
        self.n_first, self.n_second = (place.n_z, place.n_seq) if z_first else (place.n_seq, place.n_z)

    @staticmethod
    def shapes(n_dp, n_seq, units, z_first, keep):
        own, n_z = D // n_dp, n_dp // 2
        part = (units, own, D // min(n_seq, D // 128))
        n_first, n_second = (n_z, n_seq) if z_first else (n_seq, n_z)
        return [
            pltpu.VMEM((n_seq, n_z) + part, LOW), pltpu.VMEM((n_seq, n_z) + part if keep else (16, 128), LOW),
            pltpu.VMEM((n_seq, n_z) + part, LOW), pltpu.VMEM(((n_first - 1) * n_second,) + part, LOW),
            pltpu.VMEM((2 * n_second - 1,) + part, LOW), pltpu.VMEM((n_seq,) + part, LOW),
            *semaphores(1), *semaphores(n_seq - 1), *semaphores(n_z - 1), *semaphores(n_seq - 1),
        ]

    def block(self, grads, owner, lane_part):
        rows = pl.ds(pl.multiple_of(owner * self.own, self.own), self.own)
        return grads[rows, lane_part * self.lanes : lane_part * self.lanes + self.lanes]

    def core_copy(self):
        return remote(self.out, self.arrived, self.core_sems, 0, self.place.other_core())

    def axis_copy(self, along_z, step, source, target):
        place = self.place
        if along_z:
            return remote(source, target, self.z_sems, step - 1, (place.owner(place.up_z(step)), place.seq))
        return remote(source, target, self.plane_sems, step - 1, (place.dp, place.up_seq(step)))

    def first_copy(self, step):
        place = self.place
        source = self.arrived.at[:, place.up_z(step)] if self.z_first else self.arrived.at[place.up_seq(step)]
        target = self.first.at[pl.ds((step - 1) * self.n_second, self.n_second)]
        return self.axis_copy(self.z_first, step, source, target)

    def second_copy(self, step):
        place = self.place
        other = place.up_seq(step) if self.z_first else place.up_z(step)
        return self.axis_copy(not self.z_first, step, self.second.at[other], self.second.at[self.n_second + step - 1])

    def full_copy(self, to):
        place = self.place
        mine = self.final.at[place.seq]
        return remote(mine, mine, self.full_sems, to - 1, (place.dp, place.up_seq(to)))

    def put(self, unit, group, grads):
        place = self.place
        for lane_part in range(self.across):
            part = group * self.across + lane_part
            for z in range(place.n_z):
                self.out[part, z, unit] = self.block(grads, z * 2 + 1 - place.core, lane_part).astype(LOW)
                if self.kept is None:
                    self.mine[part, z, unit] = self.block(grads, place.owner(z), lane_part).astype(LOW)

    def start(self):
        self.core_copy().start()

    def to_first(self):
        place = self.place
        self.core_copy().wait_recv()
        for part in range(place.n_seq):
            for z in range(place.n_z):
                for unit in range(self.units):
                    if self.kept is None:
                        mine = self.mine[part, z, unit].astype(F32)
                    else:
                        grads = self.kept[part // self.across * self.units + unit]
                        mine = self.block(grads, place.owner(z), part % self.across)
                    self.arrived[part, z, unit] = (mine + self.arrived[part, z, unit].astype(F32)).astype(LOW)
        for step in range(1, self.n_first):
            self.first_copy(step).start()

    def to_second(self):
        place = self.place
        for step in range(1, self.n_first):
            self.first_copy(step).wait_recv()
        for at in range(self.n_second):
            total = self.arrived[at, place.z] if self.z_first else self.arrived[place.seq, at]
            total = total.astype(F32)
            for step in range(1, self.n_first):
                total = total + self.first[(step - 1) * self.n_second + at].astype(F32)
            self.second[at] = total.astype(LOW)
        for step in range(1, self.n_second):
            self.second_copy(step).start()

    def to_copies(self):
        place = self.place
        total = self.second[place.seq if self.z_first else place.z].astype(F32)
        for step in range(1, self.n_second):
            self.second_copy(step).wait_recv()
            total = total + self.second[self.n_second + step - 1].astype(F32)
        self.final[place.seq] = total.astype(LOW)
        for to in range(1, place.n_seq):
            self.full_copy(to).start()

    def finish(self):
        for to in range(1, self.place.n_seq):
            self.full_copy(to).wait_recv()

    def result(self, unit, group=0):
        parts = [self.final[group * self.across + at, unit] for at in range(self.across)]
        return jnp.concatenate(parts, axis=1)

    def drain(self):
        self.core_copy().wait_send()
        for step in range(1, self.n_first):
            self.first_copy(step).wait_send()
        for step in range(1, self.n_second):
            self.second_copy(step).wait_send()
        for to in range(1, self.place.n_seq):
            self.full_copy(to).wait_send()


UP_HALF, DOWN_HALF = 0, 1


def scatter_plan(group):
    def chunk(at):
        return [(UP_HALF, at), (DOWN_HALF, at)]

    if group == 1:
        return [
            (chunk(0) + chunk(1), False),
            (chunk(2), True),
            ([(UP_HALF, 3), ("att", OUT)], False),
            ([(DOWN_HALF, 3)], True),
            ([("att", KEY)], True),
            ([("att", VALUE), ("att", QUERY)], False),
        ]
    return [([(UP_HALF, None), (DOWN_HALF, None)], False), ([("att", None)], False)]


STATE = 2048 + 3 * D


def layer_kernel(
    sizes, x_hbm, cot_hbm, mask_ref, gains_own, wq, wk, wv, wo, wu, wd, seed_ref,
    out_hbm, grad_hbm, gain_grads_ref, dwk, dwv, dwq, dwo, up_ref, down_ref, state_hbm,
    weights, gain_buf, gains, att_grad, up_grad, down_grad, gain_sums, gain_mail,
    local, arrived, full, state, spread, n2_buf, dy_buf, da_buf, dq_buf, out_buf, out_low, pool, scale_buf,
    forms_ref, back_ref, x_sems, cot_sems, write_sems, read_sems, out_sems, grad_sems, *rest,
):
    n_dp, n_seq = sizes
    count = x_hbm.shape[0]
    own = D // n_dp
    place = Place(n_dp, n_seq)
    group = max(1, n_seq // (D // 128))
    gather_sems = (rest[0:2], rest[2:4], rest[4:6])
    gain_sems, mail_sems = rest[6:8], rest[8:10]
    sums_refs = (place, local, arrived, full, rest[10:12], rest[12:14])
    scatter_refs = rest[14:]

    my_rows = pl.ds(pl.multiple_of(place.dp * own, own), own)

    def x_copy(step):
        slot = lax.rem(step, 2)
        return pltpu.make_async_copy(x_hbm.at[lax.rem(step, count)], att_grad.at[QUERY + slot], x_sems.at[slot])

    def x_again(index):
        slot = lax.rem(index, 2)
        return pltpu.make_async_copy(x_hbm.at[index], pool.at[slot], x_sems.at[slot])

    def cot_copy(index):
        return pltpu.make_async_copy(cot_hbm.at[index], out_buf.at[index], cot_sems.at[index])

    def write_copy(step):
        slot = lax.rem(step, 2)
        return pltpu.make_async_copy(state.at[slot], state_hbm.at[step], write_sems.at[slot])

    def read_copy(event):
        slot = lax.rem(event, 2)
        return pltpu.make_async_copy(
            state_hbm.at[lax.rem(count + event, 2 * count)], state.at[slot], read_sems.at[slot]
        )

    def out_copy(index):
        return pltpu.make_async_copy(out_low, out_hbm.at[index], out_sems.at[index])

    def grad_copy(index):
        return pltpu.make_async_copy(da_buf.at[index], grad_hbm.at[index], grad_sems.at[index])

    place.arrive()
    x_copy(0).start()
    for index in range(count):
        cot_copy(index).start()
    for unit, ref in ((KEY, wk), (VALUE, wv), (QUERY, wq), (OUT, wo)):
        weights[unit, place.z, place.core] = ref[...].astype(LOW)
    for chunk in range(CHUNKS):
        columns = [wu[:, (r * CHUNKS + chunk) * own : (r * CHUNKS + chunk + 1) * own] for r in range(n_dp)]
        weights[UP + 2 * chunk, place.z, place.core] = jnp.concatenate(columns, axis=1).astype(LOW)
        weights[DOWN + 2 * chunk, place.z, place.core] = wd[chunk * own : chunk * own + own].astype(LOW)
    gain_buf[my_rows] = gains_own[...]
    place.meet()

    runs = [(KEY, 2), (QUERY, 2)] if group == 1 else [(KEY, 4)]
    gathers = [Gather(place, weights, first, units, at, gather_sems, line=False) for at, (first, units) in enumerate(runs)]
    keys_gathers, att_gathers = gathers[:1], gathers[1:]
    ffn_gathers = [
        Gather(place, weights, UP + 2 * chunk, 2, len(runs) + chunk, gather_sems, line=True) for chunk in range(CHUNKS)
    ]
    gathers = gathers + ffn_gathers

    def gain_copy(step):
        mine = gain_buf.at[my_rows]
        other = lax.rem(place.dp + step, n_dp)
        return remote(mine, mine, gain_sems, step - 1, (other, place.seq))

    for step in range(1, n_dp):
        gain_copy(step).start()
    for item in keys_gathers:
        item.start()
    feature_forms(seed_ref[0], forms_ref, back_ref)
    gathers[0].to_plane()
    gain_sums[...] = jnp.zeros_like(gain_sums)
    for item in keys_gathers[1:]:
        item.to_core()
    for item in att_gathers + ffn_gathers[:1]:
        item.start()
    gathers[0].to_core()
    for step in range(1, n_dp):
        gain_copy(step).wait_recv()
    gains[...] = gain_buf[...].astype(F32).T[:8]
    for item in keys_gathers:
        item.finish()
    for item in att_gathers:
        item.to_plane()

    sums = Sums(*sums_refs)

    def keys_step(index, carry):
        slot = lax.rem(index, 2)
        x_copy(index + 1).start()

        @pl.when(index >= 2)
        def _():
            write_copy(index - 2).wait()

        x_copy(index).wait()
        keys_phase(att_grad[QUERY + slot], gains[0:1], weights, forms_ref, state.at[slot], local.at[slot])
        sums.start(slot, index)
        write_copy(index).start()

        @pl.when(index > 0)
        def _():
            sums.add(1 - slot, index - 1)

        @pl.when(index == 0)
        def _():
            ffn_gathers[1].start()

        @pl.when(index == 2)
        def _():
            for item in att_gathers:
                item.to_core()

        @pl.when(index == count - 1)
        def _():
            ffn_gathers[0].to_core()
            ffn_gathers[2].start()

        return carry

    lax.fori_loop(0, count, keys_step, 0)
    for item in att_gathers:
        item.finish()

    plan = scatter_plan(group)
    items, of_unit = [], {}
    for at, (units, z_first) in enumerate(plan):
        kept = None
        if all(kind == "att" for kind, _ in units):
            kept = [att_grad.at[index] for _, index in units] if group == 1 else [att_grad.at[index] for index in range(4)]
        item = Scatter(place, scatter_refs[at * Scatter.REFS : (at + 1) * Scatter.REFS], z_first, kept)
        items.append(item)
        for position, unit in enumerate(units):
            of_unit[unit] = (item, position)

    def put(kind, index, grads):
        if group == 1:
            item, position = of_unit[kind, index]
            item.put(position, 0, grads)
        else:
            item, position = of_unit[kind, None]
            item.put(position, index, grads)

    def result(kind, index):
        if group == 1:
            item, position = of_unit[kind, index]
            return item.result(position)
        item, position = of_unit[kind, None]
        return item.result(position, index)

    def chunk_grads(chunk):
        return (att_grad.at[KEY], att_grad.at[VALUE]) if chunk == 1 else (up_grad, down_grad)

    def open_chunk(chunk):
        for ref in chunk_grads(chunk):
            ref[...] = jnp.zeros(ref.shape, F32)

    def ffn_step(chunk, index):
        ffn_phase(
            chunk == 0, n2_buf[index], dy_buf[index], unit_of(weights, UP + 2 * chunk), unit_of(weights, DOWN + 2 * chunk),
            out_buf.at[index], out_low if chunk == CHUNKS - 1 else None, pool.at[index], *chunk_grads(chunk),
        )

    def close_chunk(chunk):
        for kind, grads in zip((UP_HALF, DOWN_HALF), chunk_grads(chunk)):
            put(kind, chunk, grads)

    def front_step(index, carry):
        step = count + index
        slot = lax.rem(step, 2)

        @pl.when(index + 1 < count)
        def _():
            x_copy(step + 1).start()

        write_copy(step - 2).wait()
        x_copy(step).wait()
        cot_copy(index).wait()

        def sums_arrive():
            @pl.when(index == 0)
            def _():
                sums.add((count - 1) % 2, count - 1)

            sums.finish(index)

        mask = jnp.broadcast_to(mask_ref[pl.ds(index, 1)].astype(F32), (128, mask_ref.shape[1])).T
        front_phase(
            att_grad[QUERY + slot], out_buf[index], mask, gains[0:1], gains[1:2], sums_arrive, full.at[index], weights,
            forms_ref, spread, state.at[slot], out_buf.at[index], n2_buf.at[index], dy_buf.at[index],
            scale_buf.at[index],
        )
        write_copy(step).start()

        @pl.when(index == 0)
        def _():
            ffn_gathers[0].finish()

        ffn_step(0, index)

        @pl.when(index == 1)
        def _():
            ffn_gathers[1].to_core()
            ffn_gathers[3].start()

        return carry

    open_chunk(0)
    open_chunk(1)
    lax.fori_loop(0, count, front_step, 0)
    for step in (2 * count - 2, 2 * count - 1):
        write_copy(step).wait()
    read_copy(0).start()
    read_copy(1).start()
    ffn_gathers[1].finish()

    def second_step(index, carry):
        ffn_step(1, index)

        @pl.when(index == 1)
        def _():
            ffn_gathers[2].to_core()

        return carry

    lax.fori_loop(0, count, second_step, 0)
    close_chunk(0)
    close_chunk(1)
    first_items, third_items, last_items, late_items = (
        (items[0:1], items[1:2], items[2:4], items[4:6]) if group == 1 else ([], [], items[:1], items[1:])
    )
    for item in first_items:
        item.start()
    att_grad[...] = jnp.zeros_like(att_grad)
    ffn_gathers[2].finish()
    open_chunk(2)

    def third_step(index, carry):
        ffn_step(2, index)

        @pl.when(index == 1)
        def _():
            for item in first_items:
                item.to_first()

        @pl.when(index == 2)
        def _():
            ffn_gathers[3].to_core()

        return carry

    lax.fori_loop(0, count, third_step, 0)
    close_chunk(2)
    for item in third_items:
        item.start()
    ffn_gathers[3].finish()
    open_chunk(3)

    grad_sums = Sums(place, local, arrived.at[pl.ds(count, count)], full.at[pl.ds(count, count)], rest[10:12], rest[12:14])
    grad_sums.add_sems = [ref.at[pl.ds(count, count)] for ref in rest[10:12]]
    grad_sums.full_sems = [ref.at[pl.ds(count, count)] for ref in rest[12:14]]

    def attention_step(index, carry):
        slot = lax.rem(index, 2)

        @pl.when(index > 0)
        def _():
            out_copy(index - 1).wait()

        ffn_step(CHUNKS - 1, index)
        out_copy(index).start()
        read_copy(index).wait()
        attention_grad_phase(
            dy_buf[index], pool[index], n2_buf[index], scale_buf[index][:, :1], gains[1:2], full.at[index], weights,
            back_ref, state.at[slot], spread, gain_sums.at[1:2], att_grad.at[OUT], da_buf.at[index],
            dq_buf.at[index], local.at[slot],
        )
        grad_sums.start(slot, index)
        read_copy(index + 2).start()

        @pl.when(index > 0)
        def _():
            grad_sums.add(1 - slot, index - 1)

        @pl.when(index == 0)
        def _():
            for item in third_items:
                item.to_first()

        @pl.when(index == 2)
        def _():
            for item in first_items:
                item.to_second()

        @pl.when(index == count - 1)
        def _():
            for item in third_items:
                item.to_second()

        return carry

    lax.fori_loop(0, count, attention_step, 0)
    close_chunk(CHUNKS - 1)
    if group == 1:
        put("att", OUT, att_grad.at[OUT])
    for item in last_items:
        item.start()
    x_again(0).start()

    dk_buf, dv_buf = n2_buf, dy_buf

    def keys_grad_step(index, carry):
        event = count + index
        slot = lax.rem(event, 2)
        read_copy(event).wait()
        grad_sums.finish(index)
        keys_grad_phase(
            full.at[count + index], back_ref, state.at[slot], spread, dq_buf.at[index], dk_buf.at[index],
            dv_buf.at[index], att_grad,
        )

        @pl.when(index + 2 < count)
        def _():
            read_copy(event + 2).start()

        @pl.when(index == 0)
        def _():
            grad_sums.add((count - 1) % 2, count - 1)
            for item in first_items:
                item.to_copies()

        @pl.when(index == 1)
        def _():
            for item in last_items:
                item.to_first()

        @pl.when(index == 2)
        def _():
            for item in third_items:
                item.to_copies()

        return carry

    lax.fori_loop(0, count, keys_grad_step, 0)
    for unit in (KEY, VALUE, QUERY) + (() if group == 1 else (OUT,)):
        put("att", unit, att_grad.at[unit])
    for item in late_items:
        item.start()

    def input_grad_step(index, carry):
        slot = lax.rem(index, 2)

        @pl.when(index + 1 < count)
        def _():
            x_again(index + 1).start()

        x_again(index).wait()
        input_grad_phase(
            pool[slot], da_buf.at[index], dq_buf[index], dk_buf[index], dv_buf[index], gains[0:1], weights,
            gain_sums.at[0:1],
        )
        grad_copy(index).start()

        @pl.when(index == 0)
        def _():
            for item in late_items:
                item.to_first()

        @pl.when(index == 2)
        def _():
            for item in last_items:
                item.to_second()


        return carry

    lax.fori_loop(0, count, input_grad_step, 0)

    def mail_plane(step):
        mine = gain_mail.at[place.seq]
        return remote(mine, mine, mail_sems, step - 1, (place.dp, place.up_seq(step)))

    def mail_dp(step):
        mine = gain_mail.at[n_seq + place.dp]
        other = lax.rem(place.dp + step, n_dp)
        return remote(mine, mine, mail_sems, n_seq - 2 + step, (other, place.seq))

    gain_mail[place.seq] = gain_sums[...]
    for step in range(1, n_seq):
        mail_plane(step).start()
    for item in late_items:
        item.to_second()
    for item in last_items:
        item.to_copies()
    for step in range(1, n_seq):
        mail_plane(step).wait_recv()
    total = gain_mail[0]
    for at in range(1, n_seq):
        total = total + gain_mail[at]
    gain_mail[n_seq + place.dp] = total
    for step in range(1, n_dp):
        mail_dp(step).start()
    for item in late_items:
        item.to_copies()

    for item in first_items + third_items + last_items:
        item.finish()
    up_rows = [result(UP_HALF, chunk) for chunk in range(CHUNKS)]
    for r in range(n_dp):
        columns = [rows[:, r * own : r * own + own] for rows in up_rows]
        up_ref[:, r * CHUNKS * own : (r + 1) * CHUNKS * own] = jnp.concatenate(columns, axis=1)
    for chunk in range(CHUNKS):
        down_ref[chunk * own : chunk * own + own] = result(DOWN_HALF, chunk)
    if group == 1:
        dwo[...] = result("att", OUT)
    for step in range(1, n_dp):
        mail_dp(step).wait_recv()
    total = gain_mail[n_seq]
    for at in range(1, n_dp):
        total = total + gain_mail[n_seq + at]
    own_gains = jnp.zeros((8, own), F32)
    for r in range(n_dp):
        own_gains = jnp.where(place.dp == r, total[:, r * own : r * own + own], own_gains)
    gain_grads_ref[...] = own_gains
    for item in late_items:
        item.finish()
    for unit, ref in ((KEY, dwk), (VALUE, dwv), (QUERY, dwq)) + (() if group == 1 else ((OUT, dwo),)):
        ref[...] = result("att", unit)

    for item in items:
        item.drain()
    for step in range(1, n_seq):
        mail_plane(step).wait_send()
    for step in range(1, n_dp):
        mail_dp(step).wait_send()
        gain_copy(step).wait_send()
    for item in gathers:
        item.drain()
    for index in range(count):
        sums.drain(index)
        grad_sums.drain(index)
        grad_copy(index).wait()
    out_copy(count - 1).wait()


def on_device(sizes, inputs, cotangent, masked, proj_seed, gain_attn, w_query, w_key, w_value, w_out, gain_ffn, w_up, w_down):
    n_dp, n_seq = sizes
    count, length = inputs.shape[0], inputs.shape[1]
    own, own_ff = D // n_dp, FF // n_dp
    group = max(1, n_seq // (D // 128))
    n_gathers = CHUNKS + (2 if group == 1 else 1)
    scatter_scratch = []
    for units, z_first in scatter_plan(group):
        keep = not all(kind == "att" for kind, _ in units)
        scatter_scratch += Scatter.shapes(n_dp, n_seq, len(units), z_first, keep)
    part_rows = HEADS * HEAD_DIM // n_seq + 16
    gains = jnp.pad(jnp.stack([gain_attn, gain_ffn], axis=1).astype(LOW), ((0, 0), (0, 126)))
    sd = jax.ShapeDtypeStruct
    vmem = pl.BlockSpec(memory_space=pltpu.VMEM)
    anywhere = pl.BlockSpec(memory_space=pl.ANY)
    outputs, input_grad, gain_grads, dwk, dwv, dwq, dwo, up, down, _ = pl.pallas_call(
        functools.partial(layer_kernel, sizes),
        in_specs=[anywhere, anywhere] + [vmem] * 8 + [pl.BlockSpec(memory_space=pltpu.SMEM)],
        out_specs=[anywhere, anywhere] + [vmem] * 7 + [anywhere],
        out_shape=[
            sd((count, length, D), LOW), sd((count, length, D), LOW), sd((8, own), F32), *[sd((own, D), LOW)] * 4,
            sd((own, FF), LOW), sd((own_ff, D), LOW), sd((2 * count, length, STATE), LOW),
        ],
        scratch_shapes=[
            pltpu.VMEM((UNITS, n_dp // 2, 2, own, D), LOW), pltpu.VMEM((D, 128), LOW), pltpu.VMEM((8, D), F32),
            pltpu.VMEM((4, D, D), F32), pltpu.VMEM((D, D), F32), pltpu.VMEM((D, D), F32),
            pltpu.VMEM((8, D), F32), pltpu.VMEM((n_seq + n_dp, 8, D), F32),
            pltpu.VMEM((2, n_seq, part_rows, 256), LOW), pltpu.VMEM((2 * count, n_seq - 1, part_rows, 256), LOW),
            pltpu.VMEM((2 * count, n_seq, part_rows, 256), LOW),
            pltpu.VMEM((2, length, STATE), LOW), pltpu.VMEM((HEADS, 256, 256), LOW),
            pltpu.VMEM((count, length, D), LOW), pltpu.VMEM((count, length, D), LOW),
            pltpu.VMEM((count, length, D), LOW), pltpu.VMEM((count, length, D), LOW),
            pltpu.VMEM((count, length, D), F32), pltpu.VMEM((length, D), LOW), pltpu.VMEM((count, length, D), F32),
            pltpu.VMEM((count, length, 128), F32),
            pltpu.VMEM((2, 256, 256), LOW), pltpu.VMEM((512, 256), LOW),
            pltpu.SemaphoreType.DMA((2,)), pltpu.SemaphoreType.DMA((count,)),
            pltpu.SemaphoreType.DMA((2,)), pltpu.SemaphoreType.DMA((2,)),
            pltpu.SemaphoreType.DMA((count,)), pltpu.SemaphoreType.DMA((count,)),
            *semaphores(n_gathers, n_dp // 2 - 1), *semaphores(n_gathers, n_dp // 2 - 1, n_seq - 1),
            *semaphores(n_gathers),
            *semaphores(n_dp - 1), *semaphores(n_seq + n_dp - 2),
            *semaphores(2 * count, n_seq - 1), *semaphores(2 * count, n_seq - 1),
            *scatter_scratch,
        ],
        compiler_params=pltpu.CompilerParams(
            vmem_limit_bytes=63 * 2**20, collective_id=0, has_side_effects=True
        ),
        name="layer",
    )(inputs, cotangent, masked, gains, w_query, w_key, w_value, w_out, w_up, w_down, proj_seed)
    grains = 2
    block = pl.BlockSpec((None, length // grains, D), lambda i: (i // grains, lax.rem(i, grains), 0))
    small = [(own, D)] * 4 + [(own, FF), (own_ff, D)]

    def fixed(shape):
        return pl.BlockSpec(shape, lambda i: (0, 0))

    def widen(out_ref, grad_ref, gains_ref, *refs):
        wide_out, wide_grad, gain_one, gain_two = refs[len(small) : len(small) + 4]
        wide_out[...] = out_ref[...].astype(F32)
        wide_grad[...] = grad_ref[...].astype(F32)

        @pl.when(pl.program_id(0) == 0)
        def _():
            gain_one[...] = gains_ref[0:1]
            gain_two[...] = gains_ref[1:2]
            for low_ref, wide_ref in zip(refs[: len(small)], refs[len(small) + 4 :]):
                wide_ref[...] = low_ref[...].astype(F32)

    outputs, input_grad, gain_one, gain_two, dwk, dwv, dwq, dwo, up, down = pl.pallas_call(
        widen,
        grid=(count * grains,),
        in_specs=[block, block, fixed((8, own))] + [fixed(shape) for shape in small],
        out_specs=[block, block, fixed((1, own)), fixed((1, own))] + [fixed(shape) for shape in small],
        out_shape=[sd((count, length, D), F32), sd((count, length, D), F32), sd((1, own), F32), sd((1, own), F32)]
        + [sd(shape, F32) for shape in small],
        compiler_params=pltpu.CompilerParams(vmem_limit_bytes=63 * 2**20),
        name="widen",
    )(outputs, input_grad, gain_grads, dwk, dwv, dwq, dwo, up, down)
    return (
        outputs, input_grad, gain_one.reshape(own), dwq, dwk, dwv, dwo, gain_two.reshape(own), up, down,
    )


def solution(mesh):
    in_specs = (
        P("dp", "seq", None),
        P("dp", "seq", None),
        P("dp", "seq"),
        P(),
        P("dp"),
        P("dp", None),
        P("dp", None),
        P("dp", None),
        P("dp", None),
        P("dp"),
        P("dp", None),
        P("dp", None),
    )
    out_specs = (
        P("dp", "seq", None),
        P("dp", "seq", None),
        P("dp"),
        P("dp", None),
        P("dp", None),
        P("dp", None),
        P("dp", None),
        P("dp"),
        P("dp", None),
        P("dp", None),
    )
    sizes = (mesh.shape["dp"], mesh.shape["seq"])
    return jax.shard_map(functools.partial(on_device, sizes), mesh=mesh, in_specs=in_specs, out_specs=out_specs, check_vma=False)
```

```python
import functools
import math

import jax
import jax.numpy as jnp
from jax import lax
from jax.experimental import pallas as pl
from jax.experimental.pallas import tpu as pltpu
from jax.sharding import PartitionSpec as P

D = 512
HEADS = 8
PAIRS = 4
HEAD_DIM = 64
FEATURES = 256
FF = 2048
CHUNKS = 4
KEY, VALUE, QUERY, OUT, UP, DOWN, UNITS = 0, 1, 2, 3, 4, 5, 12

epsilon = 1e-05
LOG2E = math.log2(math.e)
LOW = jnp.bfloat16
F32 = jnp.float32
MESH = pl.DeviceIdType.MESH


def scramble(hashed):
    return jnp.bitwise_xor(hashed, lax.shift_right_logical(hashed, jnp.full_like(hashed, 16)))


def uniform_entries(counter, seed):
    hashed = counter * 1664525 + seed * 22695477 + 1013904223
    hashed = scramble(hashed) * 73244475
    hashed = scramble(hashed) * 73244475
    hashed = scramble(hashed)
    low_bits = jnp.bitwise_and(hashed, 8388607)
    return (low_bits.astype(F32) + 0.5) * (1.0 / 8388608.0)


def direction_entries(index, seed):
    radius = jnp.sqrt(-2.0 * jnp.log(uniform_entries(index, seed)))
    turn = uniform_entries(index + FEATURES * HEAD_DIM, seed)
    return radius * jnp.cos(2.0 * math.pi * turn)


def feature_forms(seed, forms_ref, back_ref):
    col = lax.broadcasted_iota(jnp.int32, (HEAD_DIM, FEATURES), 1)
    row = lax.broadcasted_iota(jnp.int32, (HEAD_DIM, FEATURES), 0)
    dirs_t = direction_entries(col * HEAD_DIM + row, seed) * HEAD_DIM ** (-0.25)
    scaled = dirs_t * LOG2E
    high = scaled.astype(LOW)
    rest = (scaled - high.astype(F32)).astype(LOW)
    minus = jnp.full((HEAD_DIM, FEATURES), -1.0, LOW)
    for half, pieces in enumerate(((high, high, rest, minus), (high, high, minus, rest))):
        for at, piece in enumerate(pieces):
            forms_ref[half, at * HEAD_DIM : at * HEAD_DIM + HEAD_DIM] = piece
    one, zero = jnp.ones((FEATURES, HEAD_DIM), F32), jnp.zeros((FEATURES, HEAD_DIM), F32)
    back = dirs_t.T
    back_ref[:FEATURES] = jnp.concatenate([back, zero, one, zero], axis=1).astype(LOW)
    back_ref[FEATURES:] = jnp.concatenate([zero, back, zero, one], axis=1).astype(LOW)


def dot(left, right):
    return jnp.dot(left, right, preferred_element_type=F32)


def dot_nt(left, right):
    return lax.dot_general(left, right, (((1,), (1,)), ((), ())), preferred_element_type=F32)


def dot_tn(left, right):
    return lax.dot_general(left, right, (((0,), (0,)), ((), ())), preferred_element_type=F32)


def normalize(values):
    centred = values - jnp.mean(values, axis=-1, keepdims=True)
    scale = lax.rsqrt(jnp.mean(centred * centred, axis=-1, keepdims=True) + epsilon)
    return centred * scale, scale


def norm_grad(grad_normed, unit_rows, scale, gain):
    scaled_grad = grad_normed * gain
    first = jnp.mean(scaled_grad, axis=-1, keepdims=True)
    second = jnp.mean(scaled_grad * unit_rows, axis=-1, keepdims=True)
    return scale * (scaled_grad - first - unit_rows * second)


def unit_of(weights, unit):
    return weights[unit].reshape(D, D)


def pair_lanes(pair, base=0):
    return slice(base + pair * 128, base + pair * 128 + 128)


def head_lanes(head):
    return slice(head * 256, head * 256 + 256)


def feature_pair(rows, forms_ref):
    high = rows.astype(LOW)
    rest = (rows - high.astype(F32)).astype(LOW)
    square = (rows * rows * (LOG2E / 16.0) + 1.0 / 16.0).astype(LOW)
    h0, h1 = high[:, :64], high[:, 64:]
    r0, r1 = rest[:, :64], rest[:, 64:]
    s0, s1 = square[:, :64], square[:, 64:]
    left0 = jnp.concatenate([r0, h0, h0, s0], axis=1)
    left1 = jnp.concatenate([h1, r1, s1, h1], axis=1)
    return jnp.exp2(dot(left0, forms_ref[0])), jnp.exp2(dot(left1, forms_ref[1]))


def sums_place(parts, head):
    step = HEADS * HEAD_DIM // parts
    block = min(step, HEAD_DIM)
    runs = [divmod(head * HEAD_DIM + at, step) + (at, block) for at in range(0, HEAD_DIM, block)]
    part = head * HEAD_DIM // step
    return runs, part, step + head - -(-part * step // HEAD_DIM)


def put_sums(sums_ref, head, rows, totals):
    runs, part, row = sums_place(sums_ref.shape[0], head)
    for run_part, run_row, at, block in runs:
        sums_ref[run_part, run_row : run_row + block] = rows[at : at + block].astype(LOW)
    sums_ref[part, row : row + 1] = totals.astype(LOW)


def get_sums(sums_ref, head):
    runs, part, row = sums_place(sums_ref.shape[0], head)
    rows = [sums_ref[run_part, run_row : run_row + block] for run_part, run_row, _, block in runs]
    rows = rows[0] if len(rows) == 1 else jnp.concatenate(rows, axis=0)
    return rows, sums_ref[part, row : row + 1].astype(F32)


def spread_sums(sums_ref, spread_ref):
    for head in range(HEADS):
        own, other = (head % 2) * 64, 64 - (head % 2) * 64
        rows, totals = get_sums(sums_ref, head)
        spread_ref[head, own : own + 64] = rows
        spread_ref[head, 128 + own : 192 + own] = jnp.broadcast_to(totals, (64, 256)).astype(LOW)
        spread_ref[head, other : other + 64] = jnp.zeros((64, 256), LOW)
        spread_ref[head, 128 + other : 192 + other] = jnp.zeros((64, 256), LOW)


def spread_grads(sums_ref, spread_ref):
    for head in range(HEADS):
        own, other = (head % 2) * 64, 64 - (head % 2) * 64
        rows, totals = get_sums(sums_ref, head)
        spread_ref[head, own : own + 64] = rows
        spread_ref[head, other : other + 64] = jnp.zeros((64, 256), LOW)
        row = lax.broadcasted_iota(jnp.int32, (128, 256), 0)
        spread_ref[head, 128:] = jnp.where(row == 0, jnp.broadcast_to(totals, (128, 256)), 0.0).astype(LOW)


def keys_phase(x, gain, weights, forms_ref, state_ref, sums_ref):
    unit, _ = normalize(x)
    normed = (unit * gain).astype(LOW)
    state_ref[:, 3072:3584] = normed
    values = dot(normed, unit_of(weights, VALUE)).astype(LOW)
    state_ref[:, 2560:3072] = values
    keys = dot(normed, unit_of(weights, KEY))
    state_ref[:, 2048:2560] = keys.astype(LOW)
    ones = jnp.ones((16, x.shape[0]), LOW)
    for pair in range(PAIRS):
        phi = feature_pair(keys[:, pair_lanes(pair)], forms_ref)
        values_t = values[:, pair_lanes(pair)].T
        for half in range(2):
            head = 2 * pair + half
            low = phi[half].astype(LOW)
            state_ref[:, head_lanes(head)] = low
            left = jnp.concatenate([values_t[half * 64 : half * 64 + 64], ones], axis=0)
            got = dot(left, low)
            put_sums(sums_ref, head, got[:64], got[64:65])


def front_phase(x, upstream, mask, gain_one, gain_two, sums_arrive, sums_ref, weights, forms_ref, spread_ref, state_ref, out_ref, n2_ref, dy_ref, scale_ref):
    unit, _ = normalize(x)
    queries = dot((unit * gain_one).astype(LOW), unit_of(weights, QUERY))
    state_ref[:, 2048:2560] = queries.astype(LOW)
    for pair in range(PAIRS):
        phi0, phi1 = feature_pair(queries[:, pair_lanes(pair)], forms_ref)
        state_ref[:, head_lanes(2 * pair)] = phi0.astype(LOW)
        state_ref[:, head_lanes(2 * pair + 1)] = phi1.astype(LOW)
    lanes = mask.shape[1]
    for at in range(0, D, lanes):
        dy_ref[:, at : at + lanes] = (upstream[:, at : at + lanes] * mask).astype(LOW)
    sums_arrive()
    spread_sums(sums_ref, spread_ref)
    for pair in range(PAIRS):
        low0, low1 = state_ref[:, head_lanes(2 * pair)], state_ref[:, head_lanes(2 * pair + 1)]
        both = dot_nt(low0, spread_ref[2 * pair]) + dot_nt(low1, spread_ref[2 * pair + 1])
        reciprocal = 1.0 / both[:, 128:]
        state_ref[:, pair_lanes(pair, 2560)] = (both[:, :128] * reciprocal).astype(LOW)
        state_ref[:, pair_lanes(pair, 3072)] = reciprocal.astype(LOW)
    mid = x + dot(state_ref[:, 2560:3072], unit_of(weights, OUT))
    unit, scale = normalize(mid)
    n2_ref[...] = (unit * gain_two).astype(LOW)
    scale_ref[...] = jnp.broadcast_to(scale, scale_ref.shape)
    out_ref[...] = mid


def ffn_phase(first, n2, dy, w_up, w_down, out_ref, low_out_ref, dn2_ref, up_grad_ref, down_grad_ref):
    hidden = dot(n2, w_up)
    cumulative = 0.5 * (1.0 + lax.erf(hidden * (1.0 / math.sqrt(2.0))))
    density = jnp.exp2(hidden * hidden * (-0.5 * LOG2E)) * (1.0 / math.sqrt(2.0 * math.pi))
    act = (hidden * cumulative).astype(LOW)
    du = (dot_nt(dy, w_down) * (cumulative + hidden * density)).astype(LOW)
    if low_out_ref is None:
        out_ref[...] += dot(act, w_down)
    else:
        low_out_ref[...] = (out_ref[...] + dot(act, w_down)).astype(LOW)
    down_grad_ref[...] += dot_tn(act, dy)
    dn2 = dot_nt(du, w_up)
    if first:
        dn2_ref[...] = dn2
    else:
        dn2_ref[...] += dn2
    up_grad_ref[...] += dot_tn(n2, du)


def attention_grad_phase(dy, dn2, n2, scale, gain, sums_ref, weights, back_ref, state_ref, spread_ref, gain_grad_ref, w_out_grad_ref, da_ref, dq_ref, grad_sums_ref):
    spread_sums(sums_ref, spread_ref)
    unit = n2.astype(F32) * (1.0 / gain)
    gain_grad_ref[...] += jnp.sum(dn2 * unit, axis=0, keepdims=True)
    da = (dy.astype(F32) + norm_grad(dn2, unit, scale, gain)).astype(LOW)
    da_ref[...] = da
    w_out_grad_ref[...] += dot_tn(state_ref[:, 2560:3072], da)
    datt = dot_nt(da, unit_of(weights, OUT))
    for pair in range(PAIRS):
        dnumer = datt[:, pair_lanes(pair)] * state_ref[:, pair_lanes(pair, 3072)].astype(F32)
        weighted = -dnumer * state_ref[:, pair_lanes(pair, 2560)].astype(F32)
        left = jnp.concatenate([dnumer.astype(LOW), weighted.astype(LOW)], axis=1)
        left_t = left.T
        parts = []
        for half in range(2):
            head, own = 2 * pair + half, half * 64
            pq = state_ref[:, head_lanes(head)]
            dden = jnp.sum(left_t[128 + own : 192 + own].astype(F32), axis=0, keepdims=True)
            rows = jnp.concatenate(
                [left_t[own : own + 64], jnp.broadcast_to(dden, (16, dden.shape[1])).astype(LOW)], axis=0
            )
            got = dot(rows, pq)
            put_sums(grad_sums_ref, head, got[:64], got[64:65])
            parts.append((dot(left, spread_ref[head]) * pq.astype(F32)).astype(LOW))
        grads = dot(parts[0], back_ref[:256]) + dot(parts[1], back_ref[256:])
        q = state_ref[:, pair_lanes(pair, 2048)].astype(F32)
        dq_ref[:, pair_lanes(pair)] = (grads[:, :128] - grads[:, 128:] * q * 0.125).astype(LOW)


def keys_grad_phase(sums_ref, back_ref, state_ref, spread_ref, dq_ref, dk_ref, dv_ref, att_grad_ref):
    spread_grads(sums_ref, spread_ref)
    ones = jnp.ones((dk_ref.shape[0], 128), LOW)
    for pair in range(PAIRS):
        left = jnp.concatenate([state_ref[:, pair_lanes(pair, 2560)], ones], axis=1)
        parts = []
        dv = None
        for half in range(2):
            head = 2 * pair + half
            pk = state_ref[:, head_lanes(head)]
            parts.append((dot(left, spread_ref[head]) * pk.astype(F32)).astype(LOW))
            piece = dot_nt(pk, spread_ref[head, :128])
            dv = piece if dv is None else dv + piece
        dv_ref[:, pair_lanes(pair)] = dv.astype(LOW)
        grads = dot(parts[0], back_ref[:256]) + dot(parts[1], back_ref[256:])
        k = state_ref[:, pair_lanes(pair, 2048)].astype(F32)
        dk_ref[:, pair_lanes(pair)] = (grads[:, :128] - grads[:, 128:] * k * 0.125).astype(LOW)
    normed = state_ref[:, 3072:3584]
    att_grad_ref[KEY] += dot_tn(normed, dk_ref[...])
    att_grad_ref[VALUE] += dot_tn(normed, dv_ref[...])
    att_grad_ref[QUERY] += dot_tn(normed, dq_ref[...])


def input_grad_phase(x, da_ref, dq, dk, dv, gain, weights, gain_grad_ref):
    dn1 = dot_nt(dq, unit_of(weights, QUERY)) + dot_nt(dk, unit_of(weights, KEY)) + dot_nt(dv, unit_of(weights, VALUE))
    unit, scale = normalize(x)
    gain_grad_ref[...] += jnp.sum(dn1 * unit, axis=0, keepdims=True)
    da_ref[...] = (da_ref[...].astype(F32) + norm_grad(dn1, unit, scale, gain)).astype(LOW)


class Place:
    def __init__(self, n_dp, n_seq):
        self.n_dp, self.n_seq, self.n_z = n_dp, n_seq, n_dp // 2
        self.dp, self.seq = lax.axis_index("dp"), lax.axis_index("seq")
        self.z, self.core = self.dp // 2, lax.rem(self.dp, 2)

    def up_z(self, step):
        return lax.rem(self.z + step, self.n_z)

    def up_seq(self, step):
        return lax.rem(self.seq + step, self.n_seq)

    def down_z(self, step):
        return lax.rem(self.z + (self.n_z - step), self.n_z)

    def owner(self, z):
        return z * 2 + self.core

    def other_core(self):
        return (self.z * 2 + 1 - self.core, self.seq)

    def arrive(self):
        barrier = pltpu.get_barrier_semaphore()
        for step in range(1, self.n_dp):
            other = lax.rem(self.dp + step, self.n_dp)
            pl.semaphore_signal(barrier, inc=1, device_id=(other, self.seq), device_id_type=MESH)
        for step in range(1, self.n_seq):
            pl.semaphore_signal(barrier, inc=1, device_id=(self.dp, self.up_seq(step)), device_id_type=MESH)

    def meet(self):
        pl.semaphore_wait(pltpu.get_barrier_semaphore(), self.n_dp - 1 + self.n_seq - 1)


def remote(source, target, sems, at, device):
    return pltpu.make_async_remote_copy(
        src_ref=source, dst_ref=target, send_sem=sems[0].at[at], recv_sem=sems[1].at[at],
        device_id=device, device_id_type=MESH,
    )


def semaphores(*shape):
    return [pltpu.SemaphoreType.DMA(shape), pltpu.SemaphoreType.DMA(shape)]


class Gather:
    def __init__(self, place, weights, first, count, index, sems, line=False):
        self.place, self.weights, self.first, self.count, self.index = place, weights, first, count, index
        self.line = line
        self.own = D // place.n_dp
        self.across = min(place.n_seq, D // 128)
        self.units = count // (place.n_seq // self.across)
        self.z_sems, self.plane_sems, self.core_sems = sems

    def piece(self, z, part):
        columns = D // self.across
        first = self.first + (part // self.across) * self.units
        left = pl.multiple_of(lax.rem(part, self.across) * columns, 128)
        return self.weights.at[pl.ds(first, self.units), z, self.place.core, :, pl.ds(left, columns)]

    def shard(self, z):
        return self.weights.at[pl.ds(self.first, self.count), z, self.place.core]

    def z_copy(self, step):
        place = self.place
        piece = self.shard(place.z) if self.line else self.piece(place.z, place.seq)
        return remote(piece, piece, self.z_sems, (self.index, step - 1), (place.owner(place.up_z(step)), place.seq))

    def plane_copy(self, step, to):
        place = self.place
        piece = self.piece(place.down_z(step), place.seq)
        return remote(piece, piece, self.plane_sems, (self.index, step - 1, to - 1), (place.dp, place.up_seq(to)))

    def core_copy(self):
        shards = self.weights.at[pl.ds(self.first, self.count), :, self.place.core]
        return remote(shards, shards, self.core_sems, self.index, self.place.other_core())

    def start(self):
        for step in range(1, self.place.n_z):
            self.z_copy(step).start()

    def to_plane(self):
        for step in range(1, self.place.n_z):
            self.z_copy(step).wait_recv()
            for to in range(1, self.place.n_seq):
                self.plane_copy(step, to).start()

    def to_core(self):
        for step in range(1, self.place.n_z):
            if self.line:
                self.z_copy(step).wait_recv()
            else:
                for to in range(1, self.place.n_seq):
                    self.plane_copy(step, to).wait_recv()
        self.core_copy().start()

    def finish(self):
        self.core_copy().wait_recv()

    def drain(self):
        for step in range(1, self.place.n_z):
            self.z_copy(step).wait_send()
            if not self.line:
                for to in range(1, self.place.n_seq):
                    self.plane_copy(step, to).wait_send()
        self.core_copy().wait_send()


class Sums:
    def __init__(self, place, local, arrived, full, add_sems, full_sems):
        self.place, self.local, self.arrived, self.full = place, local, arrived, full
        self.add_sems, self.full_sems = add_sems, full_sems

    def add_copy(self, slot, index, to):
        other = self.place.up_seq(to)
        return remote(
            self.local.at[slot, other], self.arrived.at[index, to - 1], self.add_sems, (index, to - 1),
            (self.place.dp, other),
        )

    def full_copy(self, index, to):
        place = self.place
        mine = self.full.at[index, place.seq]
        return remote(mine, mine, self.full_sems, (index, to - 1), (place.dp, place.up_seq(to)))

    def start(self, slot, index):
        for to in range(1, self.place.n_seq):
            self.add_copy(slot, index, to).start()

    def add(self, slot, index):
        place = self.place
        total = self.local[slot, place.seq].astype(F32)
        for to in range(1, place.n_seq):
            self.add_copy(slot, index, to).wait_recv()
            total = total + self.arrived[index, to - 1].astype(F32)
        self.full[index, place.seq] = total.astype(LOW)
        for to in range(1, place.n_seq):
            self.full_copy(index, to).start()
        for to in range(1, place.n_seq):
            self.add_copy(slot, index, to).wait_send()

    def finish(self, index):
        for to in range(1, self.place.n_seq):
            self.full_copy(index, to).wait_recv()

    def drain(self, index):
        for to in range(1, self.place.n_seq):
            self.full_copy(index, to).wait_send()


class Scatter:
    REFS = 14

    def __init__(self, place, refs, z_first, kept=None):
        self.place, self.z_first, self.kept = place, z_first, kept
        self.out, self.mine, self.arrived, self.first, self.second, self.final = refs[:6]
        self.core_sems, self.plane_sems, self.z_sems, self.full_sems = refs[6:8], refs[8:10], refs[10:12], refs[12:14]
        self.own = D // place.n_dp
        self.across = min(place.n_seq, D // 128)
        self.lanes = D // self.across
        self.units = self.out.shape[2]
        self.n_first, self.n_second = (place.n_z, place.n_seq) if z_first else (place.n_seq, place.n_z)

    @staticmethod
    def shapes(n_dp, n_seq, units, z_first, keep):
        own, n_z = D // n_dp, n_dp // 2
        part = (units, own, D // min(n_seq, D // 128))
        n_first, n_second = (n_z, n_seq) if z_first else (n_seq, n_z)
        return [
            pltpu.VMEM((n_seq, n_z) + part, LOW), pltpu.VMEM((n_seq, n_z) + part if keep else (16, 128), LOW),
            pltpu.VMEM((n_seq, n_z) + part, LOW), pltpu.VMEM(((n_first - 1) * n_second,) + part, LOW),
            pltpu.VMEM((2 * n_second - 1,) + part, LOW), pltpu.VMEM((n_seq,) + part, LOW),
            *semaphores(1), *semaphores(n_seq - 1), *semaphores(n_z - 1), *semaphores(n_seq - 1),
        ]

    def block(self, grads, owner, lane_part):
        rows = pl.ds(pl.multiple_of(owner * self.own, self.own), self.own)
        return grads[rows, lane_part * self.lanes : lane_part * self.lanes + self.lanes]

    def core_copy(self):
        return remote(self.out, self.arrived, self.core_sems, 0, self.place.other_core())

    def axis_copy(self, along_z, step, source, target):
        place = self.place
        if along_z:
            return remote(source, target, self.z_sems, step - 1, (place.owner(place.up_z(step)), place.seq))
        return remote(source, target, self.plane_sems, step - 1, (place.dp, place.up_seq(step)))

    def first_copy(self, step):
        place = self.place
        source = self.arrived.at[:, place.up_z(step)] if self.z_first else self.arrived.at[place.up_seq(step)]
        target = self.first.at[pl.ds((step - 1) * self.n_second, self.n_second)]
        return self.axis_copy(self.z_first, step, source, target)

    def second_copy(self, step):
        place = self.place
        other = place.up_seq(step) if self.z_first else place.up_z(step)
        return self.axis_copy(not self.z_first, step, self.second.at[other], self.second.at[self.n_second + step - 1])

    def full_copy(self, to):
        place = self.place
        mine = self.final.at[place.seq]
        return remote(mine, mine, self.full_sems, to - 1, (place.dp, place.up_seq(to)))

    def put(self, unit, group, grads):
        place = self.place
        for lane_part in range(self.across):
            part = group * self.across + lane_part
            for z in range(place.n_z):
                self.out[part, z, unit] = self.block(grads, z * 2 + 1 - place.core, lane_part).astype(LOW)
                if self.kept is None:
                    self.mine[part, z, unit] = self.block(grads, place.owner(z), lane_part).astype(LOW)

    def start(self):
        self.core_copy().start()

    def to_first(self):
        place = self.place
        self.core_copy().wait_recv()
        for part in range(place.n_seq):
            for z in range(place.n_z):
                for unit in range(self.units):
                    if self.kept is None:
                        mine = self.mine[part, z, unit].astype(F32)
                    else:
                        grads = self.kept[part // self.across * self.units + unit]
                        mine = self.block(grads, place.owner(z), part % self.across)
                    self.arrived[part, z, unit] = (mine + self.arrived[part, z, unit].astype(F32)).astype(LOW)
        for step in range(1, self.n_first):
            self.first_copy(step).start()

    def to_second(self):
        place = self.place
        for step in range(1, self.n_first):
            self.first_copy(step).wait_recv()
        for at in range(self.n_second):
            total = self.arrived[at, place.z] if self.z_first else self.arrived[place.seq, at]
            total = total.astype(F32)
            for step in range(1, self.n_first):
                total = total + self.first[(step - 1) * self.n_second + at].astype(F32)
            self.second[at] = total.astype(LOW)
        for step in range(1, self.n_second):
            self.second_copy(step).start()

    def to_copies(self):
        place = self.place
        total = self.second[place.seq if self.z_first else place.z].astype(F32)
        for step in range(1, self.n_second):
            self.second_copy(step).wait_recv()
            total = total + self.second[self.n_second + step - 1].astype(F32)
        self.final[place.seq] = total.astype(LOW)
        for to in range(1, place.n_seq):
            self.full_copy(to).start()

    def finish(self):
        for to in range(1, self.place.n_seq):
            self.full_copy(to).wait_recv()

    def result(self, unit, group=0):
        parts = [self.final[group * self.across + at, unit] for at in range(self.across)]
        return jnp.concatenate(parts, axis=1)

    def drain(self):
        self.core_copy().wait_send()
        for step in range(1, self.n_first):
            self.first_copy(step).wait_send()
        for step in range(1, self.n_second):
            self.second_copy(step).wait_send()
        for to in range(1, self.place.n_seq):
            self.full_copy(to).wait_send()


UP_HALF, DOWN_HALF = 0, 1


def scatter_plan(group):
    def chunk(at):
        return [(UP_HALF, at), (DOWN_HALF, at)]

    if group == 1:
        return [
            (chunk(0), False),
            (chunk(1), False),
            (chunk(2), True),
            ([(UP_HALF, 3), ("att", OUT)], False),
            ([(DOWN_HALF, 3)], True),
            ([("att", KEY)], True),
            ([("att", VALUE), ("att", QUERY)], False),
        ]
    return [([(UP_HALF, None), (DOWN_HALF, None)], False), ([("att", None)], False)]


STATE = 2048 + 3 * D


def layer_kernel(
    sizes, x_hbm, cot_hbm, mask_ref, gains_own, wq, wk, wv, wo, wu, wd, seed_ref,
    out_hbm, grad_hbm, gain_grads_ref, dwk, dwv, dwq, dwo, up_ref, down_ref, state_hbm,
    weights, gain_buf, gains, att_grad, up_grad, down_grad, gain_sums, gain_mail,
    local, arrived, full, state, spread, n2_buf, dy_buf, da_buf, dq_buf, out_buf, out_low, pool, scale_buf,
    forms_ref, back_ref, x_sems, cot_sems, write_sems, read_sems, out_sems, grad_sems, *rest,
):
    n_dp, n_seq = sizes
    count = x_hbm.shape[0]
    own = D // n_dp
    place = Place(n_dp, n_seq)
    group = max(1, n_seq // (D // 128))
    gather_sems = (rest[0:2], rest[2:4], rest[4:6])
    gain_sems, mail_sems = rest[6:8], rest[8:10]
    sums_refs = (place, local, arrived, full, rest[10:12], rest[12:14])
    scatter_refs = rest[14:]

    my_rows = pl.ds(pl.multiple_of(place.dp * own, own), own)

    def x_copy(step):
        slot = lax.rem(step, 2)
        return pltpu.make_async_copy(x_hbm.at[lax.rem(step, count)], att_grad.at[QUERY + slot], x_sems.at[slot])

    def x_again(index):
        slot = lax.rem(index, 2)
        return pltpu.make_async_copy(x_hbm.at[index], pool.at[slot], x_sems.at[slot])

    def cot_copy(index):
        return pltpu.make_async_copy(cot_hbm.at[index], out_buf.at[index], cot_sems.at[index])

    def write_copy(step):
        slot = lax.rem(step, 2)
        return pltpu.make_async_copy(state.at[slot], state_hbm.at[step], write_sems.at[slot])

    def read_copy(event):
        slot = lax.rem(event, 2)
        return pltpu.make_async_copy(
            state_hbm.at[lax.rem(count + event, 2 * count)], state.at[slot], read_sems.at[slot]
        )

    def out_copy(index):
        return pltpu.make_async_copy(out_low, out_hbm.at[index], out_sems.at[index])

    def grad_copy(index):
        return pltpu.make_async_copy(da_buf.at[index], grad_hbm.at[index], grad_sems.at[index])

    place.arrive()
    x_copy(0).start()
    for index in range(count):
        cot_copy(index).start()
    for unit, ref in ((KEY, wk), (VALUE, wv), (QUERY, wq), (OUT, wo)):
        weights[unit, place.z, place.core] = ref[...].astype(LOW)
    for chunk in range(CHUNKS):
        columns = [wu[:, (r * CHUNKS + chunk) * own : (r * CHUNKS + chunk + 1) * own] for r in range(n_dp)]
        weights[UP + 2 * chunk, place.z, place.core] = jnp.concatenate(columns, axis=1).astype(LOW)
        weights[DOWN + 2 * chunk, place.z, place.core] = wd[chunk * own : chunk * own + own].astype(LOW)
    gain_buf[my_rows] = gains_own[...]
    place.meet()

    runs = [(KEY, 2), (QUERY, 2)] if group == 1 else [(KEY, 4)]
    gathers = [Gather(place, weights, first, units, at, gather_sems, line=False) for at, (first, units) in enumerate(runs)]
    keys_gathers, att_gathers = gathers[:1], gathers[1:]
    ffn_gathers = [
        Gather(place, weights, UP + 2 * chunk, 2, len(runs) + chunk, gather_sems, line=True) for chunk in range(CHUNKS)
    ]
    gathers = gathers + ffn_gathers

    def gain_copy(step):
        mine = gain_buf.at[my_rows]
        other = lax.rem(place.dp + step, n_dp)
        return remote(mine, mine, gain_sems, step - 1, (other, place.seq))

    for step in range(1, n_dp):
        gain_copy(step).start()
    for item in keys_gathers:
        item.start()
    feature_forms(seed_ref[0], forms_ref, back_ref)
    gathers[0].to_plane()
    gain_sums[...] = jnp.zeros_like(gain_sums)
    for item in keys_gathers[1:]:
        item.to_core()
    for item in att_gathers + ffn_gathers[:1]:
        item.start()
    gathers[0].to_core()
    for step in range(1, n_dp):
        gain_copy(step).wait_recv()
    gains[...] = gain_buf[...].astype(F32).T[:8]
    for item in keys_gathers:
        item.finish()
    for item in att_gathers:
        item.to_plane()

    sums = Sums(*sums_refs)

    def keys_step(index, carry):
        slot = lax.rem(index, 2)
        x_copy(index + 1).start()

        @pl.when(index >= 2)
        def _():
            write_copy(index - 2).wait()

        x_copy(index).wait()
        keys_phase(att_grad[QUERY + slot], gains[0:1], weights, forms_ref, state.at[slot], local.at[slot])
        sums.start(slot, index)
        write_copy(index).start()

        @pl.when(index > 0)
        def _():
            sums.add(1 - slot, index - 1)

        @pl.when(index == 0)
        def _():
            ffn_gathers[1].start()

        @pl.when(index == 2)
        def _():
            for item in att_gathers:
                item.to_core()

        @pl.when(index == count - 1)
        def _():
            ffn_gathers[0].to_core()
            ffn_gathers[2].start()

        return carry

    lax.fori_loop(0, count, keys_step, 0)
    for item in att_gathers:
        item.finish()

    plan = scatter_plan(group)
    items, of_unit = [], {}
    for at, (units, z_first) in enumerate(plan):
        kept = None
        if all(kind == "att" for kind, _ in units):
            kept = [att_grad.at[index] for _, index in units] if group == 1 else [att_grad.at[index] for index in range(4)]
        item = Scatter(place, scatter_refs[at * Scatter.REFS : (at + 1) * Scatter.REFS], z_first, kept)
        items.append(item)
        for position, unit in enumerate(units):
            of_unit[unit] = (item, position)

    def put(kind, index, grads):
        if group == 1:
            item, position = of_unit[kind, index]
            item.put(position, 0, grads)
        else:
            item, position = of_unit[kind, None]
            item.put(position, index, grads)

    def result(kind, index):
        if group == 1:
            item, position = of_unit[kind, index]
            return item.result(position)
        item, position = of_unit[kind, None]
        return item.result(position, index)

    def chunk_grads(chunk):
        return (att_grad.at[KEY], att_grad.at[VALUE]) if chunk == 1 else (up_grad, down_grad)

    def open_chunk(chunk):
        for ref in chunk_grads(chunk):
            ref[...] = jnp.zeros(ref.shape, F32)

    def ffn_step(chunk, index):
        ffn_phase(
            chunk == 0, n2_buf[index], dy_buf[index], unit_of(weights, UP + 2 * chunk), unit_of(weights, DOWN + 2 * chunk),
            out_buf.at[index], out_low if chunk == CHUNKS - 1 else None, pool.at[index], *chunk_grads(chunk),
        )

    def close_chunk(chunk):
        for kind, grads in zip((UP_HALF, DOWN_HALF), chunk_grads(chunk)):
            put(kind, chunk, grads)

    def front_step(index, carry):
        step = count + index
        slot = lax.rem(step, 2)

        @pl.when(index + 1 < count)
        def _():
            x_copy(step + 1).start()

        write_copy(step - 2).wait()
        x_copy(step).wait()
        cot_copy(index).wait()

        def sums_arrive():
            @pl.when(index == 0)
            def _():
                sums.add((count - 1) % 2, count - 1)

            sums.finish(index)

        mask = jnp.broadcast_to(mask_ref[pl.ds(index, 1)].astype(F32), (128, mask_ref.shape[1])).T
        front_phase(
            att_grad[QUERY + slot], out_buf[index], mask, gains[0:1], gains[1:2], sums_arrive, full.at[index], weights,
            forms_ref, spread, state.at[slot], out_buf.at[index], n2_buf.at[index], dy_buf.at[index],
            scale_buf.at[index],
        )
        write_copy(step).start()

        @pl.when(index == 0)
        def _():
            ffn_gathers[0].finish()

        ffn_step(0, index)

        @pl.when(index == 1)
        def _():
            ffn_gathers[1].to_core()
            ffn_gathers[3].start()

        return carry

    open_chunk(0)
    open_chunk(1)
    lax.fori_loop(0, count, front_step, 0)
    for step in (2 * count - 2, 2 * count - 1):
        write_copy(step).wait()
    read_copy(0).start()
    read_copy(1).start()
    ffn_gathers[1].finish()

    close_chunk(0)
    first_items, second_items, third_items, last_items, late_items = (
        (items[:1], items[1:2], items[2:3], items[3:5], items[5:7]) if group == 1 else ([], [], [], items[:1], items[1:])
    )
    for item in first_items:
        item.start()

    def second_step(index, carry):
        ffn_step(1, index)

        @pl.when(index == 1)
        def _():
            for item in first_items:
                item.to_first()

        @pl.when(index == 1)
        def _():
            ffn_gathers[2].to_core()

        return carry

    lax.fori_loop(0, count, second_step, 0)
    close_chunk(1)
    for item in second_items:
        item.start()
    att_grad[...] = jnp.zeros_like(att_grad)
    ffn_gathers[2].finish()
    open_chunk(2)

    def third_step(index, carry):
        ffn_step(2, index)

        @pl.when(index == 1)
        def _():
            for item in second_items:
                item.to_first()
            for item in first_items:
                item.to_second()

        @pl.when(index == 2)
        def _():
            ffn_gathers[3].to_core()

        return carry

    lax.fori_loop(0, count, third_step, 0)
    close_chunk(2)
    for item in third_items:
        item.start()
    ffn_gathers[3].finish()
    open_chunk(3)

    grad_sums = Sums(place, local, arrived.at[pl.ds(count, count)], full.at[pl.ds(count, count)], rest[10:12], rest[12:14])
    grad_sums.add_sems = [ref.at[pl.ds(count, count)] for ref in rest[10:12]]
    grad_sums.full_sems = [ref.at[pl.ds(count, count)] for ref in rest[12:14]]

    def attention_step(index, carry):
        slot = lax.rem(index, 2)

        @pl.when(index > 0)
        def _():
            out_copy(index - 1).wait()

        ffn_step(CHUNKS - 1, index)
        out_copy(index).start()
        read_copy(index).wait()
        attention_grad_phase(
            dy_buf[index], pool[index], n2_buf[index], scale_buf[index][:, :1], gains[1:2], full.at[index], weights,
            back_ref, state.at[slot], spread, gain_sums.at[1:2], att_grad.at[OUT], da_buf.at[index],
            dq_buf.at[index], local.at[slot],
        )
        grad_sums.start(slot, index)
        read_copy(index + 2).start()

        @pl.when(index > 0)
        def _():
            grad_sums.add(1 - slot, index - 1)

        @pl.when(index == 0)
        def _():
            for item in third_items:
                item.to_first()

        @pl.when(index == 1)
        def _():
            for item in first_items:
                item.to_copies()

        @pl.when(index == 2)
        def _():
            for item in second_items:
                item.to_second()

        @pl.when(index == count - 1)
        def _():
            for item in third_items:
                item.to_second()

        return carry

    lax.fori_loop(0, count, attention_step, 0)
    close_chunk(CHUNKS - 1)
    if group == 1:
        put("att", OUT, att_grad.at[OUT])
    for item in last_items:
        item.start()
    x_again(0).start()

    dk_buf, dv_buf = n2_buf, dy_buf

    def keys_grad_step(index, carry):
        event = count + index
        slot = lax.rem(event, 2)
        read_copy(event).wait()
        grad_sums.finish(index)
        keys_grad_phase(
            full.at[count + index], back_ref, state.at[slot], spread, dq_buf.at[index], dk_buf.at[index],
            dv_buf.at[index], att_grad,
        )

        @pl.when(index + 2 < count)
        def _():
            read_copy(event + 2).start()

        @pl.when(index == 0)
        def _():
            grad_sums.add((count - 1) % 2, count - 1)
            for item in second_items:
                item.to_copies()

        @pl.when(index == 1)
        def _():
            for item in last_items:
                item.to_first()

        @pl.when(index == 2)
        def _():
            for item in third_items:
                item.to_copies()

        return carry

    lax.fori_loop(0, count, keys_grad_step, 0)
    for unit in (KEY, VALUE, QUERY) + (() if group == 1 else (OUT,)):
        put("att", unit, att_grad.at[unit])
    for item in late_items:
        item.start()

    def input_grad_step(index, carry):
        slot = lax.rem(index, 2)

        @pl.when(index + 1 < count)
        def _():
            x_again(index + 1).start()

        x_again(index).wait()
        input_grad_phase(
            pool[slot], da_buf.at[index], dq_buf[index], dk_buf[index], dv_buf[index], gains[0:1], weights,
            gain_sums.at[0:1],
        )
        grad_copy(index).start()

        @pl.when(index == 0)
        def _():
            for item in late_items:
                item.to_first()

        @pl.when(index == 2)
        def _():
            for item in last_items:
                item.to_second()


        return carry

    lax.fori_loop(0, count, input_grad_step, 0)

    def mail_plane(step):
        mine = gain_mail.at[place.seq]
        return remote(mine, mine, mail_sems, step - 1, (place.dp, place.up_seq(step)))

    def mail_dp(step):
        mine = gain_mail.at[n_seq + place.dp]
        other = lax.rem(place.dp + step, n_dp)
        return remote(mine, mine, mail_sems, n_seq - 2 + step, (other, place.seq))

    gain_mail[place.seq] = gain_sums[...]
    for step in range(1, n_seq):
        mail_plane(step).start()
    for item in late_items:
        item.to_second()
    for item in last_items:
        item.to_copies()
    for step in range(1, n_seq):
        mail_plane(step).wait_recv()
    total = gain_mail[0]
    for at in range(1, n_seq):
        total = total + gain_mail[at]
    gain_mail[n_seq + place.dp] = total
    for step in range(1, n_dp):
        mail_dp(step).start()
    for item in late_items:
        item.to_copies()

    for item in first_items + second_items + third_items + last_items:
        item.finish()
    up_rows = [result(UP_HALF, chunk) for chunk in range(CHUNKS)]
    for r in range(n_dp):
        columns = [rows[:, r * own : r * own + own] for rows in up_rows]
        up_ref[:, r * CHUNKS * own : (r + 1) * CHUNKS * own] = jnp.concatenate(columns, axis=1)
    for chunk in range(CHUNKS):
        down_ref[chunk * own : chunk * own + own] = result(DOWN_HALF, chunk)
    if group == 1:
        dwo[...] = result("att", OUT)
    for step in range(1, n_dp):
        mail_dp(step).wait_recv()
    total = gain_mail[n_seq]
    for at in range(1, n_dp):
        total = total + gain_mail[n_seq + at]
    own_gains = jnp.zeros((8, own), F32)
    for r in range(n_dp):
        own_gains = jnp.where(place.dp == r, total[:, r * own : r * own + own], own_gains)
    gain_grads_ref[...] = own_gains
    for item in late_items:
        item.finish()
    for unit, ref in ((KEY, dwk), (VALUE, dwv), (QUERY, dwq)) + (() if group == 1 else ((OUT, dwo),)):
        ref[...] = result("att", unit)

    for item in items:
        item.drain()
    for step in range(1, n_seq):
        mail_plane(step).wait_send()
    for step in range(1, n_dp):
        mail_dp(step).wait_send()
        gain_copy(step).wait_send()
    for item in gathers:
        item.drain()
    for index in range(count):
        sums.drain(index)
        grad_sums.drain(index)
        grad_copy(index).wait()
    out_copy(count - 1).wait()


def on_device(sizes, inputs, cotangent, masked, proj_seed, gain_attn, w_query, w_key, w_value, w_out, gain_ffn, w_up, w_down):
    n_dp, n_seq = sizes
    count, length = inputs.shape[0], inputs.shape[1]
    own, own_ff = D // n_dp, FF // n_dp
    group = max(1, n_seq // (D // 128))
    n_gathers = CHUNKS + (2 if group == 1 else 1)
    scatter_scratch = []
    for units, z_first in scatter_plan(group):
        keep = not all(kind == "att" for kind, _ in units)
        scatter_scratch += Scatter.shapes(n_dp, n_seq, len(units), z_first, keep)
    part_rows = HEADS * HEAD_DIM // n_seq + 16
    gains = jnp.pad(jnp.stack([gain_attn, gain_ffn], axis=1).astype(LOW), ((0, 0), (0, 126)))
    sd = jax.ShapeDtypeStruct
    vmem = pl.BlockSpec(memory_space=pltpu.VMEM)
    anywhere = pl.BlockSpec(memory_space=pl.ANY)
    outputs, input_grad, gain_grads, dwk, dwv, dwq, dwo, up, down, _ = pl.pallas_call(
        functools.partial(layer_kernel, sizes),
        in_specs=[anywhere, anywhere] + [vmem] * 8 + [pl.BlockSpec(memory_space=pltpu.SMEM)],
        out_specs=[anywhere, anywhere] + [vmem] * 7 + [anywhere],
        out_shape=[
            sd((count, length, D), LOW), sd((count, length, D), LOW), sd((8, own), F32), *[sd((own, D), LOW)] * 4,
            sd((own, FF), LOW), sd((own_ff, D), LOW), sd((2 * count, length, STATE), LOW),
        ],
        scratch_shapes=[
            pltpu.VMEM((UNITS, n_dp // 2, 2, own, D), LOW), pltpu.VMEM((D, 128), LOW), pltpu.VMEM((8, D), F32),
            pltpu.VMEM((4, D, D), F32), pltpu.VMEM((D, D), F32), pltpu.VMEM((D, D), F32),
            pltpu.VMEM((8, D), F32), pltpu.VMEM((n_seq + n_dp, 8, D), F32),
            pltpu.VMEM((2, n_seq, part_rows, 256), LOW), pltpu.VMEM((2 * count, n_seq - 1, part_rows, 256), LOW),
            pltpu.VMEM((2 * count, n_seq, part_rows, 256), LOW),
            pltpu.VMEM((2, length, STATE), LOW), pltpu.VMEM((HEADS, 256, 256), LOW),
            pltpu.VMEM((count, length, D), LOW), pltpu.VMEM((count, length, D), LOW),
            pltpu.VMEM((count, length, D), LOW), pltpu.VMEM((count, length, D), LOW),
            pltpu.VMEM((count, length, D), F32), pltpu.VMEM((length, D), LOW), pltpu.VMEM((count, length, D), F32),
            pltpu.VMEM((count, length, 128), F32),
            pltpu.VMEM((2, 256, 256), LOW), pltpu.VMEM((512, 256), LOW),
            pltpu.SemaphoreType.DMA((2,)), pltpu.SemaphoreType.DMA((count,)),
            pltpu.SemaphoreType.DMA((2,)), pltpu.SemaphoreType.DMA((2,)),
            pltpu.SemaphoreType.DMA((count,)), pltpu.SemaphoreType.DMA((count,)),
            *semaphores(n_gathers, n_dp // 2 - 1), *semaphores(n_gathers, n_dp // 2 - 1, n_seq - 1),
            *semaphores(n_gathers),
            *semaphores(n_dp - 1), *semaphores(n_seq + n_dp - 2),
            *semaphores(2 * count, n_seq - 1), *semaphores(2 * count, n_seq - 1),
            *scatter_scratch,
        ],
        compiler_params=pltpu.CompilerParams(
            vmem_limit_bytes=63 * 2**20, collective_id=0, has_side_effects=True
        ),
        name="layer",
    )(inputs, cotangent, masked, gains, w_query, w_key, w_value, w_out, w_up, w_down, proj_seed)
    grains = 2
    block = pl.BlockSpec((None, length // grains, D), lambda i: (i // grains, lax.rem(i, grains), 0))
    small = [(own, D)] * 4 + [(own, FF), (own_ff, D)]

    def fixed(shape):
        return pl.BlockSpec(shape, lambda i: (0, 0))

    def widen(out_ref, grad_ref, gains_ref, *refs):
        wide_out, wide_grad, gain_one, gain_two = refs[len(small) : len(small) + 4]
        wide_out[...] = out_ref[...].astype(F32)
        wide_grad[...] = grad_ref[...].astype(F32)

        @pl.when(pl.program_id(0) == 0)
        def _():
            gain_one[...] = gains_ref[0:1]
            gain_two[...] = gains_ref[1:2]
            for low_ref, wide_ref in zip(refs[: len(small)], refs[len(small) + 4 :]):
                wide_ref[...] = low_ref[...].astype(F32)

    outputs, input_grad, gain_one, gain_two, dwk, dwv, dwq, dwo, up, down = pl.pallas_call(
        widen,
        grid=(count * grains,),
        in_specs=[block, block, fixed((8, own))] + [fixed(shape) for shape in small],
        out_specs=[block, block, fixed((1, own)), fixed((1, own))] + [fixed(shape) for shape in small],
        out_shape=[sd((count, length, D), F32), sd((count, length, D), F32), sd((1, own), F32), sd((1, own), F32)]
        + [sd(shape, F32) for shape in small],
        compiler_params=pltpu.CompilerParams(vmem_limit_bytes=63 * 2**20),
        name="widen",
    )(outputs, input_grad, gain_grads, dwk, dwv, dwq, dwo, up, down)
    return (
        outputs, input_grad, gain_one.reshape(own), dwq, dwk, dwv, dwo, gain_two.reshape(own), up, down,
    )


def solution(mesh):
    in_specs = (
        P("dp", "seq", None),
        P("dp", "seq", None),
        P("dp", "seq"),
        P(),
        P("dp"),
        P("dp", None),
        P("dp", None),
        P("dp", None),
        P("dp", None),
        P("dp"),
        P("dp", None),
        P("dp", None),
    )
    out_specs = (
        P("dp", "seq", None),
        P("dp", "seq", None),
        P("dp"),
        P("dp", None),
        P("dp", None),
        P("dp", None),
        P("dp", None),
        P("dp"),
        P("dp", None),
        P("dp", None),
    )
    sizes = (mesh.shape["dp"], mesh.shape["seq"])
    return jax.shard_map(functools.partial(on_device, sizes), mesh=mesh, in_specs=in_specs, out_specs=out_specs, check_vma=False)
```
